256 devices in a mesh: ctx: 16 (over y_hi, x, core), tp: 16 (over y_lo, z).
Axes of the slice: x: 4, y: 4 (y_hi: 2, y_lo: 2; y = y_hi * 2 + y_lo), z: 8, core: 2. Of those that a mesh axis runs over, the one named last changes fastest.
Arguments:
- residual: bfloat16 [8192, 5120], P('ctx', 'tp'), may hold values from -1.5 to 1.5
- global_q: bfloat16 [8192, 4096], P('ctx', 'tp'), may hold values from -144 to 144
- global_k: bfloat16 [8192, 1024], P('ctx'), may hold values from -6 to 6
- global_v: bfloat16 [8192, 1024], P('ctx'), may hold values from -12 to 12
- global_wo: bfloat16 [4096, 5120], P('tp'), may hold values from -0.125 to 0.125
- norm_gain: float32 [5120], replicated, may hold values from 0.1 to 1.9
- stretch_wq: bfloat16 [5120, 4096], P('ctx', 'tp'), may hold values from -0.125 to 0.125
- stretch_wk: bfloat16 [5120, 1024], P('ctx'), may hold values from -0.125 to 0.125
- stretch_wv: bfloat16 [5120, 1024], P('ctx'), may hold values from -0.078125 to 0.078125
- stretch_wo: bfloat16 [4096, 5120], P('tp'), may hold values from -0.125 to 0.125
Outputs:
- block_out: bfloat16 [8192, 5120], P('ctx', 'tp')
The draws below stay inside these ranges and needn't reach their ends.
All inputs are finite; a program needn't handle non-finite values.
Results may differ from the reference program's by a relative error of at most 0.035.
Values may be sent and summed in bfloat16 or wider, within the bound.
No kernel may reach another device: no remote copies, remote signals or barrier semaphores. Data moves between devices by JAX's collectives and lax.ppermute only.
A program may use at most 128 MiB of HBM per device.

```python
import jax
import jax.numpy as jnp
from jax import lax

D = 5120
HEADS = 32
KV_HEADS = 8
HEAD_DIM = 128
STRETCH = 4096
TOK_DEV = 512
GROUP = 4
TOKENS = 8192
N_CTX = 16
N_TP = 16


def common_keys(key):
    return jnp.clip(jax.random.normal(key, (TOKENS, KV_HEADS * HEAD_DIM), jnp.float32), -6.0, 6.0)


def draw_global_k(key, part):
    return common_keys(key).astype(jnp.bfloat16)


def draw_global_q(key, part):
    key = jax.random.fold_in(key, 7)
    fresh_key = jax.random.fold_in(key, 0)
    queries = jnp.clip(jax.random.normal(fresh_key, (TOKENS, HEADS * HEAD_DIM), jnp.float32), -6.0, 6.0)
    return queries.astype(jnp.bfloat16)


def raised(drawn, own_key, source, target, blocks, factor):
    owner, partner = [(jnp.arange(drawn.shape[position]) // (drawn.shape[position] // blocks)).reshape([-1 if axis == position else 1 for axis in range(drawn.ndim)]) for position in (source, target)]
    chosen = jax.random.permutation(own_key, blocks)[partner]
    strong = (owner == chosen) | (owner == (partner + blocks // 2) % blocks)
    return jnp.where(strong, factor * drawn, drawn)


def block_levels(stream_key, extent, shards, smallest, top_value):
    level, own = 1.0, jax.random.fold_in(stream_key, 6)
    for axis_at, parts in shards:
        heights = jnp.exp(jax.random.uniform(jax.random.fold_in(own, axis_at), (parts,), jnp.float32, smallest / len(shards), top_value / len(shards)))
        level = level * jnp.repeat(heights, extent[axis_at] // parts).reshape([-1 if axis == axis_at else 1 for axis in range(len(extent))])
    return level


def noise(rng, extent, scale, bound, cuts=(), kind=jnp.bfloat16):
    values = scale * jax.random.normal(rng, extent, jnp.float32)
    if cuts:
        values = values * block_levels(rng, extent, cuts, -0.22, 0.18)
    return jnp.clip(values, -bound, bound).astype(kind)


def noise_with(key, shape, spread, reach, pieces, heavy, kind=jnp.bfloat16):
    result = spread * jax.random.normal(key, shape, jnp.float32)
    if pieces:
        result = result * block_levels(key, shape, pieces, -0.22, 0.18)
    return jnp.clip(raised(result, jax.random.fold_in(key, 3), *heavy), -reach, reach).astype(kind)


def setup_inputs(seed: int = 0) -> dict:
    seeds = jax.random.split(jax.random.key(seed), 11)
    return {
        "residual": noise(seeds[0], (TOKENS, D), 0.1, 1.5, ((0, 16), (1, 16))),
        "global_q": draw_global_q(jax.random.fold_in(seeds[10], 71), 0),
        "global_k": draw_global_k(jax.random.fold_in(seeds[10], 71), 0),
        "global_v": noise(seeds[3], (TOKENS, KV_HEADS * HEAD_DIM), 2.0, 12.0, ((0, 16),)),
        "global_wo": noise_with(seeds[4], (HEADS * HEAD_DIM, D), (HEADS * HEAD_DIM) ** -0.5, 0.125, ((0, 16),), (0, 1, 16, 2.0)),
        "norm_gain": jnp.clip(1.0 + 0.18 * jax.random.normal(seeds[5], (D,), jnp.float32), 0.1, 1.9),
        "stretch_wq": noise(seeds[6], (D, HEADS * HEAD_DIM), (D // 2) ** -0.5, 0.125, ((0, 16), (1, 16))),
        "stretch_wk": noise(seeds[7], (D, KV_HEADS * HEAD_DIM), (D // 2) ** -0.5, 0.125, ((0, 16),)),
        "stretch_wv": noise(seeds[8], (D, KV_HEADS * HEAD_DIM), D ** -0.5, 0.078125, ((0, 16),)),
        "stretch_wo": noise_with(seeds[9], (HEADS * HEAD_DIM, D), (HEADS * HEAD_DIM) ** -0.5, 0.125, ((0, 16),), (0, 1, 16, 2.0)),
    }


rope_base = 500000.0
norm_eps = 1e-05
masked_score = -1e+30

def zig_positions(row_index):
    device = row_index // TOK_DEV
    within = row_index % TOK_DEV
    half_rows = TOK_DEV // 2
    later = (2 * N_CTX - 1 - device) * half_rows + within - half_rows
    return jnp.where(within < half_rows, device * half_rows + within, later).astype(jnp.int32)

def rotate(projected, places):
    length = projected.shape[0]
    head_view = projected.reshape(length, -1, HEAD_DIM)
    half_dim = HEAD_DIM // 2
    inv_freq = rope_base ** (-(jnp.arange(half_dim).astype(jnp.float32) * 2.0 / HEAD_DIM))
    angles = places.astype(jnp.float32)[:, None] * inv_freq[None, :]
    cosine = jnp.cos(angles)[:, None, :]
    sine_part = jnp.sin(angles)[:, None, :]
    lower = head_view[..., :half_dim]
    upper = head_view[..., half_dim:]
    turned = jnp.concatenate([lower * cosine - upper * sine_part, upper * cosine + lower * sine_part], axis=-1)
    return turned.reshape(length, -1)

def attend(queries, keys_all, values_all, visible):

    def one_head(head_index):
        query_head = lax.dynamic_index_in_dim(queries, head_index, 0, keepdims=False).astype(jnp.float32)
        kv_head = head_index // GROUP
        key_head = lax.dynamic_index_in_dim(keys_all, kv_head, 0, keepdims=False).astype(jnp.float32)
        value_head = lax.dynamic_index_in_dim(values_all, kv_head, 0, keepdims=False).astype(jnp.float32)
        logits = jnp.dot(query_head, key_head.T, precision=lax.Precision.HIGHEST, preferred_element_type=jnp.float32) * HEAD_DIM ** (-0.5)
        logits = jnp.where(visible, logits, masked_score)
        highest = lax.optimization_barrier(jnp.max(logits, axis=1, keepdims=True))
        exp_terms = jnp.where(visible, jnp.exp(logits - highest), 0.0)
        weight_sum = lax.optimization_barrier(jnp.sum(exp_terms, axis=1, keepdims=True))
        rounded = exp_terms.astype(jnp.bfloat16).astype(jnp.float32)
        mixed_values = jnp.dot(rounded, value_head, precision=lax.Precision.HIGHEST, preferred_element_type=jnp.float32)
        return (mixed_values / weight_sum).astype(jnp.bfloat16)
    return lax.map(one_head, jnp.arange(HEADS, dtype=jnp.int32))

def split_heads(matrix):
    return matrix.reshape(TOKENS, -1, HEAD_DIM).transpose(1, 0, 2)

def merge_heads(stacked):
    return stacked.transpose(1, 0, 2).reshape(TOKENS, -1)

def project_groups(attended, out_weight):
    cols = HEADS * HEAD_DIM // N_TP

    def add_group(total, group_index):
        columns = lax.dynamic_slice_in_dim(attended, (group_index * cols).astype(jnp.int32), cols, 1)
        rows_part = lax.dynamic_slice_in_dim(out_weight, (group_index * cols).astype(jnp.int32), cols, 0)
        part = jnp.dot(columns, rows_part, preferred_element_type=jnp.float32).astype(jnp.bfloat16)
        part = lax.optimization_barrier(part)
        return (total + part.astype(jnp.float32), None)
    total, unused = lax.scan(add_group, jnp.zeros((TOKENS, D), jnp.float32), jnp.arange(N_TP, dtype=jnp.int32))
    return total

def reference(residual, global_q, global_k, global_v, global_wo, norm_gain, stretch_wq, stretch_wk, stretch_wv, stretch_wo):
    places = zig_positions(jnp.arange(TOKENS, dtype=jnp.int32))
    causal = places[None, :] <= places[:, None]
    global_attn = merge_heads(attend(split_heads(global_q), split_heads(global_k), split_heads(global_v), causal))
    mixed = (residual.astype(jnp.float32) + project_groups(global_attn, global_wo)).astype(jnp.bfloat16)
    widened = mixed.astype(jnp.float32)
    inverse = lax.rsqrt(lax.optimization_barrier(jnp.mean(widened * widened, axis=1, keepdims=True)) + norm_eps)
    normed = (widened * inverse * norm_gain.astype(jnp.float32)[None, :]).astype(jnp.bfloat16)
    stretch_q = rotate(jnp.dot(normed, stretch_wq, preferred_element_type=jnp.float32), places).astype(jnp.bfloat16)
    stretch_k = rotate(jnp.dot(normed, stretch_wk, preferred_element_type=jnp.float32), places).astype(jnp.bfloat16)
    stretch_v = jnp.dot(normed, stretch_wv, preferred_element_type=jnp.float32).astype(jnp.bfloat16)
    windows = places // STRETCH
    in_window = causal & (windows[None, :] == windows[:, None])
    stretch_attn = merge_heads(attend(split_heads(stretch_q), split_heads(stretch_k), split_heads(stretch_v), in_window))
    block_out = mixed.astype(jnp.float32) + project_groups(stretch_attn, stretch_wo)
    return block_out.astype(jnp.bfloat16)
```

```python
import functools

import jax
import jax.numpy as jnp
from jax import lax
from jax.experimental import pallas as pl
from jax.experimental.pallas import tpu as pltpu
from jax.sharding import PartitionSpec as P

HEAD_DIM = 128
GROUP = 4
CHUNK = 256
N_CTX = 16
N_Z = 8
COLS = 320
PAIR_COLS = 2 * COLS
rope_base = 500000.0
norm_eps = 1e-05
masked_score = -1e30
scale_log2 = 1.4426950408889634 * HEAD_DIM**-0.5
MIB = 1024 * 1024
SMEM = pl.BlockSpec(memory_space=pltpu.SMEM)
VMEM = pl.BlockSpec(memory_space=pltpu.VMEM)
ANY = pl.BlockSpec(memory_space=pl.ANY)


def permute(value, axis, target):
    return lax.ppermute(value, axis, [(place, target(place)) for place in range(16)])


def to_other_core(value):
    return permute(value, "ctx", lambda c: c ^ 1)


def to_other_y_hi(value):
    return permute(value, "ctx", lambda c: c ^ 8)


def along_x(value, step):
    return permute(value, "ctx", lambda c: (c & 9) | ((c + 2 * step) & 6))


def to_other_y_lo(value):
    return permute(value, "tp", lambda t: t ^ 8)


def along_z(value, step):
    return permute(value, "tp", lambda t: (t & 8) | ((t + step) & 7))


def gather_ctx(block):
    other = to_other_y_hi(block)
    left, right = along_x(block, 1), along_x(block, -1)
    far = along_x(left, 1)
    left_other, right_other = along_x(other, 1), along_x(other, -1)
    far_other = along_x(right_other, -1)
    mine = [block, other, left, right, left_other, right_other, far, far_other]
    offsets = [(0, 0), (1, 0), (0, 3), (0, 1), (1, 3), (1, 1), (0, 2), (1, 2)]
    pieces = mine + [to_other_core(piece) for piece in mine]
    return pieces, [(dy, dx, core) for core in (0, 1) for dy, dx in offsets]


def owners(offsets):
    me = lax.axis_index("ctx")
    return [
        ((me & 8) ^ (8 * dy)) | ((me + 2 * dx) & 6) | ((me & 1) ^ dc) for dy, dx, dc in offsets
    ]


def take_kernel(place_ref, k_ref, v_ref, out_ref, sems):
    columns = pl.ds(pl.multiple_of(place_ref[0] * HEAD_DIM, HEAD_DIM), HEAD_DIM)
    copies = [
        pltpu.make_async_copy(src.at[:, columns], out_ref.at[:, pl.ds(i * HEAD_DIM, HEAD_DIM)], sems.at[i])
        for i, src in enumerate((k_ref, v_ref))
    ]
    for copy in copies:
        copy.start()
    for copy in copies:
        copy.wait()


def take_kv(place, keys, values):
    rows = keys.shape[0]
    return pl.pallas_call(
        take_kernel,
        out_shape=jax.ShapeDtypeStruct((rows, 2 * HEAD_DIM), jnp.bfloat16),
        in_specs=[SMEM, ANY, ANY],
        out_specs=VMEM,
        scratch_shapes=[pltpu.SemaphoreType.DMA((2,))],
        compiler_params=pltpu.CompilerParams(vmem_limit_bytes=2 * MIB),
        name="take_kv",
    )(place.reshape(1), keys, values)


def attend_kernel(tiles, tile_chunks, chains, meta_ref, q_ref, *rest):
    pieces, (out_ref, kv, sems) = rest[:-3], rest[-3:]
    copies = []
    for piece in pieces:
        for part in range(piece.shape[0] // CHUNK):
            source = piece.at[pl.ds(part * CHUNK, CHUNK)]
            copies.append(
                pltpu.make_async_copy(source, kv.at[meta_ref[len(copies)]], sems.at[len(copies)])
            )
            copies[-1].start()
    for copy in copies:
        copy.wait()
    span = tile_chunks * CHUNK
    for tile, (first, heads) in enumerate(tiles):
        limit = meta_ref[len(copies) + tile]
        rows = q_ref.at[pl.ds(first, CHUNK)]
        each = len(heads) // chains
        queries = [
            jnp.concatenate(
                [rows[:, h * HEAD_DIM : (h + 1) * HEAD_DIM] for h in heads[g * each : (g + 1) * each]],
                axis=0,
            )
            for g in range(chains)
        ]
        height = each * CHUNK

        def step(i, state, masked):
            here = pl.ds(i * tile_chunks, tile_chunks)
            keys = kv[here, :, :HEAD_DIM].reshape(span, HEAD_DIM)
            values = kv[here, :, HEAD_DIM:].reshape(span, HEAD_DIM)
            if masked:
                column = lax.broadcasted_iota(jnp.int32, (height, span), 1) + i * span
                row = lax.broadcasted_iota(jnp.int32, (height, span), 0) % CHUNK
                visible = column <= row + (limit - 1) * CHUNK
            scores = [
                lax.dot_general(
                    query, keys, (((1,), (1,)), ((), ())), preferred_element_type=jnp.float32
                )
                for query in queries
            ]
            after = []
            for score, (highest, total, weighted) in zip(scores, state):
                if masked:
                    score = jnp.where(visible, score, masked_score)
                new_high = jnp.maximum(highest, jnp.max(score, axis=1, keepdims=True))
                fade = jnp.exp2((highest - new_high) * scale_log2)
                terms = jnp.exp2((score - new_high) * scale_log2)
                total = total * fade + jnp.sum(terms, axis=1, keepdims=True)
                weighted = weighted * fade + jnp.dot(
                    terms.astype(jnp.bfloat16), values, preferred_element_type=jnp.float32
                )
                after.append((new_high, total, weighted))
            return tuple(after)

        state = tuple(
            (
                jnp.full((height, 1), masked_score, jnp.float32),
                jnp.zeros((height, 1), jnp.float32),
                jnp.zeros((height, HEAD_DIM), jnp.float32),
            )
            for _ in range(chains)
        )
        whole = lax.div(limit - 1, jnp.int32(tile_chunks))
        state = lax.fori_loop(0, whole, functools.partial(step, masked=False), state)
        state = step(whole, state, True)
        for g, (_, total, weighted) in enumerate(state):
            result = (weighted / total).astype(jnp.bfloat16)
            for j in range(each):
                h = heads[g * each + j]
                out_ref[first : first + CHUNK, h * HEAD_DIM : (h + 1) * HEAD_DIM] = result[
                    j * CHUNK : (j + 1) * CHUNK
                ]


def attend(meta, queries, pieces, chunks, tiles, tile_chunks, chains, name):
    return pl.pallas_call(
        functools.partial(attend_kernel, tiles, tile_chunks, chains),
        out_shape=jax.ShapeDtypeStruct(queries.shape, jnp.bfloat16),
        in_specs=[SMEM, VMEM] + [ANY] * len(pieces),
        out_specs=VMEM,
        scratch_shapes=[
            pltpu.VMEM((chunks, CHUNK, 2 * HEAD_DIM), jnp.bfloat16),
            pltpu.SemaphoreType.DMA((chunks,)),
        ],
        compiler_params=pltpu.CompilerParams(vmem_limit_bytes=32 * MIB),
        name=name,
    )(meta, queries, *pieces)


def ring_gather(block):
    half = block.shape[0] // 2
    below, above = [block], [block]
    for _ in range(3):
        below.append(along_z(below[-1], 1))
        above.append(along_z(above[-1], -1))
    far = [along_z(below[-1][:half], 1), along_z(above[-1][half:], -1)]
    return above + below[:0:-1] + far


RING_OFFSETS = (0, 1, 2, 3, 5, 6, 7, 4)


def ring_reduce(term):
    far = term(4).astype(jnp.bfloat16)
    half = far.shape[0] // 2
    up, down = along_z(far[:half], 1), along_z(far[half:], -1)
    for hop in (3, 2, 1):
        up, down = up.astype(jnp.float32), down.astype(jnp.float32)
        if hop == 3:
            up = jnp.pad(up, ((0, half), (0, 0)))
            down = jnp.pad(down, ((half, 0), (0, 0)))
        up = along_z((term(hop) + up).astype(jnp.bfloat16), 1)
        down = along_z((term(8 - hop) + down).astype(jnp.bfloat16), -1)
    return up.astype(jnp.float32) + down.astype(jnp.float32)


def load_features(refs):
    return [ref[...] for ref in refs[:7]] + [jnp.concatenate([refs[7][...], refs[8][...]], axis=0)]


def rope(value, cosine, sine):
    return value * cosine + pltpu.roll(value, HEAD_DIM // 2, axis=1) * sine


def project_kernel(z_ref, *rest):
    blocks, (gain_ref, cos_ref, sin_ref, w_ref, q_ref, kv_ref, w_vmem, sems) = rest[:9], rest[9:]
    copies = []
    for i, offset in enumerate(RING_OFFSETS):
        source = (z_ref[0] + offset) & 7
        for y_lo in (0, 1):
            rows = pl.ds(y_lo * COLS, COLS)
            copies.append(
                pltpu.make_async_copy(w_ref.at[y_lo * N_Z + source], w_vmem.at[i, rows], sems.at[len(copies)])
            )
            copies[-1].start()
    features = load_features(blocks)
    squares = jnp.zeros((CHUNK, 1), jnp.float32)
    for value in features:
        wide = value.astype(jnp.float32)
        squares = squares + jnp.sum(wide * wide, axis=1, keepdims=True)
    inverse = lax.rsqrt(squares / (16 * COLS) + norm_eps)
    for copy in copies:
        copy.wait()
    total = jnp.zeros((CHUNK, w_vmem.shape[2]), jnp.float32)
    for i, value in enumerate(features):
        normed = (value.astype(jnp.float32) * inverse * gain_ref[i : i + 1]).astype(jnp.bfloat16)
        total = total + jnp.dot(normed, w_vmem[i], preferred_element_type=jnp.float32)
    cosine, sine = cos_ref[...], sin_ref[...]
    for h in range(GROUP):
        at = slice(h * HEAD_DIM, (h + 1) * HEAD_DIM)
        q_ref[:, at] = rope(total[:, at], cosine, sine).astype(jnp.bfloat16)
    at = GROUP * HEAD_DIM
    kv_ref[:, :HEAD_DIM] = rope(total[:, at : at + HEAD_DIM], cosine, sine).astype(jnp.bfloat16)
    kv_ref[:, HEAD_DIM:] = total[:, at + HEAD_DIM :].astype(jnp.bfloat16)


def project(z, blocks, gain, cosine, sine, weights):
    width = weights.shape[2]
    return pl.pallas_call(
        project_kernel,
        out_shape=(
            jax.ShapeDtypeStruct((CHUNK, GROUP * HEAD_DIM), jnp.bfloat16),
            jax.ShapeDtypeStruct((CHUNK, 2 * HEAD_DIM), jnp.bfloat16),
        ),
        in_specs=[SMEM] + [VMEM] * 12 + [ANY],
        out_specs=(VMEM, VMEM),
        scratch_shapes=[
            pltpu.VMEM((N_Z, PAIR_COLS, width), jnp.bfloat16),
            pltpu.SemaphoreType.DMA((2 * N_Z,)),
        ],
        compiler_params=pltpu.CompilerParams(vmem_limit_bytes=32 * MIB),
        name="norm_project",
    )(z.reshape(1), *blocks, gain, cosine, sine, weights)


def finish_kernel(place_ref, *rest):
    blocks, (mixed_ref, w_ref, own_ref, other_ref, w_vmem, sems) = rest[:9], rest[9:]
    copies = []
    for i, offset in enumerate(RING_OFFSETS):
        source = (place_ref[1] + offset) & 7
        copies.append(pltpu.make_async_copy(w_ref.at[source], w_vmem.at[i], sems.at[i]))
        copies[-1].start()
    features = load_features(blocks)
    for copy in copies:
        copy.wait()
    total = mixed_ref[...].astype(jnp.float32)
    for i, value in enumerate(features):
        total = total + jnp.dot(value, w_vmem[i], preferred_element_type=jnp.float32)
    first, second = total[:, :COLS].astype(jnp.bfloat16), total[:, COLS:].astype(jnp.bfloat16)

    @pl.when(place_ref[0] == 0)
    def _():
        own_ref[...] = first
        other_ref[...] = second

    @pl.when(place_ref[0] == 1)
    def _():
        own_ref[...] = second
        other_ref[...] = first


def finish(place, blocks, mixed, weights):
    part = jax.ShapeDtypeStruct((CHUNK, COLS), jnp.bfloat16)
    return pl.pallas_call(
        finish_kernel,
        out_shape=(part, part),
        in_specs=[SMEM] + [VMEM] * 10 + [ANY],
        out_specs=(VMEM, VMEM),
        scratch_shapes=[pltpu.VMEM(weights.shape, jnp.bfloat16), pltpu.SemaphoreType.DMA((N_Z,))],
        compiler_params=pltpu.CompilerParams(vmem_limit_bytes=24 * MIB),
        name="project_out",
    )(place, *blocks, mixed, weights)


def by_z(columns):
    rows = columns.shape[0]
    return columns.reshape(rows, 2, N_Z, COLS).transpose(2, 0, 1, 3).reshape(N_Z, rows, PAIR_COLS)


def in_order(first, own, other, axis):
    return jnp.where(
        first, jnp.concatenate([own, other], axis=axis), jnp.concatenate([other, own], axis=axis)
    )


def per_device(
    residual,
    global_q,
    global_k,
    global_v,
    global_wo,
    norm_gain,
    stretch_wq,
    stretch_wk,
    stretch_wv,
    stretch_wo,
):
    me = lax.axis_index("ctx")
    place = lax.axis_index("tp")
    y_lo, z = place // N_Z, place % N_Z
    lower = y_lo == 0
    core = me & 1

    kv_first = take_kv(place // 2, global_k, global_v)
    pieces, offsets = gather_ctx(kv_first)
    sources = owners(offsets)
    slots = [slot for c in sources for slot in (c, 2 * N_CTX - 1 - c)]
    meta = jnp.stack(slots + [me + 1, 2 * N_CTX - me]).astype(jnp.int32)

    own_wq = permute(stretch_wq, "tp", lambda t: 8 * (t % 2) + t // 2)
    other_wq = permute(stretch_wq, "tp", lambda t: 8 * (1 - t % 2) + t // 2)
    weights = jnp.concatenate(
        [
            in_order(lower, own_wq, other_wq, 1),
            lax.dynamic_slice_in_dim(stretch_wk, z * HEAD_DIM, HEAD_DIM, 1),
            lax.dynamic_slice_in_dim(stretch_wv, z * HEAD_DIM, HEAD_DIM, 1),
        ],
        axis=1,
    )
    weights = lax.all_gather(weights, "ctx", axis=0, tiled=False)

    rows = stretch_wo.shape[0] // N_CTX
    share = by_z(lax.dynamic_slice_in_dim(stretch_wo, me * rows, rows, 0))
    share = lax.all_to_all(
        share, "tp", 0, 0, axis_index_groups=[list(range(8)), list(range(8, 16))]
    )
    share = in_order(lower, share, to_other_y_lo(share), 0)
    share = lax.optimization_barrier((share, weights[0, :8, :128]))[0]
    last_weights = lax.all_gather(share, "ctx", axis=0, tiled=False)
    last_weights = last_weights.transpose(1, 0, 2, 3).reshape(N_Z, -1, PAIR_COLS)

    first_weights = by_z(global_wo)
    first_weights = lax.dynamic_slice_in_dim(
        jnp.concatenate([first_weights, first_weights], axis=0), z, N_Z, 0
    )
    half_mine = to_other_y_lo(lax.dynamic_slice_in_dim(first_weights, core * 4, 4, 0))
    half_other = to_other_core(half_mine)
    partner_weights = in_order(core == 0, half_mine, half_other, 0)

    kept = lax.dynamic_slice_in_dim(residual, y_lo * CHUNK, CHUNK, 0)
    given = lax.dynamic_slice_in_dim(residual, (1 - y_lo) * CHUNK, CHUNK, 0)
    residual_pair = in_order(lower, kept, to_other_y_lo(given), 1)

    tiles = ((0, (0, 1)), (CHUNK, (0, 1)))
    attended = attend(meta, global_q, pieces, 2 * N_CTX, tiles, 4, 2, "attend_all")
    kept = lax.dynamic_slice_in_dim(attended, y_lo * CHUNK, CHUNK, 0)
    given = lax.dynamic_slice_in_dim(attended, (1 - y_lo) * CHUNK, CHUNK, 0)
    received = to_other_y_lo(given)

    def term(offset):
        return jnp.dot(kept, first_weights[offset], preferred_element_type=jnp.float32) + jnp.dot(
            received, partner_weights[offset], preferred_element_type=jnp.float32
        )

    mixed = (residual_pair.astype(jnp.float32) + term(0) + ring_reduce(term)).astype(jnp.bfloat16)

    blocks = ring_gather(mixed)
    gain = norm_gain.reshape(2, N_Z, COLS).transpose(1, 0, 2).reshape(N_Z, PAIR_COLS)
    gain = jnp.stack([gain[(z + offset) % N_Z] for offset in RING_OFFSETS])
    chunk = jnp.where(lower, me, 2 * N_CTX - 1 - me)
    positions = (chunk * CHUNK + jnp.arange(CHUNK, dtype=jnp.int32)).astype(jnp.float32)
    half_dim = HEAD_DIM // 2
    inv_freq = rope_base ** (-(jnp.arange(half_dim).astype(jnp.float32) * 2.0 / HEAD_DIM))
    angles = positions[:, None] * inv_freq[None, :]
    cosine, sine = jnp.cos(angles), jnp.sin(angles)
    stretch_q, stretch_kv = project(
        z,
        blocks,
        gain,
        jnp.concatenate([cosine, cosine], axis=1),
        jnp.concatenate([-sine, sine], axis=1),
        weights,
    )
    pieces, offsets = gather_ctx(stretch_kv)
    slots = [jnp.where(lower, c, N_CTX - 1 - c) for c in owners(offsets)]
    limit = jnp.where(lower, me + 1, N_CTX - me)
    meta = jnp.stack(slots + [limit]).astype(jnp.int32)
    attended = attend(
        meta, stretch_q, pieces, N_CTX, ((0, (0, 1, 2, 3)),), 4, 2, "attend_window"
    )
    own, other = finish(
        jnp.stack([y_lo, z]).astype(jnp.int32), ring_gather(attended), mixed, last_weights
    )
    return in_order(lower, own, to_other_y_lo(other), 0)


def solution(mesh):
    in_specs = (
        P("ctx", "tp"),
        P("ctx", "tp"),
        P("ctx", None),
        P("ctx", None),
        P("tp", None),
        P(),
        P("ctx", "tp"),
        P("ctx", None),
        P("ctx", None),
        P("tp", None),
    )
    return jax.shard_map(
        per_device, mesh=mesh, in_specs=in_specs, out_specs=P("ctx", "tp"), check_vma=False
    )
```

```python
import functools

import jax
import jax.numpy as jnp
from jax import lax
from jax.experimental import pallas as pl
from jax.experimental.pallas import tpu as pltpu
from jax.sharding import PartitionSpec as P

HEAD_DIM = 128
GROUP = 4
CHUNK = 256
N_CTX = 16
N_Z = 8
COLS = 320
PAIR_COLS = 2 * COLS
rope_base = 500000.0
norm_eps = 1e-05
masked_score = -1e30
scale_log2 = 1.4426950408889634 * HEAD_DIM**-0.5
MIB = 1024 * 1024
SMEM = pl.BlockSpec(memory_space=pltpu.SMEM)
VMEM = pl.BlockSpec(memory_space=pltpu.VMEM)
ANY = pl.BlockSpec(memory_space=pl.ANY)


def permute(value, axis, target):
    return lax.ppermute(value, axis, [(place, target(place)) for place in range(16)])


def to_other_core(value):
    return permute(value, "ctx", lambda c: c ^ 1)


def to_other_y_hi(value):
    return permute(value, "ctx", lambda c: c ^ 8)


def along_x(value, step):
    return permute(value, "ctx", lambda c: (c & 9) | ((c + 2 * step) & 6))


def to_other_y_lo(value):
    return permute(value, "tp", lambda t: t ^ 8)


def along_z(value, step):
    return permute(value, "tp", lambda t: (t & 8) | ((t + step) & 7))


def after_kernel(*refs):
    pass


def after(value, *earlier):
    return pl.pallas_call(
        after_kernel,
        out_shape=jax.ShapeDtypeStruct(value.shape, value.dtype),
        in_specs=[ANY] * (1 + len(earlier)),
        out_specs=ANY,
        input_output_aliases={0: 0},
        compiler_params=pltpu.CompilerParams(vmem_limit_bytes=MIB),
        name="after",
    )(value, *earlier)


def gather_ctx(block):
    other = to_other_y_hi(block)
    left, right = along_x(block, 1), along_x(block, -1)
    far = along_x(left, 1)
    left_other, right_other = along_x(other, 1), along_x(other, -1)
    far_other = along_x(right_other, -1)
    mine = [block, other, left, right, far, left_other, right_other, far_other]
    offsets = [(0, 0), (1, 0), (0, 3), (0, 1), (0, 2), (1, 3), (1, 1), (1, 2)]
    pieces = mine + [
        to_other_core(jnp.stack(mine[:4])),
        to_other_core(jnp.stack(mine[4:7])),
        to_other_core(far_other),
    ]
    return pieces, [(dy, dx, core) for core in (0, 1) for dy, dx in offsets]


def owners(offsets):
    me = lax.axis_index("ctx")
    return [
        ((me & 8) ^ (8 * dy)) | ((me + 2 * dx) & 6) | ((me & 1) ^ dc) for dy, dx, dc in offsets
    ]


def take_kernel(place_ref, k_ref, v_ref, out_ref, sems):
    columns = pl.ds(pl.multiple_of(place_ref[0] * HEAD_DIM, HEAD_DIM), HEAD_DIM)
    copies = [
        pltpu.make_async_copy(src.at[:, columns], out_ref.at[:, pl.ds(i * HEAD_DIM, HEAD_DIM)], sems.at[i])
        for i, src in enumerate((k_ref, v_ref))
    ]
    for copy in copies:
        copy.start()
    for copy in copies:
        copy.wait()


def take_kv(place, keys, values):
    rows = keys.shape[0]
    return pl.pallas_call(
        take_kernel,
        out_shape=jax.ShapeDtypeStruct((rows, 2 * HEAD_DIM), jnp.bfloat16),
        in_specs=[SMEM, ANY, ANY],
        out_specs=VMEM,
        scratch_shapes=[pltpu.SemaphoreType.DMA((2,))],
        compiler_params=pltpu.CompilerParams(vmem_limit_bytes=60 * MIB),
        name="take_kv",
    )(place.reshape(1), keys, values)


def attend_kernel(tiles, tile_chunks, chains, meta_ref, q_ref, *rest):
    pieces, outs, (kv, sems) = rest[: -2 - len(tiles)], rest[-2 - len(tiles) : -2], rest[-2:]
    blocks = []
    for piece in pieces:
        blocks += [piece] if len(piece.shape) == 2 else [piece.at[b] for b in range(piece.shape[0])]
    copies = []
    for block in blocks:
        for part in range(block.shape[0] // CHUNK):
            source = block.at[pl.ds(part * CHUNK, CHUNK)]
            copies.append(
                pltpu.make_async_copy(source, kv.at[meta_ref[len(copies)]], sems.at[len(copies)])
            )
            copies[-1].start()
    for copy in copies:
        copy.wait()
    span = tile_chunks * CHUNK
    for tile, (heads, out_ref) in enumerate(zip(tiles, outs)):
        limit = meta_ref[len(copies) + 2 * tile]
        first = pl.multiple_of(meta_ref[len(copies) + 2 * tile + 1], CHUNK)
        rows = q_ref.at[pl.ds(first, CHUNK)]
        each = len(heads) // chains
        queries = [
            jnp.concatenate(
                [rows[:, h * HEAD_DIM : (h + 1) * HEAD_DIM] for h in heads[g * each : (g + 1) * each]],
                axis=0,
            )
            for g in range(chains)
        ]
        height = each * CHUNK

        def step(i, state, masked):
            here = pl.ds(i * tile_chunks, tile_chunks)
            keys = kv[here, :, :HEAD_DIM].reshape(span, HEAD_DIM)
            values = kv[here, :, HEAD_DIM:].reshape(span, HEAD_DIM)
            if masked:
                column = lax.broadcasted_iota(jnp.int32, (height, span), 1) + i * span
                row = lax.broadcasted_iota(jnp.int32, (height, span), 0) % CHUNK
                visible = column <= row + (limit - 1) * CHUNK
            scores = [
                lax.dot_general(
                    query, keys, (((1,), (1,)), ((), ())), preferred_element_type=jnp.float32
                )
                for query in queries
            ]
            after = []
            for score, (highest, total, weighted) in zip(scores, state):
                if masked:
                    score = jnp.where(visible, score, masked_score)
                new_high = jnp.maximum(highest, jnp.max(score, axis=1, keepdims=True))
                fade = jnp.exp2((highest - new_high) * scale_log2)
                terms = jnp.exp2((score - new_high) * scale_log2)
                total = total * fade + jnp.sum(terms, axis=1, keepdims=True)
                weighted = weighted * fade + jnp.dot(
                    terms.astype(jnp.bfloat16), values, preferred_element_type=jnp.float32
                )
                after.append((new_high, total, weighted))
            return tuple(after)

        state = tuple(
            (
                jnp.full((height, 1), masked_score, jnp.float32),
                jnp.zeros((height, 1), jnp.float32),
                jnp.zeros((height, HEAD_DIM), jnp.float32),
            )
            for _ in range(chains)
        )
        whole = lax.div(limit - 1, jnp.int32(tile_chunks))
        state = lax.fori_loop(0, whole, functools.partial(step, masked=False), state)
        state = step(whole, state, True)
        for g, (_, total, weighted) in enumerate(state):
            result = (weighted / total).astype(jnp.bfloat16)
            for j in range(each):
                h = heads[g * each + j]
                out_ref[:, h * HEAD_DIM : (h + 1) * HEAD_DIM] = result[
                    j * CHUNK : (j + 1) * CHUNK
                ]


def attend(meta, queries, pieces, chunks, tiles, tile_chunks, chains, name):
    return pl.pallas_call(
        functools.partial(attend_kernel, tiles, tile_chunks, chains),
        out_shape=[jax.ShapeDtypeStruct((CHUNK, queries.shape[1]), jnp.bfloat16)] * len(tiles),
        in_specs=[SMEM, VMEM] + [ANY] * len(pieces),
        out_specs=[VMEM] * len(tiles),
        scratch_shapes=[
            pltpu.VMEM((chunks, CHUNK, 2 * HEAD_DIM), jnp.bfloat16),
            pltpu.SemaphoreType.DMA((chunks,)),
        ],
        compiler_params=pltpu.CompilerParams(vmem_limit_bytes=32 * MIB),
        cost_estimate=pl.CostEstimate(
            flops=2_200_000_000, bytes_accessed=5_000_000, transcendentals=10_000_000
        ),
        name=name,
    )(meta, queries, *pieces)


def ring_gather(block):
    half = block.shape[0] // 2
    below, above = [block], [block]
    for _ in range(3):
        below.append(along_z(below[-1], 1))
        above.append(along_z(above[-1], -1))
    far = [along_z(below[-1][:half], 1), along_z(above[-1][half:], -1)]
    return above + below[:0:-1] + far


RING_OFFSETS = (0, 1, 2, 3, 5, 6, 7, 4)


def ring_reduce(term):
    far = term(4).astype(jnp.bfloat16)
    half = far.shape[0] // 2
    up, down = along_z(far[:half], 1), along_z(far[half:], -1)
    steps = []
    for hop in (3, 2, 1):
        steps.append(up)
        up, down = up.astype(jnp.float32), down.astype(jnp.float32)
        if hop == 3:
            up = jnp.pad(up, ((0, half), (0, 0)))
            down = jnp.pad(down, ((half, 0), (0, 0)))
        up = along_z((term(hop) + up).astype(jnp.bfloat16), 1)
        down = along_z((term(8 - hop) + down).astype(jnp.bfloat16), -1)
    return up.astype(jnp.float32) + down.astype(jnp.float32), steps


def load_features(refs):
    return [ref[...] for ref in refs[:7]] + [jnp.concatenate([refs[7][...], refs[8][...]], axis=0)]


def rope(value, cosine, sine):
    return value * cosine + pltpu.roll(value, HEAD_DIM // 2, axis=1) * sine


def project_kernel(z_ref, *rest):
    blocks, (gain_ref, cos_ref, sin_ref, w_ref, q_ref, kv_ref, w_vmem, sems) = rest[:9], rest[9:]
    copies = []
    for i, offset in enumerate(RING_OFFSETS):
        source = (z_ref[0] + offset) & 7
        for y_lo in (0, 1):
            rows = pl.ds(y_lo * COLS, COLS)
            copies.append(
                pltpu.make_async_copy(w_ref.at[y_lo * N_Z + source], w_vmem.at[i, rows], sems.at[len(copies)])
            )
            copies[-1].start()
    features = load_features(blocks)
    squares = jnp.zeros((CHUNK, 1), jnp.float32)
    for value in features:
        wide = value.astype(jnp.float32)
        squares = squares + jnp.sum(wide * wide, axis=1, keepdims=True)
    inverse = lax.rsqrt(squares / (16 * COLS) + norm_eps)
    total = jnp.zeros((CHUNK, w_vmem.shape[2]), jnp.float32)
    for i, value in enumerate(features):
        normed = (value.astype(jnp.float32) * inverse * gain_ref[i : i + 1]).astype(jnp.bfloat16)
        copies[2 * i].wait()
        copies[2 * i + 1].wait()
        total = total + jnp.dot(normed, w_vmem[i], preferred_element_type=jnp.float32)
    cosine, sine = cos_ref[...], sin_ref[...]
    for h in range(GROUP):
        at = slice(h * HEAD_DIM, (h + 1) * HEAD_DIM)
        q_ref[:, at] = rope(total[:, at], cosine, sine).astype(jnp.bfloat16)
    at = GROUP * HEAD_DIM
    kv_ref[:, :HEAD_DIM] = rope(total[:, at : at + HEAD_DIM], cosine, sine).astype(jnp.bfloat16)
    kv_ref[:, HEAD_DIM:] = total[:, at + HEAD_DIM :].astype(jnp.bfloat16)


def project(z, blocks, gain, cosine, sine, weights):
    width = weights.shape[2]
    return pl.pallas_call(
        project_kernel,
        out_shape=(
            jax.ShapeDtypeStruct((CHUNK, GROUP * HEAD_DIM), jnp.bfloat16),
            jax.ShapeDtypeStruct((CHUNK, 2 * HEAD_DIM), jnp.bfloat16),
        ),
        in_specs=[SMEM] + [VMEM] * 12 + [ANY],
        out_specs=(VMEM, VMEM),
        scratch_shapes=[
            pltpu.VMEM((N_Z, PAIR_COLS, width), jnp.bfloat16),
            pltpu.SemaphoreType.DMA((2 * N_Z,)),
        ],
        compiler_params=pltpu.CompilerParams(vmem_limit_bytes=54 * MIB),
        name="norm_project",
    )(z.reshape(1), *blocks, gain, cosine, sine, weights)


def finish_kernel(place_ref, *rest):
    blocks, (mixed_ref, w_ref, own_ref, other_ref, w_vmem, sems) = rest[:9], rest[9:]
    copies = []
    for i, offset in enumerate(RING_OFFSETS):
        source = (place_ref[1] + offset) & 7
        rows = w_ref.at[:, pl.ds(2 * source, 2)]
        copies.append(pltpu.make_async_copy(rows, w_vmem.at[i], sems.at[i]))
        copies[-1].start()
    features = load_features(blocks)
    total = mixed_ref[...].astype(jnp.float32)
    for i, value in enumerate(features):
        copies[i].wait()
        for j in (0, 1):
            total = total + jnp.dot(
                value[:, j * 2 * HEAD_DIM : (j + 1) * 2 * HEAD_DIM],
                w_vmem[i, :, j].reshape(2 * HEAD_DIM, PAIR_COLS),
                preferred_element_type=jnp.float32,
            )
    first, second = total[:, :COLS].astype(jnp.bfloat16), total[:, COLS:].astype(jnp.bfloat16)

    @pl.when(place_ref[0] == 0)
    def _():
        own_ref[...] = first
        other_ref[...] = second

    @pl.when(place_ref[0] == 1)
    def _():
        own_ref[...] = second
        other_ref[...] = first


def finish(place, blocks, mixed, weights):
    part = jax.ShapeDtypeStruct((CHUNK, COLS), jnp.bfloat16)
    return pl.pallas_call(
        finish_kernel,
        out_shape=(part, part),
        in_specs=[SMEM] + [VMEM] * 10 + [ANY],
        out_specs=(VMEM, VMEM),
        scratch_shapes=[
            pltpu.VMEM((N_Z, N_CTX, 2, weights.shape[2], PAIR_COLS), jnp.bfloat16),
            pltpu.SemaphoreType.DMA((N_Z,)),
        ],
        compiler_params=pltpu.CompilerParams(vmem_limit_bytes=57 * MIB),
        name="project_out",
    )(place, *blocks, mixed, weights)


def by_z(columns):
    rows = columns.shape[0]
    return columns.reshape(rows, 2, N_Z, COLS).transpose(2, 0, 1, 3).reshape(N_Z, rows, PAIR_COLS)


def turned(blocks, first):
    return lax.dynamic_slice_in_dim(jnp.concatenate([blocks, blocks], axis=0), first, N_Z, 0)


def in_order(first, own, other, axis):
    return jnp.where(
        first, jnp.concatenate([own, other], axis=axis), jnp.concatenate([other, own], axis=axis)
    )


def per_device(
    residual,
    global_q,
    global_k,
    global_v,
    global_wo,
    norm_gain,
    stretch_wq,
    stretch_wk,
    stretch_wv,
    stretch_wo,
):
    me = lax.axis_index("ctx")
    place = lax.axis_index("tp")
    y_lo, z = place // N_Z, place % N_Z
    lower = y_lo == 0
    core = me & 1

    kv_first = take_kv(place // 2, global_k, global_v)
    pieces, offsets = gather_ctx(kv_first)
    near, far = pieces[3], pieces[4]
    slots = [slot for c in owners(offsets) for slot in (c, 2 * N_CTX - 1 - c)]
    limits = jnp.where(lower, me + 1, 2 * N_CTX - me), jnp.where(lower, 2 * N_CTX - me, me + 1)
    kept_at, given_at = y_lo * CHUNK, (1 - y_lo) * CHUNK
    meta = jnp.stack(slots + [limits[0], kept_at, limits[1], given_at]).astype(jnp.int32)

    first_weights = turned(by_z(global_wo), z)
    half = first_weights.shape[1] // 2
    half_mine = lax.dynamic_slice_in_dim(first_weights, core * half, half, 1)
    half_mine = to_other_y_lo(after(half_mine, near))
    half_other = to_other_core(half_mine)

    own_wq = after(stretch_wq + jnp.bfloat16(0), far)
    other_wq = permute(own_wq, "tp", lambda t: 8 * (1 - t % 2) + t // 2)
    own_wq = permute(own_wq, "tp", lambda t: 8 * (t % 2) + t // 2)
    weights = jnp.concatenate(
        [
            in_order(lower, own_wq, other_wq, 1),
            lax.dynamic_slice_in_dim(stretch_wk, z * HEAD_DIM, HEAD_DIM, 1),
            lax.dynamic_slice_in_dim(stretch_wv, z * HEAD_DIM, HEAD_DIM, 1),
        ],
        axis=1,
    )
    weights = lax.all_gather(weights, "ctx", axis=0, tiled=False)

    kept = lax.dynamic_slice_in_dim(residual, kept_at, CHUNK, 0)
    given = lax.dynamic_slice_in_dim(residual, given_at, CHUNK, 0)
    residual_pair = in_order(lower, kept, to_other_y_lo(after(given, far)), 1)

    kept, given = attend(
        meta, global_q, pieces, 2 * N_CTX, ((0, 1), (0, 1)), 4, 2, "attend_all"
    )
    received = after(to_other_y_lo(given), half_other)
    received_mine = jnp.where(core == 0, received[:, :HEAD_DIM], received[:, HEAD_DIM:])
    received_other = jnp.where(core == 0, received[:, HEAD_DIM:], received[:, :HEAD_DIM])

    def term(offset):
        return (
            jnp.dot(kept, first_weights[offset], preferred_element_type=jnp.float32)
            + jnp.dot(received_mine, half_mine[offset], preferred_element_type=jnp.float32)
            + jnp.dot(received_other, half_other[offset], preferred_element_type=jnp.float32)
        )

    own_term = residual_pair.astype(jnp.float32) + term(0)
    others, steps = ring_reduce(term)
    mixed = (own_term + others).astype(jnp.bfloat16)

    rows = stretch_wo.shape[0] // N_CTX
    share = turned(by_z(lax.dynamic_slice_in_dim(stretch_wo, me * rows, rows, 0)), z)
    share = share.reshape(2, 2, 2, rows, PAIR_COLS)
    share = jnp.stack([share[:, :, 0], along_z(after(share[:, :, 1], given), 1)], axis=2)
    share = jnp.stack([share[:, 0], along_z(after(share[:, 1], steps[0]), 2)], axis=1)
    share = jnp.stack([share[0], along_z(after(share[1], steps[1]), 4)], axis=0)
    share = turned(share.reshape(N_Z, rows, PAIR_COLS)[::-1], 7 - z)
    share = in_order(lower, share, to_other_y_lo(after(share, steps[2])), 0)
    last_weights = lax.all_gather(share, "ctx", axis=0, tiled=False)

    blocks = ring_gather(mixed)
    gain = norm_gain.reshape(2, N_Z, COLS).transpose(1, 0, 2).reshape(N_Z, PAIR_COLS)
    gain = jnp.stack([gain[(z + offset) % N_Z] for offset in RING_OFFSETS])
    chunk = jnp.where(lower, me, 2 * N_CTX - 1 - me)
    positions = (chunk * CHUNK + jnp.arange(CHUNK, dtype=jnp.int32)).astype(jnp.float32)
    half_dim = HEAD_DIM // 2
    inv_freq = rope_base ** (-(jnp.arange(half_dim).astype(jnp.float32) * 2.0 / HEAD_DIM))
    angles = positions[:, None] * inv_freq[None, :]
    cosine, sine = jnp.cos(angles), jnp.sin(angles)
    stretch_q, stretch_kv = project(
        z,
        blocks,
        gain,
        jnp.concatenate([cosine, cosine], axis=1),
        jnp.concatenate([-sine, sine], axis=1),
        weights,
    )
    pieces, offsets = gather_ctx(stretch_kv)
    slots = [jnp.where(lower, c, N_CTX - 1 - c) for c in owners(offsets)]
    limit = jnp.where(lower, me + 1, N_CTX - me)
    meta = jnp.stack(slots + [limit, 0]).astype(jnp.int32)
    (attended,) = attend(
        meta, stretch_q, pieces, N_CTX, ((0, 1, 2, 3),), 4, 2, "attend_window"
    )
    own, other = finish(
        jnp.stack([y_lo, z]).astype(jnp.int32), ring_gather(attended), mixed, last_weights
    )
    return in_order(lower, own, to_other_y_lo(other), 0)


def solution(mesh):
    in_specs = (
        P("ctx", "tp"),
        P("ctx", "tp"),
        P("ctx", None),
        P("ctx", None),
        P("tp", None),
        P(),
        P("ctx", "tp"),
        P("ctx", None),
        P("ctx", None),
        P("tp", None),
    )
    return jax.shard_map(
        per_device, mesh=mesh, in_specs=in_specs, out_specs=P("ctx", "tp"), check_vma=False
    )
```

```python
import functools

import jax
import jax.numpy as jnp
from jax import lax
from jax.experimental import pallas as pl
from jax.experimental.pallas import tpu as pltpu
from jax.sharding import PartitionSpec as P

HEAD_DIM = 128
GROUP = 4
CHUNK = 256
N_CTX = 16
N_Z = 8
COLS = 320
PAIR_COLS = 2 * COLS
rope_base = 500000.0
norm_eps = 1e-05
masked_score = -1e30
scale_log2 = 1.4426950408889634 * HEAD_DIM**-0.5
MIB = 1024 * 1024
SMEM = pl.BlockSpec(memory_space=pltpu.SMEM)
VMEM = pl.BlockSpec(memory_space=pltpu.VMEM)
ANY = pl.BlockSpec(memory_space=pl.ANY)


def permute(value, axis, target):
    return lax.ppermute(value, axis, [(place, target(place)) for place in range(16)])


def to_other_core(value):
    return permute(value, "ctx", lambda c: c ^ 1)


def to_other_y_hi(value):
    return permute(value, "ctx", lambda c: c ^ 8)


def along_x(value, step):
    return permute(value, "ctx", lambda c: (c & 9) | ((c + 2 * step) & 6))


def to_other_y_lo(value):
    return permute(value, "tp", lambda t: t ^ 8)


def along_z(value, step):
    return permute(value, "tp", lambda t: (t & 8) | ((t + step) & 7))


def nothing_kernel(*refs):
    pass


def together(*values):
    return pl.pallas_call(
        nothing_kernel,
        out_shape=[jax.ShapeDtypeStruct(value.shape, value.dtype) for value in values],
        in_specs=[ANY] * len(values),
        out_specs=[ANY] * len(values),
        input_output_aliases={i: i for i in range(len(values))},
        compiler_params=pltpu.CompilerParams(vmem_limit_bytes=MIB),
        name="together",
    )(*values)


def copy_kernel(source, *rest):
    copy = pltpu.make_async_copy(source, rest[-2], rest[-1])
    copy.start()
    copy.wait()


def copy_after(value, *earlier):
    return pl.pallas_call(
        copy_kernel,
        out_shape=jax.ShapeDtypeStruct(value.shape, value.dtype),
        in_specs=[ANY] * (1 + len(earlier)),
        out_specs=VMEM,
        scratch_shapes=[pltpu.SemaphoreType.DMA],
        compiler_params=pltpu.CompilerParams(vmem_limit_bytes=MIB),
        name="copy_after",
    )(value, *earlier)


def arrange_kernel(row_count, place_ref, source, *rest):
    count = place_ref.shape[0] - 1
    outs, (rows, sem) = rest[-2 - count : -2], rest[-2:]
    first = pl.multiple_of(place_ref[1], 16)
    copy = pltpu.make_async_copy(source.at[pl.ds(first, row_count)], rows, sem)
    copy.start()
    copy.wait()
    for z in range(N_Z):
        offset = (z - place_ref[0]) & 7
        for y_lo in (0, 1):
            at = (y_lo * N_Z + z) * COLS
            outs[0][offset, :, y_lo * COLS : (y_lo + 1) * COLS] = rows[:, at : at + COLS]
    if len(outs) == 2:
        height = outs[1].shape[1]
        half = pl.ds(pl.multiple_of(place_ref[2], height), height)
        outs[1][...] = outs[0][:, half, :]


def arrange(z, first, half, weights, row_count, *earlier):
    shapes = [jax.ShapeDtypeStruct((N_Z, row_count, PAIR_COLS), jnp.bfloat16)]
    place = [z, first]
    if half is not None:
        shapes.append(jax.ShapeDtypeStruct((N_Z, row_count // 2, PAIR_COLS), jnp.bfloat16))
        place.append(half * (row_count // 2))
    return pl.pallas_call(
        functools.partial(arrange_kernel, row_count),
        out_shape=shapes,
        in_specs=[SMEM] + [ANY] * (1 + len(earlier)),
        out_specs=[VMEM] * len(shapes),
        scratch_shapes=[
            pltpu.VMEM((row_count, weights.shape[1]), jnp.bfloat16),
            pltpu.SemaphoreType.DMA,
        ],
        compiler_params=pltpu.CompilerParams(vmem_limit_bytes=20 * MIB),
        name="arrange",
    )(jnp.stack(place).astype(jnp.int32), weights, *earlier)


def terms_kernel(offsets, core_ref, kept_ref, received_ref, *rest):
    weights, outs, (buffer, sems) = rest[:7], rest[7:-2], rest[-2:]
    half = CHUNK // 2
    copies = []
    for i, offset in enumerate(offsets):
        part = 1 + 2 * max(0, offset // 2 - 1)
        at = offset if part == 1 else offset % 2
        targets = buffer.at[i, :CHUNK], buffer.at[i, pl.ds(CHUNK, half)], buffer.at[i, pl.ds(CHUNK + half, half)]
        sources = weights[0].at[offset], weights[part].at[at], weights[part + 1].at[at]
        for j in range(3):
            copies.append(pltpu.make_async_copy(sources[j], targets[j], sems.at[3 * i + j]))
            copies[-1].start()
    received = received_ref[...]
    low, high = received[:, :half], received[:, half:]
    first = jnp.full(low.shape, core_ref[0], jnp.int32) == 0
    rows = jnp.concatenate(
        [kept_ref[...], jnp.where(first, low, high), jnp.where(first, high, low)], axis=1
    )
    for i in range(len(offsets)):
        for copy in copies[3 * i : 3 * i + 3]:
            copy.wait()
        total = jnp.dot(rows, buffer[i], preferred_element_type=jnp.float32)
        outs[i][...] = total.astype(outs[i].dtype)


def terms(offsets, dtype, core, kept, received, own_weights, parts):
    count = len(offsets)
    return pl.pallas_call(
        functools.partial(terms_kernel, offsets),
        out_shape=[jax.ShapeDtypeStruct((CHUNK, PAIR_COLS), dtype)] * count,
        in_specs=[SMEM, VMEM, VMEM] + [ANY] * 7,
        out_specs=[VMEM] * count,
        scratch_shapes=[
            pltpu.VMEM((count, 2 * CHUNK, PAIR_COLS), jnp.bfloat16),
            pltpu.SemaphoreType.DMA((3 * count,)),
        ],
        compiler_params=pltpu.CompilerParams(vmem_limit_bytes=24 * MIB),
        name="terms",
    )(core.reshape(1), kept, received, own_weights, *parts)


GATHER_OFFSETS = [
    (dy, dx, core)
    for core in (0, 1)
    for dy, dx in ((0, 0), (1, 0), (0, 3), (0, 1), (0, 2), (1, 3), (1, 1), (1, 2))
]


def gather_ctx(block):
    other = to_other_y_hi(block)
    left, right = along_x(block, 1), along_x(block, -1)
    far = along_x(left, 1)
    left_other, right_other = along_x(other, 1), along_x(other, -1)
    far_other = along_x(right_other, -1)
    mine = [block, other, left, right, far, left_other, right_other, far_other]
    return mine + [
        to_other_core(jnp.stack(mine[:4])),
        to_other_core(jnp.stack(mine[4:7])),
        to_other_core(far_other),
    ]


def owners():
    me = lax.axis_index("ctx")
    return [
        ((me & 8) ^ (8 * dy)) | ((me + 2 * dx) & 6) | ((me & 1) ^ dc)
        for dy, dx, dc in GATHER_OFFSETS
    ]


def take_kernel(place_ref, k_ref, v_ref, out_ref, sems):
    columns = pl.ds(pl.multiple_of(place_ref[0] * HEAD_DIM, HEAD_DIM), HEAD_DIM)
    copies = [
        pltpu.make_async_copy(src.at[:, columns], out_ref.at[:, pl.ds(i * HEAD_DIM, HEAD_DIM)], sems.at[i])
        for i, src in enumerate((k_ref, v_ref))
    ]
    for copy in copies:
        copy.start()
    for copy in copies:
        copy.wait()


def take_kv(place, keys, values):
    rows = keys.shape[0]
    return pl.pallas_call(
        take_kernel,
        out_shape=jax.ShapeDtypeStruct((rows, 2 * HEAD_DIM), jnp.bfloat16),
        in_specs=[SMEM, ANY, ANY],
        out_specs=VMEM,
        scratch_shapes=[pltpu.SemaphoreType.DMA((2,))],
        compiler_params=pltpu.CompilerParams(vmem_limit_bytes=60 * MIB),
        name="take_kv",
    )(place.reshape(1), keys, values)


def attend_kernel(tiles, tile_chunks, chains, earlier, meta_ref, q_ref, *rest):
    pieces, outs, (kv, sems) = rest[: -2 - len(tiles) - earlier], rest[-2 - len(tiles) : -2], rest[-2:]
    blocks = []
    for piece in pieces:
        blocks += [piece] if len(piece.shape) == 2 else [piece.at[b] for b in range(piece.shape[0])]
    copies = []
    for block in blocks:
        for part in range(block.shape[0] // CHUNK):
            source = block.at[pl.ds(part * CHUNK, CHUNK)]
            copies.append(
                pltpu.make_async_copy(source, kv.at[meta_ref[len(copies)]], sems.at[len(copies)])
            )
            copies[-1].start()
    for copy in copies:
        copy.wait()
    span = tile_chunks * CHUNK
    for tile, (heads, out_ref) in enumerate(zip(tiles, outs)):
        limit = meta_ref[len(copies) + 2 * tile]
        first = pl.multiple_of(meta_ref[len(copies) + 2 * tile + 1], CHUNK)
        rows = q_ref.at[pl.ds(first, CHUNK)]
        each = len(heads) // chains
        queries = [
            jnp.concatenate(
                [rows[:, h * HEAD_DIM : (h + 1) * HEAD_DIM] for h in heads[g * each : (g + 1) * each]],
                axis=0,
            )
            for g in range(chains)
        ]
        height = each * CHUNK

        def step(i, state, masked):
            here = pl.ds(i * tile_chunks, tile_chunks)
            keys = kv[here, :, :HEAD_DIM].reshape(span, HEAD_DIM)
            values = kv[here, :, HEAD_DIM:].reshape(span, HEAD_DIM)
            if masked:
                column = lax.broadcasted_iota(jnp.int32, (height, span), 1) + i * span
                row = lax.broadcasted_iota(jnp.int32, (height, span), 0) % CHUNK
                visible = column <= row + (limit - 1) * CHUNK
            scores = [
                lax.dot_general(
                    query, keys, (((1,), (1,)), ((), ())), preferred_element_type=jnp.float32
                )
                for query in queries
            ]
            after = []
            for score, (highest, total, weighted) in zip(scores, state):
                if masked:
                    score = jnp.where(visible, score, masked_score)
                new_high = jnp.maximum(highest, jnp.max(score, axis=1, keepdims=True))
                fade = jnp.exp2((highest - new_high) * scale_log2)
                terms = jnp.exp2((score - new_high) * scale_log2)
                total = total * fade + jnp.sum(terms, axis=1, keepdims=True)
                weighted = weighted * fade + jnp.dot(
                    terms.astype(jnp.bfloat16), values, preferred_element_type=jnp.float32
                )
                after.append((new_high, total, weighted))
            return tuple(after)

        state = tuple(
            (
                jnp.full((height, 1), masked_score, jnp.float32),
                jnp.zeros((height, 1), jnp.float32),
                jnp.zeros((height, HEAD_DIM), jnp.float32),
            )
            for _ in range(chains)
        )
        whole = lax.div(limit - 1, jnp.int32(tile_chunks))
        state = lax.fori_loop(0, whole, functools.partial(step, masked=False), state)
        state = step(whole, state, True)
        for g, (_, total, weighted) in enumerate(state):
            result = (weighted / total).astype(jnp.bfloat16)
            for j in range(each):
                h = heads[g * each + j]
                out_ref[:, h * HEAD_DIM : (h + 1) * HEAD_DIM] = result[
                    j * CHUNK : (j + 1) * CHUNK
                ]


def attend(meta, queries, pieces, chunks, tiles, tile_chunks, chains, name, *earlier):
    return pl.pallas_call(
        functools.partial(attend_kernel, tiles, tile_chunks, chains, len(earlier)),
        out_shape=[jax.ShapeDtypeStruct((CHUNK, queries.shape[1]), jnp.bfloat16)] * len(tiles),
        in_specs=[SMEM, VMEM] + [ANY] * (len(pieces) + len(earlier)),
        out_specs=[VMEM] * len(tiles),
        scratch_shapes=[
            pltpu.VMEM((chunks, CHUNK, 2 * HEAD_DIM), jnp.bfloat16),
            pltpu.SemaphoreType.DMA((chunks,)),
        ],
        compiler_params=pltpu.CompilerParams(vmem_limit_bytes=24 * MIB),
        cost_estimate=pl.CostEstimate(
            flops=2_200_000_000, bytes_accessed=5_000_000, transcendentals=10_000_000
        ),
        name=name,
    )(meta, queries, *pieces, *earlier)


def ring_gather(block):
    half = block.shape[0] // 2
    below, above = [block], [block]
    for _ in range(3):
        below.append(along_z(below[-1], 1))
        above.append(along_z(above[-1], -1))
    far = [along_z(below[-1][:half], 1), along_z(above[-1][half:], -1)]
    return above + below[:0:-1] + far


RING_OFFSETS = (0, 1, 2, 3, 5, 6, 7, 4)


def hop_kernel(up_ref, down_ref, up_term_ref, down_term_ref, up_out_ref, down_out_ref):
    came = up_ref.shape[0]
    rest = CHUNK - came
    up_out_ref[:came] = (up_term_ref[:came] + up_ref[...]).astype(jnp.bfloat16)
    down_out_ref[rest:] = (down_term_ref[rest:] + down_ref[...]).astype(jnp.bfloat16)
    if rest:
        up_out_ref[came:] = up_term_ref[came:].astype(jnp.bfloat16)
        down_out_ref[:rest] = down_term_ref[:rest].astype(jnp.bfloat16)


def ring_reduce(far, near):
    half = far.shape[0] // 2
    up, down = along_z(far[:half], 1), along_z(far[half:], -1)
    for hop in (3, 2, 1):
        up, down = pl.pallas_call(
            hop_kernel,
            out_shape=[jax.ShapeDtypeStruct(far.shape, far.dtype)] * 2,
            in_specs=[VMEM] * 4,
            out_specs=[VMEM] * 2,
            compiler_params=pltpu.CompilerParams(vmem_limit_bytes=8 * MIB),
            name="hop",
        )(up, down, near[hop], near[8 - hop])
        up, down = along_z(up, 1), along_z(down, -1)
    return up.astype(jnp.float32) + down.astype(jnp.float32)


def load_features(refs):
    return [ref[...] for ref in refs[:7]] + [jnp.concatenate([refs[7][...], refs[8][...]], axis=0)]


def rope(value, cosine, sine):
    return value * cosine + pltpu.roll(value, HEAD_DIM // 2, axis=1) * sine


def project_kernel(z_ref, *rest):
    blocks, (gain_ref, cos_ref, sin_ref, w_ref, q_ref, kv_ref, w_vmem, sems) = rest[:9], rest[9:]
    copies = []
    for i, offset in enumerate(RING_OFFSETS):
        source = (z_ref[0] + offset) & 7
        for y_lo in (0, 1):
            rows = pl.ds(y_lo * COLS, COLS)
            copies.append(
                pltpu.make_async_copy(w_ref.at[y_lo * N_Z + source], w_vmem.at[i, rows], sems.at[len(copies)])
            )
            copies[-1].start()
    features = load_features(blocks)
    squares = jnp.zeros((CHUNK, 1), jnp.float32)
    for value in features:
        wide = value.astype(jnp.float32)
        squares = squares + jnp.sum(wide * wide, axis=1, keepdims=True)
    inverse = lax.rsqrt(squares / (16 * COLS) + norm_eps)
    total = jnp.zeros((CHUNK, w_vmem.shape[2]), jnp.float32)
    for i, value in enumerate(features):
        normed = (value.astype(jnp.float32) * inverse * gain_ref[i : i + 1]).astype(jnp.bfloat16)
        copies[2 * i].wait()
        copies[2 * i + 1].wait()
        total = total + jnp.dot(normed, w_vmem[i], preferred_element_type=jnp.float32)
    cosine, sine = cos_ref[...], sin_ref[...]
    for h in range(GROUP):
        at = slice(h * HEAD_DIM, (h + 1) * HEAD_DIM)
        q_ref[:, at] = rope(total[:, at], cosine, sine).astype(jnp.bfloat16)
    at = GROUP * HEAD_DIM
    kv_ref[:, :HEAD_DIM] = rope(total[:, at : at + HEAD_DIM], cosine, sine).astype(jnp.bfloat16)
    kv_ref[:, HEAD_DIM:] = total[:, at + HEAD_DIM :].astype(jnp.bfloat16)


def project(z, blocks, gain, cosine, sine, weights):
    width = weights.shape[2]
    return pl.pallas_call(
        project_kernel,
        out_shape=(
            jax.ShapeDtypeStruct((CHUNK, GROUP * HEAD_DIM), jnp.bfloat16),
            jax.ShapeDtypeStruct((CHUNK, 2 * HEAD_DIM), jnp.bfloat16),
        ),
        in_specs=[SMEM] + [VMEM] * 12 + [ANY],
        out_specs=(VMEM, VMEM),
        scratch_shapes=[
            pltpu.VMEM((N_Z, PAIR_COLS, width), jnp.bfloat16),
            pltpu.SemaphoreType.DMA((2 * N_Z,)),
        ],
        compiler_params=pltpu.CompilerParams(vmem_limit_bytes=54 * MIB),
        name="norm_project",
    )(z.reshape(1), *blocks, gain, cosine, sine, weights)


def finish_kernel(place_ref, *rest):
    blocks, (mixed_ref, w_ref, own_ref, other_ref, w_vmem, sems) = rest[:9], rest[9:]
    copies = []
    for i, offset in enumerate(RING_OFFSETS):
        source = (place_ref[1] + offset) & 7
        rows = w_ref.at[:, pl.ds(2 * source, 2)]
        copies.append(pltpu.make_async_copy(rows, w_vmem.at[i], sems.at[i]))
        copies[-1].start()
    features = load_features(blocks)
    total = mixed_ref[...].astype(jnp.float32)
    for i, value in enumerate(features):
        copies[i].wait()
        for j in (0, 1):
            total = total + jnp.dot(
                value[:, j * 2 * HEAD_DIM : (j + 1) * 2 * HEAD_DIM],
                w_vmem[i, :, j].reshape(2 * HEAD_DIM, PAIR_COLS),
                preferred_element_type=jnp.float32,
            )
    first, second = total[:, :COLS].astype(jnp.bfloat16), total[:, COLS:].astype(jnp.bfloat16)

    @pl.when(place_ref[0] == 0)
    def _():
        own_ref[...] = first
        other_ref[...] = second

    @pl.when(place_ref[0] == 1)
    def _():
        own_ref[...] = second
        other_ref[...] = first


def finish(place, blocks, mixed, weights):
    part = jax.ShapeDtypeStruct((CHUNK, COLS), jnp.bfloat16)
    return pl.pallas_call(
        finish_kernel,
        out_shape=(part, part),
        in_specs=[SMEM] + [VMEM] * 10 + [ANY],
        out_specs=(VMEM, VMEM),
        scratch_shapes=[
            pltpu.VMEM((N_Z, N_CTX, 2, weights.shape[2], PAIR_COLS), jnp.bfloat16),
            pltpu.SemaphoreType.DMA((N_Z,)),
        ],
        compiler_params=pltpu.CompilerParams(vmem_limit_bytes=57 * MIB),
        name="project_out",
    )(place, *blocks, mixed, weights)


def turned(blocks, first):
    return lax.dynamic_slice_in_dim(jnp.concatenate([blocks, blocks], axis=0), first, N_Z, 0)


def in_order(first, own, other, axis):
    return jnp.where(
        first, jnp.concatenate([own, other], axis=axis), jnp.concatenate([other, own], axis=axis)
    )


def per_device(
    residual,
    global_q,
    global_k,
    global_v,
    global_wo,
    norm_gain,
    stretch_wq,
    stretch_wk,
    stretch_wv,
    stretch_wo,
):
    me = lax.axis_index("ctx")
    place = lax.axis_index("tp")
    y_lo, z = place // N_Z, place % N_Z
    lower = y_lo == 0
    core = me & 1

    limits = jnp.where(lower, me + 1, 2 * N_CTX - me), jnp.where(lower, 2 * N_CTX - me, me + 1)
    kept_at, given_at = y_lo * CHUNK, (1 - y_lo) * CHUNK
    slots = [slot for c in owners() for slot in (c, 2 * N_CTX - 1 - c)]
    meta = jnp.stack(slots + [limits[0], kept_at, limits[1], given_at]).astype(jnp.int32)

    kv = take_kv(place // 2, global_k, global_v)
    rows = stretch_wo.shape[0] // N_CTX
    (share,) = arrange(z, me * rows, None, stretch_wo, rows, kv)
    share = share.reshape(2, 2, 2, rows, PAIR_COLS)
    first_weights, half_mine = arrange(
        z, jnp.int32(0), core, global_wo, global_wo.shape[0], share
    )
    other, left, right, came, half_mine = together(
        to_other_y_hi(kv), along_x(kv, 1), along_x(kv, -1), along_z(share[:, :, 1], 1), half_mine
    )
    share = jnp.stack([share[:, :, 0], came], axis=2)
    far, left_other, right_other, came, half_mine_a = together(
        along_x(left, 1),
        along_x(other, 1),
        along_x(other, -1),
        along_z(share[:, 1], 2),
        to_other_y_lo(half_mine[:4]),
    )
    share = jnp.stack([share[:, 0], came], axis=1)
    swapped = to_other_core(jnp.stack([kv, other, left, right]))
    swapped_far = to_other_core(jnp.stack([far, left_other, right_other]))
    half_other_a = to_other_core(half_mine_a)
    far_other, came, half_mine_b = together(
        along_x(right_other, -1), along_z(share[1], 4), to_other_y_lo(half_mine[4:6])
    )
    half_other_b = to_other_core(half_mine_b)
    half_mine_c = to_other_y_lo(half_mine[6:])
    share = jnp.stack([share[0], came], axis=0)
    share = turned(share.reshape(N_Z, rows, PAIR_COLS)[::-1], 7 - z)
    share_other = to_other_y_lo(share)
    swapped_last = to_other_core(far_other)
    pieces = [kv, other, left, right, far, left_other, right_other, far_other]
    pieces += [swapped, swapped_far, swapped_last]

    own_wq = copy_after(stretch_wq, far_other)
    other_wq = permute(own_wq, "tp", lambda t: 8 * (1 - t % 2) + t // 2)
    own_wq = permute(own_wq, "tp", lambda t: 8 * (t % 2) + t // 2)
    weights = jnp.concatenate(
        [
            in_order(lower, own_wq, other_wq, 1),
            lax.dynamic_slice_in_dim(stretch_wk, z * HEAD_DIM, HEAD_DIM, 1),
            lax.dynamic_slice_in_dim(stretch_wv, z * HEAD_DIM, HEAD_DIM, 1),
        ],
        axis=1,
    )
    share, weights = together(in_order(lower, share, share_other, 0), weights)
    gathered_weights = lax.all_gather(weights, "ctx", axis=0, tiled=False)
    last_weights = lax.all_gather(share, "ctx", axis=0, tiled=False)

    kept = lax.dynamic_slice_in_dim(residual, kept_at, CHUNK, 0)
    given = lax.dynamic_slice_in_dim(residual, given_at, CHUNK, 0)
    residual_pair = in_order(lower, kept, to_other_y_lo(given), 1)

    kept, given = attend(
        meta,
        global_q,
        pieces,
        2 * N_CTX,
        ((0, 1), (0, 1)),
        4,
        2,
        "attend_all",
        share,
        residual_pair,
        half_mine_c,
        half_other_a,
        half_other_b,
    )
    half_other_c = to_other_core(half_mine_c)
    received = to_other_y_lo(given)
    parts = half_mine_a, half_other_a, half_mine_b, half_other_b, half_mine_c, half_other_c
    operands = core, kept, received, first_weights, parts
    (far,) = terms((4,), jnp.bfloat16, *operands)
    offsets = (3, 5, 2, 6, 1, 7, 0)
    near = dict(zip(offsets, terms(offsets, jnp.float32, *operands)))
    others = ring_reduce(far, near)
    mixed = (residual_pair.astype(jnp.float32) + near[0] + others).astype(jnp.bfloat16)

    blocks = ring_gather(mixed)
    gain = norm_gain.reshape(2, N_Z, COLS).transpose(1, 0, 2).reshape(N_Z, PAIR_COLS)
    gain = jnp.stack([gain[(z + offset) % N_Z] for offset in RING_OFFSETS])
    chunk = jnp.where(lower, me, 2 * N_CTX - 1 - me)
    positions = (chunk * CHUNK + jnp.arange(CHUNK, dtype=jnp.int32)).astype(jnp.float32)
    half_dim = HEAD_DIM // 2
    inv_freq = rope_base ** (-(jnp.arange(half_dim).astype(jnp.float32) * 2.0 / HEAD_DIM))
    angles = positions[:, None] * inv_freq[None, :]
    cosine, sine = jnp.cos(angles), jnp.sin(angles)
    stretch_q, stretch_kv = project(
        z,
        blocks,
        gain,
        jnp.concatenate([cosine, cosine], axis=1),
        jnp.concatenate([-sine, sine], axis=1),
        gathered_weights,
    )
    pieces = gather_ctx(stretch_kv)
    slots = [jnp.where(lower, c, N_CTX - 1 - c) for c in owners()]
    limit = jnp.where(lower, me + 1, N_CTX - me)
    meta = jnp.stack(slots + [limit, 0]).astype(jnp.int32)
    (attended,) = attend(
        meta, stretch_q, pieces, N_CTX, ((0, 1, 2, 3),), 4, 2, "attend_window"
    )
    own, other = finish(
        jnp.stack([y_lo, z]).astype(jnp.int32), ring_gather(attended), mixed, last_weights
    )
    return in_order(lower, own, to_other_y_lo(other), 0)


def solution(mesh):
    in_specs = (
        P("ctx", "tp"),
        P("ctx", "tp"),
        P("ctx", None),
        P("ctx", None),
        P("tp", None),
        P(),
        P("ctx", "tp"),
        P("ctx", None),
        P("ctx", None),
        P("tp", None),
    )
    return jax.shard_map(
        per_device, mesh=mesh, in_specs=in_specs, out_specs=P("ctx", "tp"), check_vma=False
    )
```

```python
import functools

import jax
import jax.numpy as jnp
from jax import lax
from jax.experimental import pallas as pl
from jax.experimental.pallas import tpu as pltpu
from jax.sharding import PartitionSpec as P

HEAD_DIM = 128
GROUP = 4
CHUNK = 256
N_CTX = 16
N_Z = 8
COLS = 320
PAIR_COLS = 2 * COLS
rope_base = 500000.0
norm_eps = 1e-05
masked_score = -1e30
scale_log2 = 1.4426950408889634 * HEAD_DIM**-0.5
MIB = 1024 * 1024
SMEM = pl.BlockSpec(memory_space=pltpu.SMEM)
VMEM = pl.BlockSpec(memory_space=pltpu.VMEM)
HBM = pl.BlockSpec(memory_space=pltpu.HBM)


def permute(value, axis, target):
    return lax.ppermute(value, axis, [(place, target(place)) for place in range(16)])


def to_other_core(value):
    return permute(value, "ctx", lambda c: c ^ 1)


def to_other_y_hi(value):
    return permute(value, "ctx", lambda c: c ^ 8)


def along_x(value, step):
    return permute(value, "ctx", lambda c: (c & 9) | ((c + 2 * step) & 6))


def to_other_y_lo(value):
    return permute(value, "tp", lambda t: t ^ 8)


def along_z(value, step):
    return permute(value, "tp", lambda t: (t & 8) | ((t + step) & 7))


def together_kernel(count, stacked, *refs):
    if stacked:
        out, sems = refs[-2:]
        sources = refs[count - stacked : count]
        copies = [
            pltpu.make_async_copy(source, out.at[i], sems.at[i])
            for i, source in enumerate(sources)
        ]
        for copy in copies:
            copy.start()
        for copy in copies:
            copy.wait()


def together(*values, stacked=0):
    shapes = [jax.ShapeDtypeStruct(value.shape, value.dtype) for value in values]
    if stacked:
        shapes.append(jax.ShapeDtypeStruct((stacked, *values[-1].shape), values[-1].dtype))
    return pl.pallas_call(
        functools.partial(together_kernel, len(values), stacked),
        out_shape=shapes,
        in_specs=[HBM] * len(values),
        out_specs=[HBM] * len(shapes),
        input_output_aliases={i: i for i in range(len(values))},
        scratch_shapes=[pltpu.SemaphoreType.DMA((stacked,))] if stacked else [],
        compiler_params=pltpu.CompilerParams(vmem_limit_bytes=MIB),
        name="together",
    )(*values)


def copy_kernel(source, *rest):
    copy = pltpu.make_async_copy(source, rest[-2], rest[-1])
    copy.start()
    copy.wait()


def copy_after(value, *earlier):
    return pl.pallas_call(
        copy_kernel,
        out_shape=jax.ShapeDtypeStruct(value.shape, value.dtype),
        in_specs=[HBM] * (1 + len(earlier)),
        out_specs=HBM,
        scratch_shapes=[pltpu.SemaphoreType.DMA],
        compiler_params=pltpu.CompilerParams(vmem_limit_bytes=60 * MIB),
        name="copy_after",
    )(value, *earlier)


PARTS = ((0, 1, 2), (3, 4, 5), (6, 7))


def arrange_kernel(row_count, earlier, place_ref, source, *rest):
    outs, (rows, sem) = rest[earlier:-2], rest[-2:]
    first = pl.multiple_of(place_ref[1], 16)
    copy = pltpu.make_async_copy(source.at[pl.ds(first, row_count)], rows, sem)
    copy.start()
    copy.wait()
    for z in range(N_Z):
        offset = (z - place_ref[0]) & 7
        for y_lo in (0, 1):
            at = (y_lo * N_Z + z) * COLS
            outs[0][offset, :, y_lo * COLS : (y_lo + 1) * COLS] = rows[:, at : at + COLS]
    for out, part in zip(outs[1:], PARTS):
        height = out.shape[1]
        half = pl.ds(pl.multiple_of(place_ref[2], height), height)
        out[...] = outs[0][part[0] : part[-1] + 1, half, :]


def arrange(z, first, half, weights, row_count, *earlier):
    shapes = [jax.ShapeDtypeStruct((N_Z, row_count, PAIR_COLS), jnp.bfloat16)]
    place = [z, first]
    if half is not None:
        for part in PARTS:
            shapes.append(
                jax.ShapeDtypeStruct((len(part), row_count // 2, PAIR_COLS), jnp.bfloat16)
            )
        place.append(half * (row_count // 2))
    return pl.pallas_call(
        functools.partial(arrange_kernel, row_count, len(earlier)),
        out_shape=shapes,
        in_specs=[SMEM] + [HBM] * (1 + len(earlier)),
        out_specs=[VMEM] * len(shapes),
        scratch_shapes=[
            pltpu.VMEM((row_count, weights.shape[1]), jnp.bfloat16),
            pltpu.SemaphoreType.DMA,
        ],
        compiler_params=pltpu.CompilerParams(vmem_limit_bytes=60 * MIB),
        name="arrange",
    )(jnp.stack(place).astype(jnp.int32), weights, *earlier)


def pack_kernel(place_ref, k_ref, v_ref, own_ref, other_ref, out_ref, sems):
    def columns(first, width):
        return pl.ds(pl.multiple_of(first, HEAD_DIM), width)

    wide = own_ref.shape[1]
    head = columns(place_ref[1] * HEAD_DIM, HEAD_DIM)
    moves = (
        (own_ref, columns(place_ref[0] * wide, wide)),
        (other_ref, columns((1 - place_ref[0]) * wide, wide)),
        (k_ref.at[:, head], pl.ds(2 * wide, HEAD_DIM)),
        (v_ref.at[:, head], pl.ds(2 * wide + HEAD_DIM, HEAD_DIM)),
    )
    copies = [
        pltpu.make_async_copy(source, out_ref.at[:, target], sems.at[i])
        for i, (source, target) in enumerate(moves)
    ]
    for copy in copies:
        copy.start()
    for copy in copies:
        copy.wait()


def pack(place, keys, values, own, other):
    rows, wide = own.shape
    return pl.pallas_call(
        pack_kernel,
        out_shape=jax.ShapeDtypeStruct((rows, 2 * (wide + HEAD_DIM)), jnp.bfloat16),
        in_specs=[SMEM] + [HBM] * 4,
        out_specs=HBM,
        scratch_shapes=[pltpu.SemaphoreType.DMA((4,))],
        compiler_params=pltpu.CompilerParams(vmem_limit_bytes=MIB),
        name="pack",
    )(place, keys, values, own, other)


def split_kernel(place_ref, value_ref, *rest):
    outs, sems = rest[-3:-1], rest[-1]
    copies = []
    for i, half in enumerate((place_ref[0], 1 - place_ref[0])):
        rows = pl.ds(pl.multiple_of(half * CHUNK, CHUNK), CHUNK)
        copies.append(pltpu.make_async_copy(value_ref.at[rows], outs[i], sems.at[i]))
        copies[-1].start()
    for copy in copies:
        copy.wait()


def split(place, value, earlier):
    half = jax.ShapeDtypeStruct((CHUNK, value.shape[1]), value.dtype)
    return pl.pallas_call(
        split_kernel,
        out_shape=(half, half),
        in_specs=[SMEM, HBM, HBM],
        out_specs=(VMEM, VMEM),
        scratch_shapes=[pltpu.SemaphoreType.DMA((2,))],
        compiler_params=pltpu.CompilerParams(vmem_limit_bytes=MIB),
        name="split",
    )(place, value, earlier)


def mix_kernel(place_ref, kept_ref, came_ref, own_ref, up_ref, down_ref, out_ref):
    total = own_ref[...] + up_ref[...].astype(jnp.float32) + down_ref[...].astype(jnp.float32)

    def put(first, second):
        residual = (first[...].astype(jnp.float32), second[...].astype(jnp.float32))
        out_ref[:, :COLS] = (total[:, :COLS] + residual[0]).astype(jnp.bfloat16)
        out_ref[:, COLS:] = (total[:, COLS:] + residual[1]).astype(jnp.bfloat16)

    pl.when(place_ref[0] == 0)(lambda: put(kept_ref, came_ref))
    pl.when(place_ref[0] == 1)(lambda: put(came_ref, kept_ref))


def mix(place, kept, came, own, up, down):
    return pl.pallas_call(
        mix_kernel,
        out_shape=jax.ShapeDtypeStruct(up.shape, jnp.bfloat16),
        in_specs=[SMEM] + [VMEM] * 5,
        out_specs=VMEM,
        compiler_params=pltpu.CompilerParams(vmem_limit_bytes=8 * MIB),
        name="mix",
    )(place, kept, came, own, up, down)


def terms_kernel(offsets, core_ref, kept_ref, received_ref, *rest):
    weights, outs, (buffer, sems) = rest[:7], rest[7:-2], rest[-2:]
    half = CHUNK // 2
    copies = []
    for i, offset in enumerate(offsets):
        part, at = 1 + 2 * (offset // 3), offset % 3
        targets = [
            buffer.at[i, pl.ds(first, rows)]
            for first, rows in ((0, CHUNK), (CHUNK, half), (CHUNK + half, half))
        ]
        sources = weights[0].at[offset], weights[part].at[at], weights[part + 1].at[at]
        for j in range(3):
            copies.append(pltpu.make_async_copy(sources[j], targets[j], sems.at[3 * i + j]))
            copies[-1].start()
    received = received_ref[...]
    low, high = received[:, :half], received[:, half:]
    first = jnp.full(low.shape, core_ref[0], jnp.int32) == 0
    rows = jnp.concatenate(
        [kept_ref[...], jnp.where(first, low, high), jnp.where(first, high, low)], axis=1
    )
    for i in range(len(offsets)):
        for copy in copies[3 * i : 3 * i + 3]:
            copy.wait()
        total = jnp.dot(rows, buffer[i], preferred_element_type=jnp.float32)
        outs[i][...] = total.astype(outs[i].dtype)


def terms(offsets, dtype, core, kept, received, own_weights, parts):
    count = len(offsets)
    return pl.pallas_call(
        functools.partial(terms_kernel, offsets),
        out_shape=[jax.ShapeDtypeStruct((CHUNK, PAIR_COLS), dtype)] * count,
        in_specs=[SMEM, VMEM, VMEM] + [HBM] * 7,
        out_specs=[VMEM] * count,
        scratch_shapes=[
            pltpu.VMEM((count, 2 * CHUNK, PAIR_COLS), jnp.bfloat16),
            pltpu.SemaphoreType.DMA((3 * count,)),
        ],
        compiler_params=pltpu.CompilerParams(vmem_limit_bytes=24 * MIB),
        name="terms",
    )(core.reshape(1), kept, received, own_weights, *parts)


GATHER_OFFSETS = [
    (dy, dx, core)
    for core in (0, 1)
    for dy, dx in ((0, 0), (1, 0), (0, 3), (0, 1), (0, 2), (1, 3), (1, 1), (1, 2))
]


def gather_ctx(block):
    other = to_other_y_hi(block)
    left, right = along_x(block, 1), along_x(block, -1)
    far = along_x(left, 1)
    left_other, right_other = along_x(other, 1), along_x(other, -1)
    far_other = along_x(right_other, -1)
    mine = [block, other, left, right, far, left_other, right_other, far_other]
    return mine + [
        to_other_core(jnp.stack(mine[:4])),
        to_other_core(jnp.stack(mine[4:7])),
        to_other_core(far_other),
    ]


def owners():
    me = lax.axis_index("ctx")
    return [
        ((me & 8) ^ (8 * dy)) | ((me + 2 * dx) & 6) | ((me & 1) ^ dc)
        for dy, dx, dc in GATHER_OFFSETS
    ]


def take_kernel(place_ref, k_ref, v_ref, out_ref, sems):
    columns = pl.ds(pl.multiple_of(place_ref[0] * HEAD_DIM, HEAD_DIM), HEAD_DIM)
    copies = [
        pltpu.make_async_copy(src.at[:, columns], out_ref.at[:, pl.ds(i * HEAD_DIM, HEAD_DIM)], sems.at[i])
        for i, src in enumerate((k_ref, v_ref))
    ]
    for copy in copies:
        copy.start()
    for copy in copies:
        copy.wait()


def take_kv(place, keys, values):
    rows = keys.shape[0]
    return pl.pallas_call(
        take_kernel,
        out_shape=jax.ShapeDtypeStruct((rows, 2 * HEAD_DIM), jnp.bfloat16),
        in_specs=[SMEM, HBM, HBM],
        out_specs=VMEM,
        scratch_shapes=[pltpu.SemaphoreType.DMA((2,))],
        compiler_params=pltpu.CompilerParams(vmem_limit_bytes=60 * MIB),
        name="take_kv",
    )(place.reshape(1), keys, values)


def attend_kernel(tiles, tile_chunks, chains, earlier, meta_ref, q_ref, *rest):
    pieces, outs, (kv, sems) = rest[: -2 - len(tiles) - earlier], rest[-2 - len(tiles) : -2], rest[-2:]
    blocks = []
    for piece in pieces:
        blocks += [piece] if len(piece.shape) == 2 else [piece.at[b] for b in range(piece.shape[0])]
    copies = []
    for block in blocks:
        for part in range(block.shape[0] // CHUNK):
            source = block.at[pl.ds(part * CHUNK, CHUNK)]
            copies.append(
                pltpu.make_async_copy(source, kv.at[meta_ref[len(copies)]], sems.at[len(copies)])
            )
            copies[-1].start()
    for copy in copies:
        copy.wait()
    span = tile_chunks * CHUNK
    for tile, (heads, out_ref) in enumerate(zip(tiles, outs)):
        limit = meta_ref[len(copies) + 2 * tile]
        first = pl.multiple_of(meta_ref[len(copies) + 2 * tile + 1], CHUNK)
        rows = q_ref.at[pl.ds(first, CHUNK)]
        each = len(heads) // chains
        queries = [
            jnp.concatenate(
                [rows[:, h * HEAD_DIM : (h + 1) * HEAD_DIM] for h in heads[g * each : (g + 1) * each]],
                axis=0,
            )
            for g in range(chains)
        ]
        height = each * CHUNK

        def step(i, state, masked):
            here = pl.ds(i * tile_chunks, tile_chunks)
            keys = kv[here, :, :HEAD_DIM].reshape(span, HEAD_DIM)
            values = kv[here, :, HEAD_DIM:].reshape(span, HEAD_DIM)
            if masked:
                column = lax.broadcasted_iota(jnp.int32, (height, span), 1) + i * span
                row = lax.broadcasted_iota(jnp.int32, (height, span), 0) % CHUNK
                visible = column <= row + (limit - 1) * CHUNK
            scores = [
                lax.dot_general(
                    query, keys, (((1,), (1,)), ((), ())), preferred_element_type=jnp.float32
                )
                for query in queries
            ]
            after = []
            for score, (highest, total, weighted) in zip(scores, state):
                if masked:
                    score = jnp.where(visible, score, masked_score)
                new_high = jnp.maximum(highest, jnp.max(score, axis=1, keepdims=True))
                fade = jnp.exp2((highest - new_high) * scale_log2)
                terms = jnp.exp2((score - new_high) * scale_log2)
                total = total * fade + jnp.sum(terms, axis=1, keepdims=True)
                weighted = weighted * fade + jnp.dot(
                    terms.astype(jnp.bfloat16), values, preferred_element_type=jnp.float32
                )
                after.append((new_high, total, weighted))
            return tuple(after)

        state = tuple(
            (
                jnp.full((height, 1), masked_score, jnp.float32),
                jnp.zeros((height, 1), jnp.float32),
                jnp.zeros((height, HEAD_DIM), jnp.float32),
            )
            for _ in range(chains)
        )
        whole = lax.div(limit - 1, jnp.int32(tile_chunks))
        state = lax.fori_loop(0, whole, functools.partial(step, masked=False), state)
        state = step(whole, state, True)
        for g, (_, total, weighted) in enumerate(state):
            result = (weighted / total).astype(jnp.bfloat16)
            for j in range(each):
                h = heads[g * each + j]
                out_ref[:, h * HEAD_DIM : (h + 1) * HEAD_DIM] = result[
                    j * CHUNK : (j + 1) * CHUNK
                ]


def attend(meta, queries, pieces, chunks, tiles, tile_chunks, chains, name, *earlier):
    return pl.pallas_call(
        functools.partial(attend_kernel, tiles, tile_chunks, chains, len(earlier)),
        out_shape=[jax.ShapeDtypeStruct((CHUNK, queries.shape[1]), jnp.bfloat16)] * len(tiles),
        in_specs=[SMEM, VMEM] + [HBM] * (len(pieces) + len(earlier)),
        out_specs=[VMEM] * len(tiles),
        scratch_shapes=[
            pltpu.VMEM((chunks, CHUNK, 2 * HEAD_DIM), jnp.bfloat16),
            pltpu.SemaphoreType.DMA((chunks,)),
        ],
        compiler_params=pltpu.CompilerParams(vmem_limit_bytes=24 * MIB),
        cost_estimate=pl.CostEstimate(
            flops=2_200_000_000, bytes_accessed=5_000_000, transcendentals=10_000_000
        ),
        name=name,
    )(meta, queries, *pieces, *earlier)


def ring_gather(block):
    half = block.shape[0] // 2
    below, above = [block], [block]
    for _ in range(3):
        below.append(along_z(below[-1], 1))
        above.append(along_z(above[-1], -1))
    far = [along_z(below[-1][:half], 1), along_z(above[-1][half:], -1)]
    return above + below[:0:-1] + far


RING_OFFSETS = (0, 1, 2, 3, 5, 6, 7, 4)


def hop_kernel(up_ref, down_ref, up_term_ref, down_term_ref, _, up_out_ref, down_out_ref):
    came = up_ref.shape[0]
    rest = CHUNK - came
    up_out_ref[:came] = (up_term_ref[:came] + up_ref[...]).astype(jnp.bfloat16)
    down_out_ref[rest:] = (down_term_ref[rest:] + down_ref[...]).astype(jnp.bfloat16)
    if rest:
        up_out_ref[came:] = up_term_ref[came:].astype(jnp.bfloat16)
        down_out_ref[:rest] = down_term_ref[:rest].astype(jnp.bfloat16)


def ring_reduce(far, near, earlier):
    half = far.shape[0] // 2
    up, down = along_z(far[:half], 1), along_z(far[half:], -1)
    for hop in (3, 2, 1):
        up, down = pl.pallas_call(
            hop_kernel,
            out_shape=[jax.ShapeDtypeStruct(far.shape, far.dtype)] * 2,
            in_specs=[VMEM] * 4 + [HBM],
            out_specs=[VMEM] * 2,
            compiler_params=pltpu.CompilerParams(vmem_limit_bytes=8 * MIB),
            name="hop",
        )(up, down, near[hop], near[8 - hop], earlier)
        up, down = along_z(up, 1), along_z(down, -1)
    return up, down


def load_features(refs):
    return [ref[...] for ref in refs[:7]] + [jnp.concatenate([refs[7][...], refs[8][...]], axis=0)]


def rope(value, cosine, sine):
    return value * cosine + pltpu.roll(value, HEAD_DIM // 2, axis=1) * sine


def project_kernel(z_ref, *rest):
    blocks, (gain_ref, cos_ref, sin_ref, w_ref, q_ref, kv_ref, w_vmem, sems) = rest[:9], rest[9:]
    copies = []
    for i, offset in enumerate(RING_OFFSETS):
        source = (z_ref[0] + offset) & 7
        for y_lo in (0, 1):
            rows = pl.ds(y_lo * COLS, COLS)
            copies.append(
                pltpu.make_async_copy(w_ref.at[y_lo * N_Z + source], w_vmem.at[i, rows], sems.at[len(copies)])
            )
            copies[-1].start()
    features = load_features(blocks)
    squares = jnp.zeros((CHUNK, 1), jnp.float32)
    for value in features:
        wide = value.astype(jnp.float32)
        squares = squares + jnp.sum(wide * wide, axis=1, keepdims=True)
    inverse = lax.rsqrt(squares / (16 * COLS) + norm_eps)
    total = jnp.zeros((CHUNK, w_vmem.shape[2]), jnp.float32)
    for i, value in enumerate(features):
        normed = (value.astype(jnp.float32) * inverse * gain_ref[i : i + 1]).astype(jnp.bfloat16)
        copies[2 * i].wait()
        copies[2 * i + 1].wait()
        total = total + jnp.dot(normed, w_vmem[i], preferred_element_type=jnp.float32)
    cosine, sine = cos_ref[...], sin_ref[...]
    for h in range(GROUP):
        at = slice(h * HEAD_DIM, (h + 1) * HEAD_DIM)
        q_ref[:, at] = rope(total[:, at], cosine, sine).astype(jnp.bfloat16)
    at = GROUP * HEAD_DIM
    kv_ref[:, :HEAD_DIM] = rope(total[:, at : at + HEAD_DIM], cosine, sine).astype(jnp.bfloat16)
    kv_ref[:, HEAD_DIM:] = total[:, at + HEAD_DIM :].astype(jnp.bfloat16)


def project(z, blocks, gain, cosine, sine, weights):
    width = weights.shape[2]
    return pl.pallas_call(
        project_kernel,
        out_shape=(
            jax.ShapeDtypeStruct((CHUNK, GROUP * HEAD_DIM), jnp.bfloat16),
            jax.ShapeDtypeStruct((CHUNK, 2 * HEAD_DIM), jnp.bfloat16),
        ),
        in_specs=[SMEM] + [VMEM] * 12 + [HBM],
        out_specs=(VMEM, VMEM),
        scratch_shapes=[
            pltpu.VMEM((N_Z, PAIR_COLS, width), jnp.bfloat16),
            pltpu.SemaphoreType.DMA((2 * N_Z,)),
        ],
        compiler_params=pltpu.CompilerParams(vmem_limit_bytes=54 * MIB),
        name="norm_project",
    )(z.reshape(1), *blocks, gain, cosine, sine, weights)


def finish_kernel(place_ref, *rest):
    blocks, (mixed_ref, w_ref, own_ref, other_ref, w_vmem, sems) = rest[:9], rest[9:]
    copies = []
    for i, offset in enumerate(RING_OFFSETS):
        source = (place_ref[1] + offset) & 7
        for j in (0, 1):
            at = (place_ref[1] - 2 * source - j) & 7
            at = at + N_Z * ((source >> 2) ^ place_ref[0])
            copies.append(pltpu.make_async_copy(w_ref.at[:, at], w_vmem.at[i, j], sems.at[2 * i + j]))
            copies[-1].start()
    features = load_features(blocks)
    total = mixed_ref[...].astype(jnp.float32)
    for i, value in enumerate(features):
        for j in (0, 1):
            copies[2 * i + j].wait()
            total = total + jnp.dot(
                value[:, j * 2 * HEAD_DIM : (j + 1) * 2 * HEAD_DIM],
                w_vmem[i, j].reshape(2 * HEAD_DIM, PAIR_COLS),
                preferred_element_type=jnp.float32,
            )
    first, second = total[:, :COLS].astype(jnp.bfloat16), total[:, COLS:].astype(jnp.bfloat16)

    @pl.when(place_ref[0] == 0)
    def _():
        own_ref[...] = first
        other_ref[...] = second

    @pl.when(place_ref[0] == 1)
    def _():
        own_ref[...] = second
        other_ref[...] = first


def finish(place, blocks, mixed, weights):
    part = jax.ShapeDtypeStruct((CHUNK, COLS), jnp.bfloat16)
    return pl.pallas_call(
        finish_kernel,
        out_shape=(part, part),
        in_specs=[SMEM] + [VMEM] * 10 + [HBM],
        out_specs=(VMEM, VMEM),
        scratch_shapes=[
            pltpu.VMEM((N_Z, 2, N_CTX, weights.shape[2], PAIR_COLS), jnp.bfloat16),
            pltpu.SemaphoreType.DMA((2 * N_Z,)),
        ],
        compiler_params=pltpu.CompilerParams(vmem_limit_bytes=57 * MIB),
        name="project_out",
    )(place, *blocks, mixed, weights)


def turned(blocks, first):
    return lax.dynamic_slice_in_dim(jnp.concatenate([blocks, blocks], axis=0), first, N_Z, 0)


def in_order(first, own, other, axis):
    return jnp.where(
        first, jnp.concatenate([own, other], axis=axis), jnp.concatenate([other, own], axis=axis)
    )


def per_device(
    residual,
    global_q,
    global_k,
    global_v,
    global_wo,
    norm_gain,
    stretch_wq,
    stretch_wk,
    stretch_wv,
    stretch_wo,
):
    me = lax.axis_index("ctx")
    place = lax.axis_index("tp")
    y_lo, z = place // N_Z, place % N_Z
    lower = y_lo == 0
    core = me & 1

    limits = jnp.where(lower, me + 1, 2 * N_CTX - me), jnp.where(lower, 2 * N_CTX - me, me + 1)
    kept_at, given_at = y_lo * CHUNK, (1 - y_lo) * CHUNK
    slots = [slot for c in owners() for slot in (c, 2 * N_CTX - 1 - c)]
    meta = jnp.stack(slots + [limits[0], kept_at, limits[1], given_at]).astype(jnp.int32)

    place_pair = jnp.stack([y_lo, z]).astype(jnp.int32)
    kv = take_kv(place // 2, global_k, global_v)
    own_wq = permute(copy_after(stretch_wq, kv), "tp", lambda t: 8 * (t % 2) + t // 2)
    rows = stretch_wo.shape[0] // N_CTX
    (share,) = arrange(z, me * rows, None, stretch_wo, rows, kv)
    share = share.reshape(2, 2, 2, rows, PAIR_COLS)
    first_weights, *halves = arrange(
        z, jnp.int32(0), core, global_wo, global_wo.shape[0], share
    )
    came, half, kv, other, left, right, near = together(
        along_z(share[:, :, 1], 1),
        halves[0],
        kv,
        to_other_y_hi(kv),
        along_x(kv, 1),
        along_x(kv, -1),
        stacked=4,
    )
    share = jnp.stack([share[:, :, 0], came], axis=2)
    came, half_a, own_wq, far, left_other, right_other, middle = together(
        along_z(share[:, 1], 2),
        to_other_y_lo(half),
        own_wq,
        along_x(left, 1),
        along_x(other, 1),
        along_x(other, -1),
        stacked=3,
    )
    share = jnp.stack([share[:, 0], came], axis=1)
    came, half_b, other_wq, far_other, near, middle = together(
        along_z(share[1], 4),
        to_other_y_lo(halves[1]),
        to_other_y_lo(own_wq),
        along_x(right_other, -1),
        to_other_core(near),
        to_other_core(middle),
    )
    share = jnp.stack([share[0], came], axis=0).reshape(N_Z, rows, PAIR_COLS)
    came, last, half_c, swapped_a, swapped_b = together(
        to_other_y_lo(share),
        to_other_core(far_other),
        to_other_y_lo(halves[2]),
        to_other_core(half_a),
        to_other_core(half_b),
    )
    share = jnp.concatenate([share, came], axis=0)
    pieces = [kv, other, left, right, far, left_other, right_other, far_other, near, middle, last]

    weights = pack(place_pair, stretch_wk, stretch_wv, own_wq, other_wq)
    share, weights = together(share, weights)
    gathered_weights = lax.all_gather(weights, "ctx", axis=0, tiled=False)
    last_weights = lax.all_gather(share, "ctx", axis=0, tiled=False)

    kept, given = attend(
        meta, global_q, pieces, 2 * N_CTX, ((0, 1), (0, 1)), 4, 2, "attend_all", share
    )
    received = to_other_y_lo(given)
    residual_kept, residual_given = split(place_pair, residual, received)
    parts = half_a, swapped_a, half_b, swapped_b, half_c, to_other_core(half_c)
    operands = core, kept, received, first_weights, parts
    (far,) = terms((4,), jnp.bfloat16, *operands)
    offsets = (3, 5, 2, 6, 1, 7, 0)
    near = dict(zip(offsets, terms(offsets, jnp.float32, *operands)))
    residual_came = to_other_y_lo(residual_given)
    up, down = ring_reduce(far, near, residual_came)
    mixed = mix(place_pair, residual_kept, residual_came, near[0], up, down)

    blocks = ring_gather(mixed)
    gain = norm_gain.reshape(2, N_Z, COLS).transpose(1, 0, 2).reshape(N_Z, PAIR_COLS)
    gain = jnp.stack([gain[(z + offset) % N_Z] for offset in RING_OFFSETS])
    chunk = jnp.where(lower, me, 2 * N_CTX - 1 - me)
    positions = (chunk * CHUNK + jnp.arange(CHUNK, dtype=jnp.int32)).astype(jnp.float32)
    half_dim = HEAD_DIM // 2
    inv_freq = rope_base ** (-(jnp.arange(half_dim).astype(jnp.float32) * 2.0 / HEAD_DIM))
    angles = positions[:, None] * inv_freq[None, :]
    cosine, sine = jnp.cos(angles), jnp.sin(angles)
    stretch_q, stretch_kv = project(
        z,
        blocks,
        gain,
        jnp.concatenate([cosine, cosine], axis=1),
        jnp.concatenate([-sine, sine], axis=1),
        gathered_weights,
    )
    pieces = gather_ctx(stretch_kv)
    slots = [jnp.where(lower, c, N_CTX - 1 - c) for c in owners()]
    limit = jnp.where(lower, me + 1, N_CTX - me)
    meta = jnp.stack(slots + [limit, 0]).astype(jnp.int32)
    (attended,) = attend(
        meta, stretch_q, pieces, N_CTX, ((0, 1, 2, 3),), 4, 2, "attend_window"
    )
    own, other = finish(place_pair, ring_gather(attended), mixed, last_weights)
    return in_order(lower, own, to_other_y_lo(other), 0)


def solution(mesh):
    in_specs = (
        P("ctx", "tp"),
        P("ctx", "tp"),
        P("ctx", None),
        P("ctx", None),
        P("tp", None),
        P(),
        P("ctx", "tp"),
        P("ctx", None),
        P("ctx", None),
        P("tp", None),
    )
    return jax.shard_map(
        per_device, mesh=mesh, in_specs=in_specs, out_specs=P("ctx", "tp"), check_vma=False
    )
```

```python
import functools

import jax
import jax.numpy as jnp
from jax import lax
from jax.experimental import pallas as pl
from jax.experimental.pallas import tpu as pltpu
from jax.sharding import PartitionSpec as P

HEAD_DIM = 128
GROUP = 4
CHUNK = 256
N_CTX = 16
N_Z = 8
COLS = 320
PAIR_COLS = 2 * COLS
rope_base = 500000.0
norm_eps = 1e-05
masked_score = -1e30
scale_log2 = 1.4426950408889634 * HEAD_DIM**-0.5
MIB = 1024 * 1024
SMEM = pl.BlockSpec(memory_space=pltpu.SMEM)
VMEM = pl.BlockSpec(memory_space=pltpu.VMEM)
HBM = pl.BlockSpec(memory_space=pltpu.HBM)


def permute(value, axis, target):
    return lax.ppermute(value, axis, [(place, target(place)) for place in range(16)])


def to_other_core(value):
    return permute(value, "ctx", lambda c: c ^ 1)


def to_other_y_hi(value):
    return permute(value, "ctx", lambda c: c ^ 8)


def along_x(value, step):
    return permute(value, "ctx", lambda c: (c & 9) | ((c + 2 * step) & 6))


def to_other_y_lo(value):
    return permute(value, "tp", lambda t: t ^ 8)


def along_z(value, step):
    return permute(value, "tp", lambda t: (t & 8) | ((t + step) & 7))


def together_kernel(*refs):
    pass


def together(*values):
    return pl.pallas_call(
        together_kernel,
        out_shape=[jax.ShapeDtypeStruct(value.shape, value.dtype) for value in values],
        in_specs=[HBM] * len(values),
        out_specs=[HBM] * len(values),
        input_output_aliases={i: i for i in range(len(values))},
        compiler_params=pltpu.CompilerParams(vmem_limit_bytes=MIB),
        name="together",
    )(*values)


def arrange_kernel(row_count, place_ref, source, *rest):
    outs, (rows, sem) = rest[:-2], rest[-2:]
    first = pl.multiple_of(place_ref[1], 16)
    copy = pltpu.make_async_copy(source.at[pl.ds(first, row_count)], rows, sem)
    copy.start()
    copy.wait()
    for z in range(N_Z):
        offset = (z - place_ref[0]) & 7
        for y_lo in (0, 1):
            at = (y_lo * N_Z + z) * COLS
            outs[0][offset, :, y_lo * COLS : (y_lo + 1) * COLS] = rows[:, at : at + COLS]
    for out in outs[1:]:
        height = out.shape[1]
        half = pl.ds(pl.multiple_of(place_ref[2], height), height)
        out[...] = outs[0][:, half, :]


def arrange(z, first, half, weights, row_count):
    shapes = [jax.ShapeDtypeStruct((N_Z, row_count, PAIR_COLS), jnp.bfloat16)]
    place = [z, first]
    if half is not None:
        shapes.append(jax.ShapeDtypeStruct((N_Z, row_count // 2, PAIR_COLS), jnp.bfloat16))
        place.append(half * (row_count // 2))
    return pl.pallas_call(
        functools.partial(arrange_kernel, row_count),
        out_shape=shapes,
        in_specs=[SMEM, HBM],
        out_specs=[VMEM] * len(shapes),
        scratch_shapes=[
            pltpu.VMEM((row_count, weights.shape[1]), jnp.bfloat16),
            pltpu.SemaphoreType.DMA,
        ],
        compiler_params=pltpu.CompilerParams(vmem_limit_bytes=60 * MIB),
        name="arrange",
    )(jnp.stack(place).astype(jnp.int32), weights)


def pack_kernel(place_ref, k_ref, v_ref, own_ref, other_ref, out_ref, sems):
    def columns(first, width):
        return pl.ds(pl.multiple_of(first, HEAD_DIM), width)

    wide = own_ref.shape[1]
    head = columns(place_ref[1] * HEAD_DIM, HEAD_DIM)
    moves = (
        (own_ref, columns(place_ref[0] * wide, wide)),
        (other_ref, columns((1 - place_ref[0]) * wide, wide)),
        (k_ref.at[:, head], pl.ds(2 * wide, HEAD_DIM)),
        (v_ref.at[:, head], pl.ds(2 * wide + HEAD_DIM, HEAD_DIM)),
    )
    copies = [
        pltpu.make_async_copy(source, out_ref.at[:, target], sems.at[i])
        for i, (source, target) in enumerate(moves)
    ]
    for copy in copies:
        copy.start()
    for copy in copies:
        copy.wait()


def pack(place, keys, values, own, other):
    rows, wide = own.shape
    return pl.pallas_call(
        pack_kernel,
        out_shape=jax.ShapeDtypeStruct((rows, 2 * (wide + HEAD_DIM)), jnp.bfloat16),
        in_specs=[SMEM] + [HBM] * 4,
        out_specs=HBM,
        scratch_shapes=[pltpu.SemaphoreType.DMA((4,))],
        compiler_params=pltpu.CompilerParams(vmem_limit_bytes=MIB),
        name="pack",
    )(place, keys, values, own, other)


def split_kernel(place_ref, value_ref, *rest):
    outs, sems = rest[-3:-1], rest[-1]
    copies = []
    for i, half in enumerate((place_ref[0], 1 - place_ref[0])):
        rows = pl.ds(pl.multiple_of(half * CHUNK, CHUNK), CHUNK)
        copies.append(pltpu.make_async_copy(value_ref.at[rows], outs[i], sems.at[i]))
        copies[-1].start()
    for copy in copies:
        copy.wait()


def split(place, value):
    half = jax.ShapeDtypeStruct((CHUNK, value.shape[1]), value.dtype)
    return pl.pallas_call(
        split_kernel,
        out_shape=(half, half),
        in_specs=[SMEM, HBM],
        out_specs=(VMEM, VMEM),
        scratch_shapes=[pltpu.SemaphoreType.DMA((2,))],
        compiler_params=pltpu.CompilerParams(vmem_limit_bytes=MIB),
        name="split",
    )(place, value)


def mix_kernel(place_ref, kept_ref, came_ref, own_ref, up_ref, down_ref, out_ref):
    total = sum(ref[...].astype(jnp.float32) for ref in (own_ref, up_ref, down_ref))

    def put(first, second):
        residual = (first[...].astype(jnp.float32), second[...].astype(jnp.float32))
        out_ref[:, :COLS] = (total[:, :COLS] + residual[0]).astype(jnp.bfloat16)
        out_ref[:, COLS:] = (total[:, COLS:] + residual[1]).astype(jnp.bfloat16)

    pl.when(place_ref[0] == 0)(lambda: put(kept_ref, came_ref))
    pl.when(place_ref[0] == 1)(lambda: put(came_ref, kept_ref))


def mix(place, kept, came, own, up, down):
    return pl.pallas_call(
        mix_kernel,
        out_shape=jax.ShapeDtypeStruct(up.shape, jnp.bfloat16),
        in_specs=[SMEM] + [VMEM] * 5,
        out_specs=VMEM,
        compiler_params=pltpu.CompilerParams(vmem_limit_bytes=8 * MIB),
        name="mix",
    )(place, kept, came, own, up, down)


def terms_kernel(offsets, core_ref, kept_ref, received_ref, *rest):
    weights, outs, (buffer, sems) = rest[:3], rest[3:-2], rest[-2:]
    half = CHUNK // 2
    copies = []
    for i, offset in enumerate(offsets):
        for j, (first, rows) in enumerate(((0, CHUNK), (CHUNK, half), (CHUNK + half, half))):
            target = buffer.at[i, pl.ds(first, rows)]
            copies.append(
                pltpu.make_async_copy(weights[j].at[offset], target, sems.at[3 * i + j])
            )
            copies[-1].start()
    received = received_ref[...]
    low, high = received[:, :half], received[:, half:]
    first = jnp.full(low.shape, core_ref[0], jnp.int32) == 0
    rows = jnp.concatenate(
        [kept_ref[...], jnp.where(first, low, high), jnp.where(first, high, low)], axis=1
    )
    for i in range(len(offsets)):
        for copy in copies[3 * i : 3 * i + 3]:
            copy.wait()
        total = jnp.dot(rows, buffer[i], preferred_element_type=jnp.float32)
        outs[i][...] = total.astype(outs[i].dtype)


def terms(offsets, core, kept, received, weights):
    count = len(offsets)
    return pl.pallas_call(
        functools.partial(terms_kernel, offsets),
        out_shape=[jax.ShapeDtypeStruct((CHUNK, PAIR_COLS), jnp.bfloat16)] * count,
        in_specs=[SMEM, VMEM, VMEM] + [HBM] * 3,
        out_specs=[VMEM] * count,
        scratch_shapes=[
            pltpu.VMEM((count, 2 * CHUNK, PAIR_COLS), jnp.bfloat16),
            pltpu.SemaphoreType.DMA((3 * count,)),
        ],
        compiler_params=pltpu.CompilerParams(vmem_limit_bytes=58 * MIB),
        name="terms",
    )(core.reshape(1), kept, received, *weights)


GATHER_OFFSETS = [
    (dy, dx, core)
    for core in (0, 1)
    for dy, dx in ((0, 0), (1, 0), (0, 3), (0, 1), (0, 2), (1, 3), (1, 1), (1, 2))
]


def gather_ctx(block):
    other = to_other_y_hi(block)
    left, right = along_x(block, 1), along_x(block, -1)
    far = along_x(left, 1)
    left_other, right_other = along_x(other, 1), along_x(other, -1)
    far_other = along_x(right_other, -1)
    mine = [block, other, left, right, far, left_other, right_other, far_other]
    return mine + [
        to_other_core(jnp.stack(mine[:4])),
        to_other_core(jnp.stack(mine[4:7])),
        to_other_core(far_other),
    ]


def owners():
    me = lax.axis_index("ctx")
    return [
        ((me & 8) ^ (8 * dy)) | ((me + 2 * dx) & 6) | ((me & 1) ^ dc)
        for dy, dx, dc in GATHER_OFFSETS
    ]


def take_kernel(place_ref, k_ref, v_ref, out_ref, sems):
    columns = pl.ds(pl.multiple_of(place_ref[0] * HEAD_DIM, HEAD_DIM), HEAD_DIM)
    copies = [
        pltpu.make_async_copy(src.at[:, columns], out_ref.at[:, pl.ds(i * HEAD_DIM, HEAD_DIM)], sems.at[i])
        for i, src in enumerate((k_ref, v_ref))
    ]
    for copy in copies:
        copy.start()
    for copy in copies:
        copy.wait()


def take_kv(place, keys, values):
    rows = keys.shape[0]
    return pl.pallas_call(
        take_kernel,
        out_shape=jax.ShapeDtypeStruct((rows, 2 * HEAD_DIM), jnp.bfloat16),
        in_specs=[SMEM, HBM, HBM],
        out_specs=VMEM,
        scratch_shapes=[pltpu.SemaphoreType.DMA((2,))],
        compiler_params=pltpu.CompilerParams(vmem_limit_bytes=60 * MIB),
        name="take_kv",
    )(place.reshape(1), keys, values)


def attend_kernel(tiles, tile_chunks, chains, earlier, meta_ref, q_ref, *rest):
    pieces, outs, (kv, sems) = rest[: -2 - len(tiles) - earlier], rest[-2 - len(tiles) : -2], rest[-2:]
    blocks = []
    for piece in pieces:
        blocks += [piece] if len(piece.shape) == 2 else [piece.at[b] for b in range(piece.shape[0])]
    copies = []
    for block in blocks:
        for part in range(block.shape[0] // CHUNK):
            source = block.at[pl.ds(part * CHUNK, CHUNK)]
            copies.append(
                pltpu.make_async_copy(source, kv.at[meta_ref[len(copies)]], sems.at[len(copies)])
            )
            copies[-1].start()
    for copy in copies:
        copy.wait()
    span = tile_chunks * CHUNK
    for tile, (heads, out_ref) in enumerate(zip(tiles, outs)):
        limit = meta_ref[len(copies) + 2 * tile]
        first = pl.multiple_of(meta_ref[len(copies) + 2 * tile + 1], CHUNK)
        rows = q_ref.at[pl.ds(first, CHUNK)]
        each = len(heads) // chains
        queries = [
            jnp.concatenate(
                [rows[:, h * HEAD_DIM : (h + 1) * HEAD_DIM] for h in heads[g * each : (g + 1) * each]],
                axis=0,
            )
            for g in range(chains)
        ]
        height = each * CHUNK

        def step(i, state, masked):
            here = pl.ds(i * tile_chunks, tile_chunks)
            keys = kv[here, :, :HEAD_DIM].reshape(span, HEAD_DIM)
            values = kv[here, :, HEAD_DIM:].reshape(span, HEAD_DIM)
            if masked:
                column = lax.broadcasted_iota(jnp.int32, (height, span), 1) + i * span
                row = lax.broadcasted_iota(jnp.int32, (height, span), 0) % CHUNK
                visible = column <= row + (limit - 1) * CHUNK
            scores = [
                lax.dot_general(
                    query, keys, (((1,), (1,)), ((), ())), preferred_element_type=jnp.float32
                )
                for query in queries
            ]
            after = []
            for score, (highest, total, weighted) in zip(scores, state):
                if masked:
                    score = jnp.where(visible, score, masked_score)
                new_high = jnp.maximum(highest, jnp.max(score, axis=1, keepdims=True))
                fade = jnp.exp2((highest - new_high) * scale_log2)
                terms = jnp.exp2((score - new_high) * scale_log2)
                total = total * fade + jnp.sum(terms, axis=1, keepdims=True)
                weighted = weighted * fade + jnp.dot(
                    terms.astype(jnp.bfloat16), values, preferred_element_type=jnp.float32
                )
                after.append((new_high, total, weighted))
            return tuple(after)

        state = tuple(
            (
                jnp.full((height, 1), masked_score, jnp.float32),
                jnp.zeros((height, 1), jnp.float32),
                jnp.zeros((height, HEAD_DIM), jnp.float32),
            )
            for _ in range(chains)
        )
        whole = lax.div(limit - 1, jnp.int32(tile_chunks))
        state = lax.fori_loop(0, whole, functools.partial(step, masked=False), state)
        state = step(whole, state, True)
        for g, (_, total, weighted) in enumerate(state):
            result = (weighted / total).astype(jnp.bfloat16)
            for j in range(each):
                h = heads[g * each + j]
                out_ref[:, h * HEAD_DIM : (h + 1) * HEAD_DIM] = result[
                    j * CHUNK : (j + 1) * CHUNK
                ]


def attend(meta, queries, pieces, chunks, tiles, tile_chunks, chains, name, *earlier):
    return pl.pallas_call(
        functools.partial(attend_kernel, tiles, tile_chunks, chains, len(earlier)),
        out_shape=[jax.ShapeDtypeStruct((CHUNK, queries.shape[1]), jnp.bfloat16)] * len(tiles),
        in_specs=[SMEM, VMEM] + [HBM] * (len(pieces) + len(earlier)),
        out_specs=[VMEM] * len(tiles),
        scratch_shapes=[
            pltpu.VMEM((chunks, CHUNK, 2 * HEAD_DIM), jnp.bfloat16),
            pltpu.SemaphoreType.DMA((chunks,)),
        ],
        compiler_params=pltpu.CompilerParams(vmem_limit_bytes=58 * MIB),
        cost_estimate=pl.CostEstimate(
            flops=2_200_000_000, bytes_accessed=5_000_000, transcendentals=10_000_000
        ),
        name=name,
    )(meta, queries, *pieces, *earlier)


def ring_gather(block):
    half = block.shape[0] // 2
    below, above = [block], [block]
    for _ in range(3):
        below.append(along_z(below[-1], 1))
        above.append(along_z(above[-1], -1))
    far = [along_z(below[-1][:half], 1), along_z(above[-1][half:], -1)]
    return above + below[:0:-1] + far


RING_OFFSETS = (0, 1, 2, 3, 5, 6, 7, 4)


def hop_kernel(up_ref, down_ref, up_term_ref, down_term_ref, up_out_ref, down_out_ref):
    came = up_ref.shape[0]
    rest = CHUNK - came
    up, down = up_term_ref[:came].astype(jnp.float32), down_term_ref[rest:].astype(jnp.float32)
    up_out_ref[:came] = (up + up_ref[...].astype(jnp.float32)).astype(jnp.bfloat16)
    down_out_ref[rest:] = (down + down_ref[...].astype(jnp.float32)).astype(jnp.bfloat16)
    if rest:
        up_out_ref[came:] = up_term_ref[came:]
        down_out_ref[:rest] = down_term_ref[:rest]


def ring_reduce(far, near):
    half = far.shape[0] // 2
    up, down = along_z(far[:half], 1), along_z(far[half:], -1)
    for hop in (3, 2, 1):
        up, down = pl.pallas_call(
            hop_kernel,
            out_shape=[jax.ShapeDtypeStruct(far.shape, far.dtype)] * 2,
            in_specs=[VMEM] * 4,
            out_specs=[VMEM] * 2,
            compiler_params=pltpu.CompilerParams(vmem_limit_bytes=8 * MIB),
            name="hop",
        )(up, down, near[hop], near[8 - hop])
        up, down = along_z(up, 1), along_z(down, -1)
    return up, down


def load_features(refs):
    return [ref[...] for ref in refs[:7]] + [jnp.concatenate([refs[7][...], refs[8][...]], axis=0)]


def rope(value, cosine, sine):
    return value * cosine + pltpu.roll(value, HEAD_DIM // 2, axis=1) * sine


def project_kernel(z_ref, *rest):
    blocks, (gain_ref, cos_ref, sin_ref, w_ref, q_ref, kv_ref, w_vmem, sems) = rest[:9], rest[9:]
    copies = []
    for i, offset in enumerate(RING_OFFSETS):
        source = (z_ref[0] + offset) & 7
        for y_lo in (0, 1):
            rows = pl.ds(y_lo * COLS, COLS)
            copies.append(
                pltpu.make_async_copy(w_ref.at[y_lo * N_Z + source], w_vmem.at[i, rows], sems.at[len(copies)])
            )
            copies[-1].start()
    features = load_features(blocks)
    squares = jnp.zeros((CHUNK, 1), jnp.float32)
    for value in features:
        wide = value.astype(jnp.float32)
        squares = squares + jnp.sum(wide * wide, axis=1, keepdims=True)
    inverse = lax.rsqrt(squares / (16 * COLS) + norm_eps)
    total = jnp.zeros((CHUNK, w_vmem.shape[2]), jnp.float32)
    for i, value in enumerate(features):
        normed = (value.astype(jnp.float32) * inverse * gain_ref[i : i + 1]).astype(jnp.bfloat16)
        copies[2 * i].wait()
        copies[2 * i + 1].wait()
        total = total + jnp.dot(normed, w_vmem[i], preferred_element_type=jnp.float32)
    cosine, sine = cos_ref[...], sin_ref[...]
    for h in range(GROUP):
        at = slice(h * HEAD_DIM, (h + 1) * HEAD_DIM)
        q_ref[:, at] = rope(total[:, at], cosine, sine).astype(jnp.bfloat16)
    at = GROUP * HEAD_DIM
    kv_ref[:, :HEAD_DIM] = rope(total[:, at : at + HEAD_DIM], cosine, sine).astype(jnp.bfloat16)
    kv_ref[:, HEAD_DIM:] = total[:, at + HEAD_DIM :].astype(jnp.bfloat16)


def project(z, blocks, gain, cosine, sine, weights):
    width = weights.shape[2]
    return pl.pallas_call(
        project_kernel,
        out_shape=(
            jax.ShapeDtypeStruct((CHUNK, GROUP * HEAD_DIM), jnp.bfloat16),
            jax.ShapeDtypeStruct((CHUNK, 2 * HEAD_DIM), jnp.bfloat16),
        ),
        in_specs=[SMEM] + [VMEM] * 12 + [HBM],
        out_specs=(VMEM, VMEM),
        scratch_shapes=[
            pltpu.VMEM((N_Z, PAIR_COLS, width), jnp.bfloat16),
            pltpu.SemaphoreType.DMA((2 * N_Z,)),
        ],
        compiler_params=pltpu.CompilerParams(vmem_limit_bytes=54 * MIB),
        name="norm_project",
    )(z.reshape(1), *blocks, gain, cosine, sine, weights)


def finish_kernel(place_ref, *rest):
    blocks, (mixed_ref, w_ref, own_ref, other_ref, w_vmem, sems) = rest[:9], rest[9:]
    copies = []
    for i, offset in enumerate(RING_OFFSETS):
        source = (place_ref[1] + offset) & 7
        for j in (0, 1):
            at = (place_ref[1] - 2 * source - j) & 7
            at = at + N_Z * ((source >> 2) ^ place_ref[0])
            copies.append(pltpu.make_async_copy(w_ref.at[:, at], w_vmem.at[i, j], sems.at[2 * i + j]))
            copies[-1].start()
    features = load_features(blocks)
    total = mixed_ref[...].astype(jnp.float32)
    for i, value in enumerate(features):
        for j in (0, 1):
            copies[2 * i + j].wait()
            total = total + jnp.dot(
                value[:, j * 2 * HEAD_DIM : (j + 1) * 2 * HEAD_DIM],
                w_vmem[i, j].reshape(2 * HEAD_DIM, PAIR_COLS),
                preferred_element_type=jnp.float32,
            )
    first, second = total[:, :COLS].astype(jnp.bfloat16), total[:, COLS:].astype(jnp.bfloat16)

    @pl.when(place_ref[0] == 0)
    def _():
        own_ref[...] = first
        other_ref[...] = second

    @pl.when(place_ref[0] == 1)
    def _():
        own_ref[...] = second
        other_ref[...] = first


def finish(place, blocks, mixed, weights):
    part = jax.ShapeDtypeStruct((CHUNK, COLS), jnp.bfloat16)
    return pl.pallas_call(
        finish_kernel,
        out_shape=(part, part),
        in_specs=[SMEM] + [VMEM] * 10 + [HBM],
        out_specs=(VMEM, VMEM),
        scratch_shapes=[
            pltpu.VMEM((N_Z, 2, N_CTX, weights.shape[2], PAIR_COLS), jnp.bfloat16),
            pltpu.SemaphoreType.DMA((2 * N_Z,)),
        ],
        compiler_params=pltpu.CompilerParams(vmem_limit_bytes=57 * MIB),
        name="project_out",
    )(place, *blocks, mixed, weights)


def turned(blocks, first):
    return lax.dynamic_slice_in_dim(jnp.concatenate([blocks, blocks], axis=0), first, N_Z, 0)


def in_order(first, own, other, axis):
    return jnp.where(
        first, jnp.concatenate([own, other], axis=axis), jnp.concatenate([other, own], axis=axis)
    )


def per_device(
    residual,
    global_q,
    global_k,
    global_v,
    global_wo,
    norm_gain,
    stretch_wq,
    stretch_wk,
    stretch_wv,
    stretch_wo,
):
    me = lax.axis_index("ctx")
    place = lax.axis_index("tp")
    y_lo, z = place // N_Z, place % N_Z
    lower = y_lo == 0
    core = me & 1

    place_pair = jnp.stack([y_lo, z]).astype(jnp.int32)

    all_kv = lax.all_gather(take_kv(place // 2, global_k, global_v), "ctx", axis=0, tiled=False)
    slots = [slot for c in range(N_CTX) for slot in (c, 2 * N_CTX - 1 - c)]
    limits = jnp.where(lower, me + 1, 2 * N_CTX - me), jnp.where(lower, 2 * N_CTX - me, me + 1)
    ends = limits[0], y_lo * CHUNK, limits[1], (1 - y_lo) * CHUNK
    meta = jnp.stack([jnp.int32(slot) for slot in slots] + list(ends)).astype(jnp.int32)

    first_weights, half_mine = arrange(
        z, jnp.int32(0), core, global_wo, global_wo.shape[0]
    )
    rows = stretch_wo.shape[0] // N_CTX
    (share,) = arrange(z, me * rows, None, stretch_wo, rows)
    share = share.reshape(2, 2, 2, rows, PAIR_COLS)
    residual_kept, residual_given = split(place_pair, residual)
    half_mine, own_wq, came = together(
        to_other_y_lo(half_mine),
        permute(stretch_wq, "tp", lambda t: 8 * (t % 2) + t // 2),
        along_z(share[:, :, 1], 1),
    )
    share = jnp.stack([share[:, :, 0], came], axis=2)
    half_other, other_wq, came, residual_came = together(
        to_other_core(half_mine),
        to_other_y_lo(own_wq),
        along_z(share[:, 1], 2),
        to_other_y_lo(residual_given),
    )
    weights = pack(place_pair, stretch_wk, stretch_wv, own_wq, other_wq)
    share = jnp.stack([share[:, 0], came], axis=1)
    share = jnp.stack([share[0], along_z(share[1], 4)], axis=0).reshape(N_Z, rows, PAIR_COLS)
    share = jnp.concatenate([share, to_other_y_lo(share)], axis=0)

    share, weights = together(share, weights)
    gathered_weights = lax.all_gather(weights, "ctx", axis=0, tiled=False)
    last_weights = lax.all_gather(share, "ctx", axis=0, tiled=False)

    kept, given = attend(
        meta,
        global_q,
        [all_kv],
        2 * N_CTX,
        ((0, 1), (0, 1)),
        4,
        2,
        "attend_all",
        share,
        half_other,
        residual_came,
    )
    operands = core, kept, to_other_y_lo(given), (first_weights, half_mine, half_other)
    (far,) = terms((4,), *operands)
    offsets = (3, 5, 2, 6, 1, 7, 0)
    near = dict(zip(offsets, terms(offsets, *operands)))
    up, down = ring_reduce(far, near)
    mixed = mix(place_pair, residual_kept, residual_came, near[0], up, down)

    blocks = ring_gather(mixed)
    gain = norm_gain.reshape(2, N_Z, COLS).transpose(1, 0, 2).reshape(N_Z, PAIR_COLS)
    gain = jnp.stack([gain[(z + offset) % N_Z] for offset in RING_OFFSETS])
    chunk = jnp.where(lower, me, 2 * N_CTX - 1 - me)
    positions = (chunk * CHUNK + jnp.arange(CHUNK, dtype=jnp.int32)).astype(jnp.float32)
    half_dim = HEAD_DIM // 2
    inv_freq = rope_base ** (-(jnp.arange(half_dim).astype(jnp.float32) * 2.0 / HEAD_DIM))
    angles = positions[:, None] * inv_freq[None, :]
    cosine, sine = jnp.cos(angles), jnp.sin(angles)
    stretch_q, stretch_kv = project(
        z,
        blocks,
        gain,
        jnp.concatenate([cosine, cosine], axis=1),
        jnp.concatenate([-sine, sine], axis=1),
        gathered_weights,
    )
    pieces = gather_ctx(stretch_kv)
    slots = [jnp.where(lower, c, N_CTX - 1 - c) for c in owners()]
    limit = jnp.where(lower, me + 1, N_CTX - me)
    meta = jnp.stack(slots + [limit, 0]).astype(jnp.int32)
    (attended,) = attend(
        meta, stretch_q, pieces, N_CTX, ((0, 1, 2, 3),), 4, 2, "attend_window"
    )
    own, other = finish(place_pair, ring_gather(attended), mixed, last_weights)
    return in_order(lower, own, to_other_y_lo(other), 0)


def solution(mesh):
    in_specs = (
        P("ctx", "tp"),
        P("ctx", "tp"),
        P("ctx", None),
        P("ctx", None),
        P("tp", None),
        P(),
        P("ctx", "tp"),
        P("ctx", None),
        P("ctx", None),
        P("tp", None),
    )
    return jax.shard_map(
        per_device, mesh=mesh, in_specs=in_specs, out_specs=P("ctx", "tp"), check_vma=False
    )
```

```python
import functools

import jax
import jax.numpy as jnp
from jax import lax
from jax.experimental import pallas as pl
from jax.experimental.pallas import tpu as pltpu
from jax.sharding import PartitionSpec as P

HEAD_DIM = 128
GROUP = 4
CHUNK = 256
N_CTX = 16
N_Z = 8
COLS = 320
PAIR_COLS = 2 * COLS
rope_base = 500000.0
norm_eps = 1e-05
masked_score = -1e30
scale_log2 = 1.4426950408889634 * HEAD_DIM**-0.5
MIB = 1024 * 1024
SMEM = pl.BlockSpec(memory_space=pltpu.SMEM)
VMEM = pl.BlockSpec(memory_space=pltpu.VMEM)
HBM = pl.BlockSpec(memory_space=pltpu.HBM)


def permute(value, axis, target):
    return lax.ppermute(value, axis, [(place, target(place)) for place in range(16)])


def to_other_core(value):
    return permute(value, "ctx", lambda c: c ^ 1)


def to_other_y_hi(value):
    return permute(value, "ctx", lambda c: c ^ 8)


def along_x(value, step):
    return permute(value, "ctx", lambda c: (c & 9) | ((c + 2 * step) & 6))


def to_other_y_lo(value):
    return permute(value, "tp", lambda t: t ^ 8)


def along_z(value, step):
    return permute(value, "tp", lambda t: (t & 8) | ((t + step) & 7))


def together_kernel(*refs):
    pass


def together(*values):
    return pl.pallas_call(
        together_kernel,
        out_shape=[jax.ShapeDtypeStruct(value.shape, value.dtype) for value in values],
        in_specs=[HBM] * len(values),
        out_specs=[HBM] * len(values),
        input_output_aliases={i: i for i in range(len(values))},
        compiler_params=pltpu.CompilerParams(vmem_limit_bytes=MIB),
        name="together",
    )(*values)


def arrange_kernel(row_count, place_ref, source, *rest):
    outs, (rows, sem) = rest[:-2], rest[-2:]
    first = pl.multiple_of(place_ref[1], 16)
    copy = pltpu.make_async_copy(source.at[pl.ds(first, row_count)], rows, sem)
    copy.start()
    copy.wait()
    for z in range(N_Z):
        offset = (z - place_ref[0]) & 7
        for y_lo in (0, 1):
            at = (y_lo * N_Z + z) * COLS
            outs[0][offset, :, y_lo * COLS : (y_lo + 1) * COLS] = rows[:, at : at + COLS]
    for out in outs[1:]:
        height = out.shape[1]
        half = pl.ds(pl.multiple_of(place_ref[2], height), height)
        out[...] = outs[0][:, half, :]


def arrange(z, first, half, weights, row_count):
    shapes = [jax.ShapeDtypeStruct((N_Z, row_count, PAIR_COLS), jnp.bfloat16)]
    place = [z, first]
    if half is not None:
        shapes.append(jax.ShapeDtypeStruct((N_Z, row_count // 2, PAIR_COLS), jnp.bfloat16))
        place.append(half * (row_count // 2))
    return pl.pallas_call(
        functools.partial(arrange_kernel, row_count),
        out_shape=shapes,
        in_specs=[SMEM, HBM],
        out_specs=[VMEM] * len(shapes),
        scratch_shapes=[
            pltpu.VMEM((row_count, weights.shape[1]), jnp.bfloat16),
            pltpu.SemaphoreType.DMA,
        ],
        compiler_params=pltpu.CompilerParams(vmem_limit_bytes=20 * MIB),
        name="arrange",
    )(jnp.stack(place).astype(jnp.int32), weights)


def pack_kernel(place_ref, k_ref, v_ref, own_ref, other_ref, out_ref, sems):
    def columns(first, width):
        return pl.ds(pl.multiple_of(first, HEAD_DIM), width)

    wide = own_ref.shape[1]
    head = columns(place_ref[1] * HEAD_DIM, HEAD_DIM)
    moves = (
        (own_ref, columns(place_ref[0] * wide, wide)),
        (other_ref, columns((1 - place_ref[0]) * wide, wide)),
        (k_ref.at[:, head], pl.ds(2 * wide, HEAD_DIM)),
        (v_ref.at[:, head], pl.ds(2 * wide + HEAD_DIM, HEAD_DIM)),
    )
    copies = [
        pltpu.make_async_copy(source, out_ref.at[:, target], sems.at[i])
        for i, (source, target) in enumerate(moves)
    ]
    for copy in copies:
        copy.start()
    for copy in copies:
        copy.wait()


def pack(place, keys, values, own, other):
    rows, wide = own.shape
    return pl.pallas_call(
        pack_kernel,
        out_shape=jax.ShapeDtypeStruct((rows, 2 * (wide + HEAD_DIM)), jnp.bfloat16),
        in_specs=[SMEM] + [HBM] * 4,
        out_specs=HBM,
        scratch_shapes=[pltpu.SemaphoreType.DMA((4,))],
        compiler_params=pltpu.CompilerParams(vmem_limit_bytes=MIB),
        name="pack",
    )(place, keys, values, own, other)


def split_kernel(place_ref, value_ref, *rest):
    outs, sems = rest[-3:-1], rest[-1]
    copies = []
    for i, half in enumerate((place_ref[0], 1 - place_ref[0])):
        rows = pl.ds(pl.multiple_of(half * CHUNK, CHUNK), CHUNK)
        copies.append(pltpu.make_async_copy(value_ref.at[rows], outs[i], sems.at[i]))
        copies[-1].start()
    for copy in copies:
        copy.wait()


def split(place, value):
    half = jax.ShapeDtypeStruct((CHUNK, value.shape[1]), value.dtype)
    return pl.pallas_call(
        split_kernel,
        out_shape=(half, half),
        in_specs=[SMEM, HBM],
        out_specs=(VMEM, VMEM),
        scratch_shapes=[pltpu.SemaphoreType.DMA((2,))],
        compiler_params=pltpu.CompilerParams(vmem_limit_bytes=MIB),
        name="split",
    )(place, value)


def own_terms(offsets, core_ref, kept_ref, received_ref, weights, others, refs):
    buffer, landing, sems = refs
    half = CHUNK // 2
    copies = []
    for i, offset in enumerate(offsets):
        for j, (first, rows) in enumerate(((0, CHUNK), (CHUNK, half), (CHUNK + half, half))):
            target = buffer.at[i, pl.ds(first, rows)]
            copies.append(
                pltpu.make_async_copy(weights[j].at[offset], target, sems.at[3 * i + j])
            )
            copies[-1].start()
    landed = []
    for i, other in enumerate(others):
        target = landing.at[i, pl.ds(0, other.shape[0]), pl.ds(0, other.shape[1])]
        copies.append(pltpu.make_async_copy(other, target, sems.at[len(copies)]))
        copies[-1].start()
    received = received_ref[...]
    low, high = received[:, :half], received[:, half:]
    first = jnp.full(low.shape, core_ref[0], jnp.int32) == 0
    rows = jnp.concatenate(
        [kept_ref[...], jnp.where(first, low, high), jnp.where(first, high, low)], axis=1
    )
    for copy in copies:
        copy.wait()
    for i, other in enumerate(others):
        landed.append(landing[i, : other.shape[0]].astype(jnp.float32))
    parts = [
        jnp.dot(rows, buffer[i], preferred_element_type=jnp.float32) for i in range(len(offsets))
    ]
    return parts, landed


def far_kernel(core_ref, kept_ref, received_ref, *refs):
    weights, (up_ref, down_ref, *scratch) = refs[:3], refs[3:]
    (part,), _ = own_terms((4,), core_ref, kept_ref, received_ref, weights, (), scratch)
    half = CHUNK // 2
    up_ref[...] = part[:half].astype(jnp.bfloat16)
    down_ref[...] = part[half:].astype(jnp.bfloat16)


def hop_kernel(hop, core_ref, kept_ref, received_ref, *refs):
    weights, (up_ref, down_ref, up_out_ref, down_out_ref, *scratch) = refs[:3], refs[3:]
    parts, (up, down) = own_terms(
        (hop, N_Z - hop), core_ref, kept_ref, received_ref, weights, (up_ref, down_ref), scratch
    )
    came = up.shape[0]
    rest = CHUNK - came
    up_out_ref[:came] = (parts[0][:came] + up).astype(jnp.bfloat16)
    down_out_ref[rest:] = (parts[1][rest:] + down).astype(jnp.bfloat16)
    if rest:
        up_out_ref[came:] = parts[0][came:].astype(jnp.bfloat16)
        down_out_ref[:rest] = parts[1][:rest].astype(jnp.bfloat16)


def mix_kernel(core_ref, kept_ref, received_ref, *refs):
    weights, (up_ref, down_ref, place_ref, *residual, out_ref), scratch = (
        refs[:3],
        refs[3:-3],
        refs[-3:],
    )
    (part,), (up, down) = own_terms(
        (0,), core_ref, kept_ref, received_ref, weights, (up_ref, down_ref), scratch
    )
    total = part + up + down

    def put(first, second):
        out_ref[:, :COLS] = (total[:, :COLS] + first[...].astype(jnp.float32)).astype(jnp.bfloat16)
        out_ref[:, COLS:] = (total[:, COLS:] + second[...].astype(jnp.float32)).astype(jnp.bfloat16)

    pl.when(place_ref[0] == 0)(lambda: put(*residual))
    pl.when(place_ref[0] == 1)(lambda: put(*residual[::-1]))


def ring_step(kernel, name, shapes, count, operands, moving=(), extra=(), extra_specs=()):
    core, kept, received, weights = operands
    return pl.pallas_call(
        kernel,
        out_shape=[jax.ShapeDtypeStruct(shape, jnp.bfloat16) for shape in shapes],
        in_specs=[SMEM, VMEM, VMEM] + [HBM] * (3 + len(moving)) + list(extra_specs),
        out_specs=[VMEM] * len(shapes),
        scratch_shapes=[
            pltpu.VMEM((count, 2 * CHUNK, PAIR_COLS), jnp.bfloat16),
            pltpu.VMEM((2, CHUNK, PAIR_COLS), jnp.bfloat16),
            pltpu.SemaphoreType.DMA((3 * count + 2,)),
        ],
        compiler_params=pltpu.CompilerParams(vmem_limit_bytes=20 * MIB),
        name=name,
    )(core.reshape(1), kept, received, *weights, *moving, *extra)


def ring_reduce(operands, place, residual):
    whole, half = (CHUNK, PAIR_COLS), (CHUNK // 2, PAIR_COLS)
    moving = ring_step(far_kernel, "far", (half, half), 1, operands)
    for hop in (3, 2, 1):
        moving = along_z(moving[0], 1), along_z(moving[1], -1)
        kernel = functools.partial(hop_kernel, hop)
        moving = ring_step(kernel, "hop", (whole, whole), 2, operands, moving)
    moving = along_z(moving[0], 1), along_z(moving[1], -1)
    extra, specs = (place, *residual), (SMEM, VMEM, VMEM)
    return ring_step(mix_kernel, "mix", (whole,), 1, operands, moving, extra, specs)[0]


GATHER_OFFSETS = [
    (dy, dx, core)
    for core in (0, 1)
    for dy, dx in ((0, 0), (1, 0), (0, 3), (0, 1), (0, 2), (1, 3), (1, 1), (1, 2))
]


def gather_ctx(block):
    other = to_other_y_hi(block)
    left, right = along_x(block, 1), along_x(block, -1)
    far = along_x(left, 1)
    left_other, right_other = along_x(other, 1), along_x(other, -1)
    far_other = along_x(right_other, -1)
    mine = [block, other, left, right, far, left_other, right_other, far_other]
    return mine + [
        to_other_core(jnp.stack(mine[:4])),
        to_other_core(jnp.stack(mine[4:7])),
        to_other_core(far_other),
    ]


def owners():
    me = lax.axis_index("ctx")
    return [
        ((me & 8) ^ (8 * dy)) | ((me + 2 * dx) & 6) | ((me & 1) ^ dc)
        for dy, dx, dc in GATHER_OFFSETS
    ]


def take_kernel(place_ref, k_ref, v_ref, out_ref, sems):
    columns = pl.ds(pl.multiple_of(place_ref[0] * HEAD_DIM, HEAD_DIM), HEAD_DIM)
    copies = [
        pltpu.make_async_copy(src.at[:, columns], out_ref.at[:, pl.ds(i * HEAD_DIM, HEAD_DIM)], sems.at[i])
        for i, src in enumerate((k_ref, v_ref))
    ]
    for copy in copies:
        copy.start()
    for copy in copies:
        copy.wait()


def take_kv(place, keys, values):
    rows = keys.shape[0]
    return pl.pallas_call(
        take_kernel,
        out_shape=jax.ShapeDtypeStruct((rows, 2 * HEAD_DIM), jnp.bfloat16),
        in_specs=[SMEM, HBM, HBM],
        out_specs=VMEM,
        scratch_shapes=[pltpu.SemaphoreType.DMA((2,))],
        compiler_params=pltpu.CompilerParams(vmem_limit_bytes=60 * MIB),
        name="take_kv",
    )(place.reshape(1), keys, values)


def attend_kernel(tiles, tile_chunks, chains, earlier, meta_ref, q_ref, *rest):
    pieces, outs, (kv, sems) = rest[: -2 - len(tiles) - earlier], rest[-2 - len(tiles) : -2], rest[-2:]
    blocks = []
    for piece in pieces:
        blocks += [piece] if len(piece.shape) == 2 else [piece.at[b] for b in range(piece.shape[0])]
    copies = []
    for block in blocks:
        for part in range(block.shape[0] // CHUNK):
            source = block.at[pl.ds(part * CHUNK, CHUNK)]
            copies.append(
                pltpu.make_async_copy(source, kv.at[meta_ref[len(copies)]], sems.at[len(copies)])
            )
            copies[-1].start()
    for copy in copies:
        copy.wait()
    span = tile_chunks * CHUNK
    for tile, (heads, out_ref) in enumerate(zip(tiles, outs)):
        limit = meta_ref[len(copies) + 2 * tile]
        first = pl.multiple_of(meta_ref[len(copies) + 2 * tile + 1], CHUNK)
        rows = q_ref.at[pl.ds(first, CHUNK)]
        each = len(heads) // chains
        queries = [
            jnp.concatenate(
                [rows[:, h * HEAD_DIM : (h + 1) * HEAD_DIM] for h in heads[g * each : (g + 1) * each]],
                axis=0,
            )
            for g in range(chains)
        ]
        height = each * CHUNK

        def step(i, state, masked):
            here = pl.ds(i * tile_chunks, tile_chunks)
            keys = kv[here, :, :HEAD_DIM].reshape(span, HEAD_DIM)
            values = kv[here, :, HEAD_DIM:].reshape(span, HEAD_DIM)
            values = jnp.concatenate([values, jnp.ones(values.shape, values.dtype)], axis=1)
            if masked:
                column = lax.broadcasted_iota(jnp.int32, (height, span), 1) + i * span
                row = lax.broadcasted_iota(jnp.int32, (height, span), 0) % CHUNK
                visible = column <= row + (limit - 1) * CHUNK
            scores = [
                lax.dot_general(
                    query, keys, (((1,), (1,)), ((), ())), preferred_element_type=jnp.float32
                )
                for query in queries
            ]
            after = []
            for score, (highest, weighted) in zip(scores, state):
                if masked:
                    score = jnp.where(visible, score, masked_score)
                new_high = jnp.maximum(highest, jnp.max(score, axis=1, keepdims=True))
                fade = jnp.exp2((highest - new_high) * scale_log2)
                scores_here = score * scale_log2 - new_high * scale_log2
                weights = jnp.exp2(scores_here).astype(jnp.bfloat16)
                weighted = weighted * fade + jnp.dot(
                    weights, values, preferred_element_type=jnp.float32
                )
                after.append((new_high, weighted))
            return tuple(after)

        state = tuple(
            (
                jnp.full((height, 1), masked_score, jnp.float32),
                jnp.zeros((height, 2 * HEAD_DIM), jnp.float32),
            )
            for _ in range(chains)
        )
        whole = lax.div(limit - 1, jnp.int32(tile_chunks))
        state = lax.fori_loop(0, whole, functools.partial(step, masked=False), state)
        state = step(whole, state, True)
        for g, (_, weighted) in enumerate(state):
            result = (weighted[:, :HEAD_DIM] / weighted[:, HEAD_DIM:]).astype(jnp.bfloat16)
            for j in range(each):
                h = heads[g * each + j]
                out_ref[:, h * HEAD_DIM : (h + 1) * HEAD_DIM] = result[
                    j * CHUNK : (j + 1) * CHUNK
                ]


def attend(meta, queries, pieces, chunks, tiles, tile_chunks, chains, name, *earlier):
    return pl.pallas_call(
        functools.partial(attend_kernel, tiles, tile_chunks, chains, len(earlier)),
        out_shape=[jax.ShapeDtypeStruct((CHUNK, queries.shape[1]), jnp.bfloat16)] * len(tiles),
        in_specs=[SMEM, VMEM] + [HBM] * (len(pieces) + len(earlier)),
        out_specs=[VMEM] * len(tiles),
        scratch_shapes=[
            pltpu.VMEM((chunks, CHUNK, 2 * HEAD_DIM), jnp.bfloat16),
            pltpu.SemaphoreType.DMA((chunks,)),
        ],
        compiler_params=pltpu.CompilerParams(vmem_limit_bytes=32 * MIB),
        cost_estimate=pl.CostEstimate(
            flops=2_200_000_000, bytes_accessed=5_000_000, transcendentals=10_000_000
        ),
        name=name,
    )(meta, queries, *pieces, *earlier)


def ring_gather(block, work):
    half = block.shape[0] // 2
    below, above = along_z(block, 1), along_z(block, -1)
    offsets, blocks, state = (0, 1, 7), (block, above, below), ()
    for hop in (2, 3, 4):
        if hop == 4:
            below, above = below[:half], above[half:]
        below, above = along_z(below, 1), along_z(above, -1)
        below, above, *state = together(below, above, *work(offsets, blocks, state))
        offsets, blocks = (hop, 8 - hop), (above, below)
    return (4,), (below, above), state


def rope(value, cosine, sine):
    return value * cosine + pltpu.roll(value, HEAD_DIM // 2, axis=1) * sine


def take_blocks(offsets, refs):
    if offsets == (4,):
        return [jnp.concatenate([refs[0][...], refs[1][...]], axis=0)], refs[2:]
    return [ref[...] for ref in refs[: len(offsets)]], refs[len(offsets) :]


def project_kernel(offsets, first, z_ref, *refs):
    last = offsets == (4,)
    blocks, (gain_ref, w_ref, *refs) = take_blocks(offsets, refs)
    w_vmem, sems = refs[-2:]
    copies = []
    for i, offset in enumerate(offsets):
        source = (z_ref[0] + offset) & 7
        for y_lo in (0, 1):
            rows = pl.ds(y_lo * COLS, COLS)
            copies.append(
                pltpu.make_async_copy(
                    w_ref.at[y_lo * N_Z + source], w_vmem.at[i, rows], sems.at[len(copies)]
                )
            )
            copies[-1].start()
    if first:
        squares, total = jnp.zeros((CHUNK, 128), jnp.float32), None
    else:
        squares, total = refs[0][...], refs[1][...]
    for i, (offset, block) in enumerate(zip(offsets, blocks)):
        wide = block.astype(jnp.float32)
        for at in range(0, PAIR_COLS, 128):
            squares = squares + wide[:, at : at + 128] * wide[:, at : at + 128]
        scaled = (wide * gain_ref[offset : offset + 1]).astype(jnp.bfloat16)
        copies[2 * i].wait()
        copies[2 * i + 1].wait()
        part = jnp.dot(scaled, w_vmem[i], preferred_element_type=jnp.float32)
        total = part if total is None else total + part
    if not last:
        squares_ref, total_ref = refs[-4:-2]
        squares_ref[...], total_ref[...] = squares, total
        return
    cos_ref, sin_ref, q_ref, kv_ref = refs[2:6]
    mean = jnp.sum(squares, axis=1, keepdims=True) / (16 * COLS)
    total = total * lax.rsqrt(mean + norm_eps)
    cosine, sine = cos_ref[...], sin_ref[...]
    for h in range(GROUP):
        at = slice(h * HEAD_DIM, (h + 1) * HEAD_DIM)
        q_ref[:, at] = rope(total[:, at], cosine, sine).astype(jnp.bfloat16)
    at = GROUP * HEAD_DIM
    kv_ref[:, :HEAD_DIM] = rope(total[:, at : at + HEAD_DIM], cosine, sine).astype(jnp.bfloat16)
    kv_ref[:, HEAD_DIM:] = total[:, at + HEAD_DIM :].astype(jnp.bfloat16)


def project(z, gain, weights, rotation, offsets, blocks, state):
    width = weights.shape[2]
    shapes = ((CHUNK, 128), jnp.float32), ((CHUNK, width), jnp.float32)
    extra = ()
    if offsets == (4,):
        shapes = ((CHUNK, GROUP * HEAD_DIM), jnp.bfloat16), ((CHUNK, 2 * HEAD_DIM), jnp.bfloat16)
        extra = rotation
    return pl.pallas_call(
        functools.partial(project_kernel, offsets, not state),
        out_shape=[jax.ShapeDtypeStruct(*shape) for shape in shapes],
        in_specs=[SMEM] + [VMEM] * (len(blocks) + 1) + [HBM] + [VMEM] * (len(state) + len(extra)),
        out_specs=[VMEM] * 2,
        scratch_shapes=[
            pltpu.VMEM((len(offsets), PAIR_COLS, width), jnp.bfloat16),
            pltpu.SemaphoreType.DMA((2 * len(offsets),)),
        ],
        compiler_params=pltpu.CompilerParams(vmem_limit_bytes=16 * MIB),
        cost_estimate=pl.CostEstimate(
            flops=2 * CHUNK * PAIR_COLS * width * len(offsets),
            bytes_accessed=2 * PAIR_COLS * width * len(offsets),
            transcendentals=0,
        ),
        name="norm_project",
    )(z.reshape(1), *blocks, gain, weights, *state, *extra)


def finish_kernel(offsets, place_ref, *refs):
    last = offsets == (4,)
    blocks, (total_ref, w_ref, *outs, w_vmem, sems) = take_blocks(offsets, refs)
    copies = []
    for i, offset in enumerate(offsets):
        source = (place_ref[1] + offset) & 7
        for j in (0, 1):
            at = (place_ref[1] - 2 * source - j) & 7
            at = at + N_Z * ((source >> 2) ^ place_ref[0])
            copies.append(
                pltpu.make_async_copy(w_ref.at[:, at], w_vmem.at[i, j], sems.at[len(copies)])
            )
            copies[-1].start()
    total = total_ref[...].astype(jnp.float32)
    for i, block in enumerate(blocks):
        for j in (0, 1):
            copies[2 * i + j].wait()
            total = total + jnp.dot(
                block[:, j * 2 * HEAD_DIM : (j + 1) * 2 * HEAD_DIM],
                w_vmem[i, j].reshape(2 * HEAD_DIM, PAIR_COLS),
                preferred_element_type=jnp.float32,
            )
    if not last:
        outs[0][...] = total
        return
    own_ref, other_ref = outs
    first, second = total[:, :COLS].astype(jnp.bfloat16), total[:, COLS:].astype(jnp.bfloat16)

    @pl.when(place_ref[0] == 0)
    def _():
        own_ref[...] = first
        other_ref[...] = second

    @pl.when(place_ref[0] == 1)
    def _():
        own_ref[...] = second
        other_ref[...] = first


def finish(place, mixed, weights, offsets, blocks, state):
    shapes = [jax.ShapeDtypeStruct((CHUNK, PAIR_COLS), jnp.float32)]
    if offsets == (4,):
        shapes = [jax.ShapeDtypeStruct((CHUNK, COLS), jnp.bfloat16)] * 2
    return pl.pallas_call(
        functools.partial(finish_kernel, offsets),
        out_shape=shapes,
        in_specs=[SMEM] + [VMEM] * (len(blocks) + 1) + [HBM],
        out_specs=[VMEM] * len(shapes),
        scratch_shapes=[
            pltpu.VMEM((len(offsets), 2, N_CTX, weights.shape[2], PAIR_COLS), jnp.bfloat16),
            pltpu.SemaphoreType.DMA((2 * len(offsets),)),
        ],
        compiler_params=pltpu.CompilerParams(vmem_limit_bytes=16 * MIB),
        cost_estimate=pl.CostEstimate(
            flops=2 * CHUNK * PAIR_COLS * 4 * HEAD_DIM * len(offsets),
            bytes_accessed=8 * PAIR_COLS * HEAD_DIM * len(offsets),
            transcendentals=0,
        ),
        name="project_out",
    )(place, *blocks, *(state or (mixed,)), weights)


def in_order(first, own, other, axis):
    return jnp.where(
        first, jnp.concatenate([own, other], axis=axis), jnp.concatenate([other, own], axis=axis)
    )


def per_device(
    residual,
    global_q,
    global_k,
    global_v,
    global_wo,
    norm_gain,
    stretch_wq,
    stretch_wk,
    stretch_wv,
    stretch_wo,
):
    me = lax.axis_index("ctx")
    place = lax.axis_index("tp")
    y_lo, z = place // N_Z, place % N_Z
    lower = y_lo == 0
    core = me & 1

    place_pair = jnp.stack([y_lo, z]).astype(jnp.int32)

    all_kv = lax.all_gather(take_kv(place // 2, global_k, global_v), "ctx", axis=0, tiled=False)
    slots = [slot for c in range(N_CTX) for slot in (c, 2 * N_CTX - 1 - c)]
    limits = jnp.where(lower, me + 1, 2 * N_CTX - me), jnp.where(lower, 2 * N_CTX - me, me + 1)
    ends = limits[0], y_lo * CHUNK, limits[1], (1 - y_lo) * CHUNK
    meta = jnp.stack([jnp.int32(slot) for slot in slots] + list(ends)).astype(jnp.int32)

    first_weights, half_mine = arrange(
        z, jnp.int32(0), core, global_wo, global_wo.shape[0]
    )
    rows = stretch_wo.shape[0] // N_CTX
    (share,) = arrange(z, me * rows, None, stretch_wo, rows)
    share = share.reshape(2, 2, 2, rows, PAIR_COLS)
    residual_kept, residual_given = split(place_pair, residual)
    half_mine, own_wq, came = together(
        to_other_y_lo(half_mine),
        permute(stretch_wq, "tp", lambda t: 8 * (t % 2) + t // 2),
        along_z(share[:, :, 1], 1),
    )
    share = jnp.stack([share[:, :, 0], came], axis=2)
    half_other, other_wq, came, residual_came = together(
        to_other_core(half_mine),
        to_other_y_lo(own_wq),
        along_z(share[:, 1], 2),
        to_other_y_lo(residual_given),
    )
    weights = pack(place_pair, stretch_wk, stretch_wv, own_wq, other_wq)
    share = jnp.stack([share[:, 0], came], axis=1)
    share = jnp.stack([share[0], along_z(share[1], 4)], axis=0).reshape(N_Z, rows, PAIR_COLS)
    share = jnp.concatenate([share, to_other_y_lo(share)], axis=0)

    share, weights = together(share, weights)
    gathered_weights = lax.all_gather(weights, "ctx", axis=0, tiled=False)
    last_weights = lax.all_gather(share, "ctx", axis=0, tiled=False)

    kept, given = attend(
        meta,
        global_q,
        [all_kv],
        2 * N_CTX,
        ((0, 1), (0, 1)),
        8,
        2,
        "attend_all",
        share,
        half_other,
        residual_came,
    )
    operands = core, kept, to_other_y_lo(given), (first_weights, half_mine, half_other)
    mixed = ring_reduce(operands, place_pair, (residual_kept, residual_came))

    gain = norm_gain.reshape(2, N_Z, COLS).transpose(1, 0, 2).reshape(N_Z, PAIR_COLS)
    gain = lax.dynamic_slice_in_dim(jnp.concatenate([gain, gain], axis=0), z, N_Z, 0)
    chunk = jnp.where(lower, me, 2 * N_CTX - 1 - me)
    positions = (chunk * CHUNK + jnp.arange(CHUNK, dtype=jnp.int32)).astype(jnp.float32)
    half_dim = HEAD_DIM // 2
    inv_freq = rope_base ** (-(jnp.arange(half_dim).astype(jnp.float32) * 2.0 / HEAD_DIM))
    angles = positions[:, None] * inv_freq[None, :]
    cosine, sine = jnp.cos(angles), jnp.sin(angles)
    rotation = (
        jnp.concatenate([cosine, cosine], axis=1),
        jnp.concatenate([-sine, sine], axis=1),
    )
    work = functools.partial(project, z, gain, gathered_weights, rotation)
    stretch_q, stretch_kv = work(*ring_gather(mixed, work))
    pieces = gather_ctx(stretch_kv)
    slots = [jnp.where(lower, c, N_CTX - 1 - c) for c in owners()]
    limit = jnp.where(lower, me + 1, N_CTX - me)
    meta = jnp.stack(slots + [limit, 0]).astype(jnp.int32)
    (attended,) = attend(
        meta, stretch_q, pieces, N_CTX, ((0, 1, 2, 3),), 8, 4, "attend_window"
    )
    work = functools.partial(finish, place_pair, mixed, last_weights)
    own, other = work(*ring_gather(attended, work))
    return in_order(lower, own, to_other_y_lo(other), 0)


def solution(mesh):
    in_specs = (
        P("ctx", "tp"),
        P("ctx", "tp"),
        P("ctx", None),
        P("ctx", None),
        P("tp", None),
        P(),
        P("ctx", "tp"),
        P("ctx", None),
        P("ctx", None),
        P("tp", None),
    )
    return jax.shard_map(
        per_device, mesh=mesh, in_specs=in_specs, out_specs=P("ctx", "tp"), check_vma=False
    )
```

```python
import functools

import jax
import jax.numpy as jnp
from jax import lax
from jax.experimental import pallas as pl
from jax.experimental.pallas import tpu as pltpu
from jax.sharding import PartitionSpec as P

HEAD_DIM = 128
GROUP = 4
CHUNK = 256
N_CTX = 16
N_Z = 8
COLS = 320
PAIR_COLS = 2 * COLS
rope_base = 500000.0
norm_eps = 1e-05
masked_score = -1e30
scale_log2 = 1.4426950408889634 * HEAD_DIM**-0.5
MIB = 1024 * 1024
SMEM = pl.BlockSpec(memory_space=pltpu.SMEM)
VMEM = pl.BlockSpec(memory_space=pltpu.VMEM)
HBM = pl.BlockSpec(memory_space=pltpu.HBM)


def permute(value, axis, target):
    return lax.ppermute(value, axis, [(place, target(place)) for place in range(16)])


def to_other_core(value):
    return permute(value, "ctx", lambda c: c ^ 1)


def to_other_y_hi(value):
    return permute(value, "ctx", lambda c: c ^ 8)


def along_x(value, step):
    return permute(value, "ctx", lambda c: (c & 9) | ((c + 2 * step) & 6))


def to_other_y_lo(value):
    return permute(value, "tp", lambda t: t ^ 8)


def along_z(value, step):
    return permute(value, "tp", lambda t: (t & 8) | ((t + step) & 7))


def together_kernel(*refs):
    pass


def together(*values):
    return pl.pallas_call(
        together_kernel,
        out_shape=[jax.ShapeDtypeStruct(value.shape, value.dtype) for value in values],
        in_specs=[HBM] * len(values),
        out_specs=[HBM] * len(values),
        input_output_aliases={i: i for i in range(len(values))},
        compiler_params=pltpu.CompilerParams(vmem_limit_bytes=MIB),
        name="together",
    )(*values)


def arrange_kernel(row_count, place_ref, source, *rest):
    outs, (rows, sem) = rest[:-2], rest[-2:]
    first = pl.multiple_of(place_ref[1], 16)
    copy = pltpu.make_async_copy(source.at[pl.ds(first, row_count)], rows, sem)
    copy.start()
    copy.wait()
    for z in range(N_Z):
        offset = (z - place_ref[0]) & 7
        for y_lo in (0, 1):
            at = (y_lo * N_Z + z) * COLS
            outs[0][offset, :, y_lo * COLS : (y_lo + 1) * COLS] = rows[:, at : at + COLS]
    for i, out in enumerate(outs[1:]):
        count, height = out.shape[:2]
        half = pl.ds(pl.multiple_of(place_ref[2], height), height)
        out[...] = outs[0][i * count : (i + 1) * count, half, :]


def arrange(z, first, half, weights, row_count):
    shapes = [jax.ShapeDtypeStruct((N_Z, row_count, PAIR_COLS), jnp.bfloat16)]
    place = [z, first]
    if half is not None:
        shapes += [
            jax.ShapeDtypeStruct((N_Z // 2, row_count // 2, PAIR_COLS), jnp.bfloat16)
        ] * 2
        place.append(half * (row_count // 2))
    return pl.pallas_call(
        functools.partial(arrange_kernel, row_count),
        out_shape=shapes,
        in_specs=[SMEM, HBM],
        out_specs=[VMEM] * len(shapes),
        scratch_shapes=[
            pltpu.VMEM((row_count, weights.shape[1]), jnp.bfloat16),
            pltpu.SemaphoreType.DMA,
        ],
        compiler_params=pltpu.CompilerParams(vmem_limit_bytes=20 * MIB),
        name="arrange",
    )(jnp.stack(place).astype(jnp.int32), weights)


def pack_kernel(place_ref, k_ref, v_ref, own_ref, other_ref, out_ref, sems):
    def columns(first, width):
        return pl.ds(pl.multiple_of(first, HEAD_DIM), width)

    wide = own_ref.shape[1]
    head = columns(place_ref[1] * HEAD_DIM, HEAD_DIM)
    moves = (
        (own_ref, columns(place_ref[0] * wide, wide)),
        (other_ref, columns((1 - place_ref[0]) * wide, wide)),
        (k_ref.at[:, head], pl.ds(2 * wide, HEAD_DIM)),
        (v_ref.at[:, head], pl.ds(2 * wide + HEAD_DIM, HEAD_DIM)),
    )
    copies = [
        pltpu.make_async_copy(source, out_ref.at[:, target], sems.at[i])
        for i, (source, target) in enumerate(moves)
    ]
    for copy in copies:
        copy.start()
    for copy in copies:
        copy.wait()


def pack(place, keys, values, own, other):
    rows, wide = own.shape
    return pl.pallas_call(
        pack_kernel,
        out_shape=jax.ShapeDtypeStruct((rows, 2 * (wide + HEAD_DIM)), jnp.bfloat16),
        in_specs=[SMEM] + [HBM] * 4,
        out_specs=HBM,
        scratch_shapes=[pltpu.SemaphoreType.DMA((4,))],
        compiler_params=pltpu.CompilerParams(vmem_limit_bytes=MIB),
        name="pack",
    )(place, keys, values, own, other)


def split_kernel(place_ref, value_ref, *rest):
    outs, sems = rest[-3:-1], rest[-1]
    copies = []
    for i, half in enumerate((place_ref[0], 1 - place_ref[0])):
        rows = pl.ds(pl.multiple_of(half * CHUNK, CHUNK), CHUNK)
        copies.append(pltpu.make_async_copy(value_ref.at[rows], outs[i], sems.at[i]))
        copies[-1].start()
    for copy in copies:
        copy.wait()


def split(place, value):
    half = jax.ShapeDtypeStruct((CHUNK, value.shape[1]), value.dtype)
    return pl.pallas_call(
        split_kernel,
        out_shape=(half, half),
        in_specs=[SMEM, HBM],
        out_specs=(VMEM, VMEM),
        scratch_shapes=[pltpu.SemaphoreType.DMA((2,))],
        compiler_params=pltpu.CompilerParams(vmem_limit_bytes=MIB),
        name="split",
    )(place, value)


def own_terms(offsets, core_ref, kept_ref, received_ref, weights, others, refs):
    buffer, landing, sems = refs
    half = CHUNK // 2
    copies = []
    for i, offset in enumerate(offsets):
        late, at = offset // 4, offset % 4
        sources = weights[0].at[offset], weights[1 + late].at[at], weights[3 + late].at[at]
        for j, (first, rows) in enumerate(((0, CHUNK), (CHUNK, half), (CHUNK + half, half))):
            target = buffer.at[i, pl.ds(first, rows)]
            copies.append(pltpu.make_async_copy(sources[j], target, sems.at[3 * i + j]))
            copies[-1].start()
    landed = []
    for i, other in enumerate(others):
        target = landing.at[i, pl.ds(0, other.shape[0]), pl.ds(0, other.shape[1])]
        copies.append(pltpu.make_async_copy(other, target, sems.at[len(copies)]))
        copies[-1].start()
    received = received_ref[...]
    low, high = received[:, :half], received[:, half:]
    first = jnp.full(low.shape, core_ref[0], jnp.int32) == 0
    rows = jnp.concatenate(
        [kept_ref[...], jnp.where(first, low, high), jnp.where(first, high, low)], axis=1
    )
    for copy in copies:
        copy.wait()
    for i, other in enumerate(others):
        landed.append(landing[i, : other.shape[0]].astype(jnp.float32))
    parts = [
        jnp.dot(rows, buffer[i], preferred_element_type=jnp.float32) for i in range(len(offsets))
    ]
    return parts, landed


def far_kernel(core_ref, kept_ref, received_ref, *refs):
    weights, (up_ref, down_ref, *scratch) = refs[:5], refs[5:]
    (part,), _ = own_terms((4,), core_ref, kept_ref, received_ref, weights, (), scratch)
    half = CHUNK // 2
    up_ref[...] = part[:half].astype(jnp.bfloat16)
    down_ref[...] = part[half:].astype(jnp.bfloat16)


def hop_kernel(hop, core_ref, kept_ref, received_ref, *refs):
    weights, (up_ref, down_ref, up_out_ref, down_out_ref, *scratch) = refs[:5], refs[5:]
    parts, (up, down) = own_terms(
        (hop, N_Z - hop), core_ref, kept_ref, received_ref, weights, (up_ref, down_ref), scratch
    )
    came = up.shape[0]
    rest = CHUNK - came
    up_out_ref[:came] = (parts[0][:came] + up).astype(jnp.bfloat16)
    down_out_ref[rest:] = (parts[1][rest:] + down).astype(jnp.bfloat16)
    if rest:
        up_out_ref[came:] = parts[0][came:].astype(jnp.bfloat16)
        down_out_ref[:rest] = parts[1][:rest].astype(jnp.bfloat16)


def mix_kernel(core_ref, kept_ref, received_ref, *refs):
    weights, (up_ref, down_ref, place_ref, *residual, out_ref, again_ref), scratch = (
        refs[:5],
        refs[5:-3],
        refs[-3:],
    )
    (part,), (up, down) = own_terms(
        (0,), core_ref, kept_ref, received_ref, weights, (up_ref, down_ref), scratch
    )
    total = part + up + down

    def put(first, second):
        out_ref[:, :COLS] = (total[:, :COLS] + first[...].astype(jnp.float32)).astype(jnp.bfloat16)
        out_ref[:, COLS:] = (total[:, COLS:] + second[...].astype(jnp.float32)).astype(jnp.bfloat16)

    pl.when(place_ref[0] == 0)(lambda: put(*residual))
    pl.when(place_ref[0] == 1)(lambda: put(*residual[::-1]))
    again_ref[...] = out_ref[...]


def ring_step(kernel, name, shapes, count, operands, moving=(), extra=(), extra_specs=()):
    core, kept, received, weights = operands
    return pl.pallas_call(
        kernel,
        out_shape=[jax.ShapeDtypeStruct(shape, jnp.bfloat16) for shape in shapes],
        in_specs=[SMEM, VMEM, VMEM] + [HBM] * (5 + len(moving)) + list(extra_specs),
        out_specs=[VMEM] * len(shapes),
        scratch_shapes=[
            pltpu.VMEM((count, 2 * CHUNK, PAIR_COLS), jnp.bfloat16),
            pltpu.VMEM((2, CHUNK, PAIR_COLS), jnp.bfloat16),
            pltpu.SemaphoreType.DMA((3 * count + 2,)),
        ],
        compiler_params=pltpu.CompilerParams(vmem_limit_bytes=20 * MIB),
        name=name,
    )(core.reshape(1), kept, received, *weights, *moving, *extra)


def ring_reduce(operands, place, residual):
    whole, half = (CHUNK, PAIR_COLS), (CHUNK // 2, PAIR_COLS)
    moving = ring_step(far_kernel, "far", (half, half), 1, operands)
    for hop in (3, 2, 1):
        moving = along_z(moving[0], 1), along_z(moving[1], -1)
        kernel = functools.partial(hop_kernel, hop)
        moving = ring_step(kernel, "hop", (whole, whole), 2, operands, moving)
    moving = along_z(moving[0], 1), along_z(moving[1], -1)
    extra, specs = (place, *residual), (SMEM, VMEM, VMEM)
    return ring_step(mix_kernel, "mix", (whole, whole), 1, operands, moving, extra, specs)


GATHER_OFFSETS = [
    (dy, dx, core)
    for core in (0, 1)
    for dy, dx in ((0, 0), (1, 0), (0, 3), (0, 1), (0, 2), (1, 3), (1, 1), (1, 2))
]


def gather_ctx(block):
    other = to_other_y_hi(block)
    left, right = along_x(block, 1), along_x(block, -1)
    far = along_x(left, 1)
    left_other, right_other = along_x(other, 1), along_x(other, -1)
    far_other = along_x(right_other, -1)
    mine = [block, other, left, right, far, left_other, right_other, far_other]
    return mine + [
        to_other_core(jnp.stack(mine[:4])),
        to_other_core(jnp.stack(mine[4:7])),
        to_other_core(far_other),
    ]


CLASSES = [list(range(0, N_CTX, 2)), list(range(1, N_CTX, 2))]


def gather_class(block):
    return lax.all_gather(block, "ctx", axis=0, tiled=False, axis_index_groups=CLASSES)


def owners():
    me = lax.axis_index("ctx")
    return [
        ((me & 8) ^ (8 * dy)) | ((me + 2 * dx) & 6) | ((me & 1) ^ dc)
        for dy, dx, dc in GATHER_OFFSETS
    ]


def take_kernel(place_ref, k_ref, v_ref, out_ref, sems):
    columns = pl.ds(pl.multiple_of(place_ref[0] * HEAD_DIM, HEAD_DIM), HEAD_DIM)
    copies = [
        pltpu.make_async_copy(src.at[:, columns], out_ref.at[:, pl.ds(i * HEAD_DIM, HEAD_DIM)], sems.at[i])
        for i, src in enumerate((k_ref, v_ref))
    ]
    for copy in copies:
        copy.start()
    for copy in copies:
        copy.wait()


def take_kv(place, keys, values):
    rows = keys.shape[0]
    return pl.pallas_call(
        take_kernel,
        out_shape=jax.ShapeDtypeStruct((rows, 2 * HEAD_DIM), jnp.bfloat16),
        in_specs=[SMEM, HBM, HBM],
        out_specs=VMEM,
        scratch_shapes=[pltpu.SemaphoreType.DMA((2,))],
        compiler_params=pltpu.CompilerParams(vmem_limit_bytes=60 * MIB),
        name="take_kv",
    )(place.reshape(1), keys, values)


def attend_kernel(tiles, tile_chunks, chains, earlier, meta_ref, q_ref, *rest):
    pieces, outs, (kv, sems) = rest[: -2 - len(tiles) - earlier], rest[-2 - len(tiles) : -2], rest[-2:]
    blocks = []
    for piece in pieces:
        blocks += [piece] if len(piece.shape) == 2 else [piece.at[b] for b in range(piece.shape[0])]
    copies = []
    for block in blocks:
        for part in range(block.shape[0] // CHUNK):
            source = block.at[pl.ds(part * CHUNK, CHUNK)]
            copies.append(
                pltpu.make_async_copy(source, kv.at[meta_ref[len(copies)]], sems.at[len(copies)])
            )
            copies[-1].start()
    for copy in copies:
        copy.wait()
    span = tile_chunks * CHUNK
    for tile, (heads, out_ref) in enumerate(zip(tiles, outs)):
        limit = meta_ref[len(copies) + 2 * tile]
        first = pl.multiple_of(meta_ref[len(copies) + 2 * tile + 1], CHUNK)
        rows = q_ref.at[pl.ds(first, CHUNK)]
        each = len(heads) // chains
        queries = [
            jnp.concatenate(
                [rows[:, h * HEAD_DIM : (h + 1) * HEAD_DIM] for h in heads[g * each : (g + 1) * each]],
                axis=0,
            )
            for g in range(chains)
        ]
        height = each * CHUNK

        def step(i, state, masked):
            here = pl.ds(i * tile_chunks, tile_chunks)
            keys = kv[here, :, :HEAD_DIM].reshape(span, HEAD_DIM)
            values = kv[here, :, HEAD_DIM:].reshape(span, HEAD_DIM)
            values = jnp.concatenate([values, jnp.ones(values.shape, values.dtype)], axis=1)
            if masked:
                column = lax.broadcasted_iota(jnp.int32, (height, span), 1) + i * span
                row = lax.broadcasted_iota(jnp.int32, (height, span), 0) % CHUNK
                visible = column <= row + (limit - 1) * CHUNK
            scores = [
                lax.dot_general(
                    query, keys, (((1,), (1,)), ((), ())), preferred_element_type=jnp.float32
                )
                for query in queries
            ]
            after = []
            for score, (highest, weighted) in zip(scores, state):
                if masked:
                    score = jnp.where(visible, score, masked_score)
                new_high = jnp.maximum(highest, jnp.max(score, axis=1, keepdims=True))
                fade = jnp.exp2((highest - new_high) * scale_log2)
                scores_here = score * scale_log2 - new_high * scale_log2
                weights = jnp.exp2(scores_here).astype(jnp.bfloat16)
                weighted = weighted * fade + jnp.dot(
                    weights, values, preferred_element_type=jnp.float32
                )
                after.append((new_high, weighted))
            return tuple(after)

        state = tuple(
            (
                jnp.full((height, 1), masked_score, jnp.float32),
                jnp.zeros((height, 2 * HEAD_DIM), jnp.float32),
            )
            for _ in range(chains)
        )
        whole = lax.div(limit - 1, jnp.int32(tile_chunks))
        state = lax.fori_loop(0, whole, functools.partial(step, masked=False), state)
        state = step(whole, state, True)
        for g, (_, weighted) in enumerate(state):
            result = (weighted[:, :HEAD_DIM] / weighted[:, HEAD_DIM:]).astype(jnp.bfloat16)
            for j in range(each):
                h = heads[g * each + j]
                out_ref[:, h * HEAD_DIM : (h + 1) * HEAD_DIM] = result[
                    j * CHUNK : (j + 1) * CHUNK
                ]


def attend(meta, queries, pieces, chunks, tiles, tile_chunks, chains, name, *earlier):
    return pl.pallas_call(
        functools.partial(attend_kernel, tiles, tile_chunks, chains, len(earlier)),
        out_shape=[jax.ShapeDtypeStruct((CHUNK, queries.shape[1]), jnp.bfloat16)] * len(tiles),
        in_specs=[SMEM, VMEM] + [HBM] * (len(pieces) + len(earlier)),
        out_specs=[VMEM] * len(tiles),
        scratch_shapes=[
            pltpu.VMEM((chunks, CHUNK, 2 * HEAD_DIM), jnp.bfloat16),
            pltpu.SemaphoreType.DMA((chunks,)),
        ],
        compiler_params=pltpu.CompilerParams(vmem_limit_bytes=32 * MIB),
        cost_estimate=pl.CostEstimate(
            flops=2_200_000_000, bytes_accessed=5_000_000, transcendentals=10_000_000
        ),
        name=name,
    )(meta, queries, *pieces, *earlier)


def ring_gather(block, again, work):
    half = block.shape[0] // 2
    below, above = along_z(block, 1), along_z(again, -1)
    offsets, blocks, state = (0, 1, 7), (block, above, below), ()
    for hop in (2, 3, 4):
        if hop == 4:
            below, above = below[:half], above[half:]
        below, above = along_z(below, 1), along_z(above, -1)
        below, above, *state = together(below, above, *work(offsets, blocks, state))
        offsets, blocks = (hop, 8 - hop), (above, below)
    return (4,), (below, above), state


def rope(value, cosine, sine):
    return value * cosine + pltpu.roll(value, HEAD_DIM // 2, axis=1) * sine


def take_blocks(offsets, refs):
    if offsets == (4,):
        return [jnp.concatenate([refs[0][...], refs[1][...]], axis=0)], refs[2:]
    return [ref[...] for ref in refs[: len(offsets)]], refs[len(offsets) :]


def project_kernel(offsets, first, z_ref, *refs):
    last = offsets == (4,)
    blocks, (gain_ref, w_ref, *refs) = take_blocks(offsets, refs)
    w_vmem, sems = refs[-2:]
    copies = []
    for i, offset in enumerate(offsets):
        source = (z_ref[0] + offset) & 7
        for y_lo in (0, 1):
            rows = pl.ds(y_lo * COLS, COLS)
            copies.append(
                pltpu.make_async_copy(
                    w_ref.at[y_lo * N_Z + source], w_vmem.at[i, rows], sems.at[len(copies)]
                )
            )
            copies[-1].start()
    if first:
        squares, total = jnp.zeros((CHUNK, 128), jnp.float32), None
    else:
        squares, total = refs[0][...], refs[1][...]
    for i, (offset, block) in enumerate(zip(offsets, blocks)):
        wide = block.astype(jnp.float32)
        for at in range(0, PAIR_COLS, 128):
            squares = squares + wide[:, at : at + 128] * wide[:, at : at + 128]
        scaled = (wide * gain_ref[offset : offset + 1]).astype(jnp.bfloat16)
        copies[2 * i].wait()
        copies[2 * i + 1].wait()
        part = jnp.dot(scaled, w_vmem[i], preferred_element_type=jnp.float32)
        total = part if total is None else total + part
    if not last:
        squares_ref, total_ref = refs[-4:-2]
        squares_ref[...], total_ref[...] = squares, total
        return
    cos_ref, sin_ref, q_ref, kv_ref = refs[2:6]
    mean = jnp.sum(squares, axis=1, keepdims=True) / (16 * COLS)
    total = total * lax.rsqrt(mean + norm_eps)
    cosine, sine = cos_ref[...], sin_ref[...]
    for h in range(GROUP):
        at = slice(h * HEAD_DIM, (h + 1) * HEAD_DIM)
        q_ref[:, at] = rope(total[:, at], cosine, sine).astype(jnp.bfloat16)
    at = GROUP * HEAD_DIM
    kv_ref[:, :HEAD_DIM] = rope(total[:, at : at + HEAD_DIM], cosine, sine).astype(jnp.bfloat16)
    kv_ref[:, HEAD_DIM:] = total[:, at + HEAD_DIM :].astype(jnp.bfloat16)


def project(z, gain, weights, rotation, offsets, blocks, state):
    width = weights.shape[2]
    shapes = ((CHUNK, 128), jnp.float32), ((CHUNK, width), jnp.float32)
    extra = ()
    if offsets == (4,):
        shapes = ((CHUNK, GROUP * HEAD_DIM), jnp.bfloat16), ((CHUNK, 2 * HEAD_DIM), jnp.bfloat16)
        extra = rotation
    return pl.pallas_call(
        functools.partial(project_kernel, offsets, not state),
        out_shape=[jax.ShapeDtypeStruct(*shape) for shape in shapes],
        in_specs=[SMEM] + [VMEM] * (len(blocks) + 1) + [HBM] + [VMEM] * (len(state) + len(extra)),
        out_specs=[VMEM] * 2,
        scratch_shapes=[
            pltpu.VMEM((len(offsets), PAIR_COLS, width), jnp.bfloat16),
            pltpu.SemaphoreType.DMA((2 * len(offsets),)),
        ],
        compiler_params=pltpu.CompilerParams(vmem_limit_bytes=16 * MIB),
        cost_estimate=pl.CostEstimate(
            flops=2 * CHUNK * PAIR_COLS * width * len(offsets),
            bytes_accessed=2 * PAIR_COLS * width * len(offsets),
            transcendentals=0,
        ),
        name="norm_project",
    )(z.reshape(1), *blocks, gain, weights, *state, *extra)


def finish_kernel(offsets, place_ref, *refs):
    last = offsets == (4,)
    blocks, (total_ref, w_ref, *outs, w_vmem, sems) = take_blocks(offsets, refs)
    copies = []
    for i, offset in enumerate(offsets):
        source = (place_ref[1] + offset) & 7
        for j in (0, 1):
            at = (place_ref[1] - 2 * source - j) & 7
            at = at + N_Z * ((source >> 2) ^ place_ref[0])
            copies.append(
                pltpu.make_async_copy(w_ref.at[:, at], w_vmem.at[i, j], sems.at[len(copies)])
            )
            copies[-1].start()
    total = total_ref[...].astype(jnp.float32)
    for i, block in enumerate(blocks):
        for j in (0, 1):
            copies[2 * i + j].wait()
            total = total + jnp.dot(
                block[:, j * 2 * HEAD_DIM : (j + 1) * 2 * HEAD_DIM],
                w_vmem[i, j].reshape(2 * HEAD_DIM, PAIR_COLS),
                preferred_element_type=jnp.float32,
            )
    if not last:
        outs[0][...] = total
        return
    own_ref, other_ref = outs
    first, second = total[:, :COLS].astype(jnp.bfloat16), total[:, COLS:].astype(jnp.bfloat16)

    @pl.when(place_ref[0] == 0)
    def _():
        own_ref[...] = first
        other_ref[...] = second

    @pl.when(place_ref[0] == 1)
    def _():
        own_ref[...] = second
        other_ref[...] = first


def finish(place, mixed, weights, offsets, blocks, state):
    shapes = [jax.ShapeDtypeStruct((CHUNK, PAIR_COLS), jnp.float32)]
    if offsets == (4,):
        shapes = [jax.ShapeDtypeStruct((CHUNK, COLS), jnp.bfloat16)] * 2
    return pl.pallas_call(
        functools.partial(finish_kernel, offsets),
        out_shape=shapes,
        in_specs=[SMEM] + [VMEM] * (len(blocks) + 1) + [HBM],
        out_specs=[VMEM] * len(shapes),
        scratch_shapes=[
            pltpu.VMEM((len(offsets), 2, N_CTX, weights.shape[2], PAIR_COLS), jnp.bfloat16),
            pltpu.SemaphoreType.DMA((2 * len(offsets),)),
        ],
        compiler_params=pltpu.CompilerParams(vmem_limit_bytes=16 * MIB),
        cost_estimate=pl.CostEstimate(
            flops=2 * CHUNK * PAIR_COLS * 4 * HEAD_DIM * len(offsets),
            bytes_accessed=8 * PAIR_COLS * HEAD_DIM * len(offsets),
            transcendentals=0,
        ),
        name="project_out",
    )(place, *blocks, *(state or (mixed,)), weights)


def in_order(first, own, other, axis):
    return jnp.where(
        first, jnp.concatenate([own, other], axis=axis), jnp.concatenate([other, own], axis=axis)
    )


def per_device(
    residual,
    global_q,
    global_k,
    global_v,
    global_wo,
    norm_gain,
    stretch_wq,
    stretch_wk,
    stretch_wv,
    stretch_wo,
):
    me = lax.axis_index("ctx")
    place = lax.axis_index("tp")
    y_lo, z = place // N_Z, place % N_Z
    lower = y_lo == 0
    core = me & 1

    place_pair = jnp.stack([y_lo, z]).astype(jnp.int32)

    class_kv = gather_class(take_kv(place // 2, global_k, global_v))
    ctx_order = [2 * k + side for side in (core, 1 - core) for k in range(N_CTX // 2)]
    slots = [slot for c in ctx_order for slot in (c, 2 * N_CTX - 1 - c)]
    limits = jnp.where(lower, me + 1, 2 * N_CTX - me), jnp.where(lower, 2 * N_CTX - me, me + 1)
    ends = limits[0], y_lo * CHUNK, limits[1], (1 - y_lo) * CHUNK
    meta = jnp.stack([*slots, *ends]).astype(jnp.int32)

    first_weights, mine_a, mine_b = arrange(
        z, jnp.int32(0), core, global_wo, global_wo.shape[0]
    )
    rows = stretch_wo.shape[0] // N_CTX
    (share,) = arrange(z, me * rows, None, stretch_wo, rows)
    share = share.reshape(2, 2, 2, rows, PAIR_COLS)
    residual_kept, residual_given = split(place_pair, residual)
    own_wq, mine_a, came = together(
        permute(stretch_wq, "tp", lambda t: 8 * (t % 2) + t // 2),
        to_other_y_lo(mine_a),
        along_z(share[:, :, 1], 1),
    )
    share = jnp.stack([share[:, :, 0], came], axis=2)
    other_wq, mine_b, came = together(
        to_other_y_lo(own_wq), to_other_y_lo(mine_b), along_z(share[:, 1], 2)
    )
    share = jnp.stack([share[:, 0], came], axis=1)
    weights = pack(place_pair, stretch_wk, stretch_wv, own_wq, other_wq)
    other_a, other_b, residual_came, came, weights = together(
        to_other_core(mine_a),
        to_other_core(mine_b),
        to_other_y_lo(residual_given),
        along_z(share[1], 4),
        weights,
    )
    share = jnp.stack([share[0], came], axis=0).reshape(N_Z, rows, PAIR_COLS)
    share = jnp.concatenate([share, to_other_y_lo(share)], axis=0)

    weights, _ = together(weights, class_kv[0, :16, :HEAD_DIM])
    gathered_weights = lax.all_gather(weights, "ctx", axis=0, tiled=False)

    kept, given = attend(
        meta,
        global_q,
        [class_kv, to_other_core(class_kv)],
        2 * N_CTX,
        ((0, 1), (0, 1)),
        8,
        2,
        "attend_all",
        other_a,
        residual_came,
    )
    kept, share = together(kept, share)
    last_weights = lax.all_gather(share, "ctx", axis=0, tiled=False)
    parts = first_weights, mine_a, mine_b, other_a, other_b
    operands = core, kept, to_other_y_lo(given), parts
    mixed, again = ring_reduce(operands, place_pair, (residual_kept, residual_came))

    gain = norm_gain.reshape(2, N_Z, COLS).transpose(1, 0, 2).reshape(N_Z, PAIR_COLS)
    gain = lax.dynamic_slice_in_dim(jnp.concatenate([gain, gain], axis=0), z, N_Z, 0)
    chunk = jnp.where(lower, me, 2 * N_CTX - 1 - me)
    positions = (chunk * CHUNK + jnp.arange(CHUNK, dtype=jnp.int32)).astype(jnp.float32)
    half_dim = HEAD_DIM // 2
    inv_freq = rope_base ** (-(jnp.arange(half_dim).astype(jnp.float32) * 2.0 / HEAD_DIM))
    angles = positions[:, None] * inv_freq[None, :]
    cosine, sine = jnp.cos(angles), jnp.sin(angles)
    rotation = (
        jnp.concatenate([cosine, cosine], axis=1),
        jnp.concatenate([-sine, sine], axis=1),
    )
    work = functools.partial(project, z, gain, gathered_weights, rotation)
    stretch_q, stretch_kv = work(*ring_gather(mixed, again, work))
    pieces = gather_ctx(stretch_kv)
    slots = [jnp.where(lower, c, N_CTX - 1 - c) for c in owners()]
    limit = jnp.where(lower, me + 1, N_CTX - me)
    meta = jnp.stack(slots + [limit, 0]).astype(jnp.int32)
    (attended,) = attend(
        meta, stretch_q, pieces, N_CTX, ((0, 1, 2, 3),), 8, 4, "attend_window"
    )
    work = functools.partial(finish, place_pair, mixed, last_weights)
    own, other = work(*ring_gather(attended, attended, work))
    return in_order(lower, own, to_other_y_lo(other), 0)


def solution(mesh):
    in_specs = (
        P("ctx", "tp"),
        P("ctx", "tp"),
        P("ctx", None),
        P("ctx", None),
        P("tp", None),
        P(),
        P("ctx", "tp"),
        P("ctx", None),
        P("ctx", None),
        P("tp", None),
    )
    return jax.shard_map(
        per_device, mesh=mesh, in_specs=in_specs, out_specs=P("ctx", "tp"), check_vma=False
    )
```

```python
import functools

import jax
import jax.numpy as jnp
from jax import lax
from jax.experimental import pallas as pl
from jax.experimental.pallas import tpu as pltpu
from jax.sharding import PartitionSpec as P

HEAD_DIM = 128
GROUP = 4
CHUNK = 256
N_CTX = 16
N_Z = 8
COLS = 320
PAIR_COLS = 2 * COLS
rope_base = 500000.0
norm_eps = 1e-05
masked_score = -1e30
scale_log2 = 1.4426950408889634 * HEAD_DIM**-0.5
MIB = 1024 * 1024
SMEM = pl.BlockSpec(memory_space=pltpu.SMEM)
VMEM = pl.BlockSpec(memory_space=pltpu.VMEM)
HBM = pl.BlockSpec(memory_space=pltpu.HBM)


def permute(value, axis, target):
    return lax.ppermute(value, axis, [(place, target(place)) for place in range(16)])


def to_other_core(value):
    return permute(value, "ctx", lambda c: c ^ 1)


def to_other_y_hi(value):
    return permute(value, "ctx", lambda c: c ^ 8)


def along_x(value, step):
    return permute(value, "ctx", lambda c: (c & 9) | ((c + 2 * step) & 6))


def to_other_y_lo(value):
    return permute(value, "tp", lambda t: t ^ 8)


def along_z(value, step):
    return permute(value, "tp", lambda t: (t & 8) | ((t + step) & 7))


def together_kernel(*refs):
    pass


def together(*values):
    return pl.pallas_call(
        together_kernel,
        out_shape=[jax.ShapeDtypeStruct(value.shape, value.dtype) for value in values],
        in_specs=[HBM] * len(values),
        out_specs=[HBM] * len(values),
        input_output_aliases={i: i for i in range(len(values))},
        compiler_params=pltpu.CompilerParams(vmem_limit_bytes=MIB),
        name="together",
    )(*values)


def arrange_kernel(row_count, place_ref, source, *rest):
    outs, (rows, sem) = rest[:-2], rest[-2:]
    first = pl.multiple_of(place_ref[1], 16)
    copy = pltpu.make_async_copy(source.at[pl.ds(first, row_count)], rows, sem)
    copy.start()
    copy.wait()
    for z in range(N_Z):
        offset = (z - place_ref[0]) & 7
        for y_lo in (0, 1):
            at = (y_lo * N_Z + z) * COLS
            outs[0][offset, :, y_lo * COLS : (y_lo + 1) * COLS] = rows[:, at : at + COLS]
    for i, out in enumerate(outs[1:]):
        count, height = out.shape[:2]
        half = pl.ds(pl.multiple_of(place_ref[2], height), height)
        out[...] = outs[0][i * count : (i + 1) * count, half, :]


def arrange(z, first, half, weights, row_count):
    shapes = [jax.ShapeDtypeStruct((N_Z, row_count, PAIR_COLS), jnp.bfloat16)]
    place = [z, first]
    if half is not None:
        shapes += [
            jax.ShapeDtypeStruct((N_Z // 2, row_count // 2, PAIR_COLS), jnp.bfloat16)
        ] * 2
        place.append(half * (row_count // 2))
    return pl.pallas_call(
        functools.partial(arrange_kernel, row_count),
        out_shape=shapes,
        in_specs=[SMEM, HBM],
        out_specs=[VMEM] * len(shapes),
        scratch_shapes=[
            pltpu.VMEM((row_count, weights.shape[1]), jnp.bfloat16),
            pltpu.SemaphoreType.DMA,
        ],
        compiler_params=pltpu.CompilerParams(vmem_limit_bytes=20 * MIB),
        name="arrange",
    )(jnp.stack(place).astype(jnp.int32), weights)


def pack_kernel(place_ref, k_ref, v_ref, own_ref, other_ref, out_ref, sems):
    def columns(first, width):
        return pl.ds(pl.multiple_of(first, HEAD_DIM), width)

    wide = own_ref.shape[1]
    head = columns(place_ref[1] * HEAD_DIM, HEAD_DIM)
    moves = (
        (own_ref, columns(place_ref[0] * wide, wide)),
        (other_ref, columns((1 - place_ref[0]) * wide, wide)),
        (k_ref.at[:, head], pl.ds(2 * wide, HEAD_DIM)),
        (v_ref.at[:, head], pl.ds(2 * wide + HEAD_DIM, HEAD_DIM)),
    )
    copies = [
        pltpu.make_async_copy(source, out_ref.at[:, target], sems.at[i])
        for i, (source, target) in enumerate(moves)
    ]
    for copy in copies:
        copy.start()
    for copy in copies:
        copy.wait()


def pack(place, keys, values, own, other):
    rows, wide = own.shape
    return pl.pallas_call(
        pack_kernel,
        out_shape=jax.ShapeDtypeStruct((rows, 2 * (wide + HEAD_DIM)), jnp.bfloat16),
        in_specs=[SMEM] + [HBM] * 4,
        out_specs=HBM,
        scratch_shapes=[pltpu.SemaphoreType.DMA((4,))],
        compiler_params=pltpu.CompilerParams(vmem_limit_bytes=MIB),
        name="pack",
    )(place, keys, values, own, other)


def split_kernel(place_ref, value_ref, *rest):
    outs, sems = rest[-3:-1], rest[-1]
    copies = []
    for i, half in enumerate((place_ref[0], 1 - place_ref[0])):
        rows = pl.ds(pl.multiple_of(half * CHUNK, CHUNK), CHUNK)
        copies.append(pltpu.make_async_copy(value_ref.at[rows], outs[i], sems.at[i]))
        copies[-1].start()
    for copy in copies:
        copy.wait()


def split(place, value):
    half = jax.ShapeDtypeStruct((CHUNK, value.shape[1]), value.dtype)
    return pl.pallas_call(
        split_kernel,
        out_shape=(half, half),
        in_specs=[SMEM, HBM],
        out_specs=(VMEM, VMEM),
        scratch_shapes=[pltpu.SemaphoreType.DMA((2,))],
        compiler_params=pltpu.CompilerParams(vmem_limit_bytes=MIB),
        name="split",
    )(place, value)


def own_terms(offsets, core_ref, kept_ref, received_ref, weights, others, refs):
    buffer, landing, sems = refs
    half = CHUNK // 2
    copies = []
    for i, offset in enumerate(offsets):
        late, at = offset // 4, offset % 4
        sources = weights[0].at[offset], weights[1 + late].at[at], weights[3 + late].at[at]
        for j, (first, rows) in enumerate(((0, CHUNK), (CHUNK, half), (CHUNK + half, half))):
            target = buffer.at[i, pl.ds(first, rows)]
            copies.append(pltpu.make_async_copy(sources[j], target, sems.at[3 * i + j]))
            copies[-1].start()
    landed = []
    for i, other in enumerate(others):
        target = landing.at[i, pl.ds(0, other.shape[0]), pl.ds(0, other.shape[1])]
        copies.append(pltpu.make_async_copy(other, target, sems.at[len(copies)]))
        copies[-1].start()
    received = received_ref[...]
    low, high = received[:, :half], received[:, half:]
    first = jnp.full(low.shape, core_ref[0], jnp.int32) == 0
    rows = jnp.concatenate(
        [kept_ref[...], jnp.where(first, low, high), jnp.where(first, high, low)], axis=1
    )
    for copy in copies:
        copy.wait()
    for i, other in enumerate(others):
        landed.append(landing[i, : other.shape[0]].astype(jnp.float32))
    parts = [
        jnp.dot(rows, buffer[i], preferred_element_type=jnp.float32) for i in range(len(offsets))
    ]
    return parts, landed


def terms_kernel(offsets, core_ref, kept_ref, received_ref, *refs):
    weights, (*outs, buffer, landing, sems) = refs[:5], refs[5:]
    scratch = buffer, landing, sems
    parts, _ = own_terms(offsets, core_ref, kept_ref, received_ref, weights, (), scratch)
    if offsets == (4,):
        parts = parts[0][: CHUNK // 2], parts[0][CHUNK // 2 :]
    for part, out in zip(parts, outs):
        out[...] = part.astype(jnp.bfloat16)


def hop_kernel(up_ref, down_ref, up_term_ref, down_term_ref, up_out_ref, down_out_ref):
    came = up_ref.shape[0]
    rest = CHUNK - came
    up, down = up_term_ref[:came].astype(jnp.float32), down_term_ref[rest:].astype(jnp.float32)
    up_out_ref[:came] = (up + up_ref[...].astype(jnp.float32)).astype(jnp.bfloat16)
    down_out_ref[rest:] = (down + down_ref[...].astype(jnp.float32)).astype(jnp.bfloat16)
    if rest:
        up_out_ref[came:] = up_term_ref[came:]
        down_out_ref[:rest] = down_term_ref[:rest]


def mix_kernel(up_ref, down_ref, term_ref, place_ref, *refs):
    *residual, out_ref, again_ref = refs
    total = sum(ref[...].astype(jnp.float32) for ref in (up_ref, down_ref, term_ref))

    def put(first, second):
        out_ref[:, :COLS] = (total[:, :COLS] + first[...].astype(jnp.float32)).astype(jnp.bfloat16)
        out_ref[:, COLS:] = (total[:, COLS:] + second[...].astype(jnp.float32)).astype(jnp.bfloat16)

    pl.when(place_ref[0] == 0)(lambda: put(*residual))
    pl.when(place_ref[0] == 1)(lambda: put(*residual[::-1]))
    again_ref[...] = out_ref[...]


def terms(offsets, core, kept, received, weights):
    count = len(offsets)
    shapes = [(CHUNK, PAIR_COLS)] * count if offsets != (4,) else [(CHUNK // 2, PAIR_COLS)] * 2
    return pl.pallas_call(
        functools.partial(terms_kernel, offsets),
        out_shape=[jax.ShapeDtypeStruct(shape, jnp.bfloat16) for shape in shapes],
        in_specs=[SMEM, VMEM, VMEM] + [HBM] * 5,
        out_specs=[VMEM] * len(shapes),
        scratch_shapes=[
            pltpu.VMEM((count, 2 * CHUNK, PAIR_COLS), jnp.bfloat16),
            pltpu.VMEM((1, 16, 128), jnp.bfloat16),
            pltpu.SemaphoreType.DMA((3 * count,)),
        ],
        compiler_params=pltpu.CompilerParams(vmem_limit_bytes=24 * MIB),
        name="terms",
    )(core.reshape(1), kept, received, *weights)


def ring_step(kernel, name, *operands):
    specs = [SMEM if operand.ndim == 1 else VMEM for operand in operands]
    return pl.pallas_call(
        kernel,
        out_shape=[jax.ShapeDtypeStruct((CHUNK, PAIR_COLS), jnp.bfloat16)] * 2,
        in_specs=specs,
        out_specs=[VMEM] * 2,
        compiler_params=pltpu.CompilerParams(vmem_limit_bytes=8 * MIB),
        name=name,
    )(*operands)


def ring_reduce(operands, place, residual):
    up, down = terms((4,), *operands)
    up, down = along_z(up, 1), along_z(down, -1)
    offsets = (3, 5, 2, 6, 1, 7, 0)
    term = dict(zip(offsets, terms(offsets, *operands)))
    for hop in (3, 2, 1):
        up, down = ring_step(hop_kernel, "hop", up, down, term[hop], term[N_Z - hop])
        up, down = along_z(up, 1), along_z(down, -1)
    return ring_step(mix_kernel, "mix", up, down, term[0], place, *residual)


GATHER_OFFSETS = [
    (dy, dx, core)
    for core in (0, 1)
    for dy, dx in ((0, 0), (1, 0), (0, 3), (0, 1), (0, 2), (1, 3), (1, 1), (1, 2))
]


def gather_ctx(block):
    other = to_other_y_hi(block)
    left, right = along_x(block, 1), along_x(block, -1)
    far = along_x(left, 1)
    left_other, right_other = along_x(other, 1), along_x(other, -1)
    far_other = along_x(right_other, -1)
    mine = [block, other, left, right, far, left_other, right_other, far_other]
    return mine + [
        to_other_core(jnp.stack(mine[:4])),
        to_other_core(jnp.stack(mine[4:7])),
        to_other_core(far_other),
    ]


CLASSES = [list(range(0, N_CTX, 2)), list(range(1, N_CTX, 2))]


def gather_class(block):
    return lax.all_gather(block, "ctx", axis=0, tiled=False, axis_index_groups=CLASSES)


def owners():
    me = lax.axis_index("ctx")
    return [
        ((me & 8) ^ (8 * dy)) | ((me + 2 * dx) & 6) | ((me & 1) ^ dc)
        for dy, dx, dc in GATHER_OFFSETS
    ]


def take_kernel(place_ref, k_ref, v_ref, out_ref, sems):
    columns = pl.ds(pl.multiple_of(place_ref[0] * HEAD_DIM, HEAD_DIM), HEAD_DIM)
    copies = [
        pltpu.make_async_copy(src.at[:, columns], out_ref.at[:, pl.ds(i * HEAD_DIM, HEAD_DIM)], sems.at[i])
        for i, src in enumerate((k_ref, v_ref))
    ]
    for copy in copies:
        copy.start()
    for copy in copies:
        copy.wait()


def take_kv(place, keys, values):
    rows = keys.shape[0]
    return pl.pallas_call(
        take_kernel,
        out_shape=jax.ShapeDtypeStruct((rows, 2 * HEAD_DIM), jnp.bfloat16),
        in_specs=[SMEM, HBM, HBM],
        out_specs=VMEM,
        scratch_shapes=[pltpu.SemaphoreType.DMA((2,))],
        compiler_params=pltpu.CompilerParams(vmem_limit_bytes=60 * MIB),
        name="take_kv",
    )(place.reshape(1), keys, values)


def attend_kernel(tiles, tile_chunks, chains, earlier, meta_ref, q_ref, *rest):
    pieces, outs, (kv, sems) = rest[: -2 - len(tiles) - earlier], rest[-2 - len(tiles) : -2], rest[-2:]
    blocks = []
    for piece in pieces:
        blocks += [piece] if len(piece.shape) == 2 else [piece.at[b] for b in range(piece.shape[0])]
    copies = []
    for block in blocks:
        for part in range(block.shape[0] // CHUNK):
            source = block.at[pl.ds(part * CHUNK, CHUNK)]
            copies.append(
                pltpu.make_async_copy(source, kv.at[meta_ref[len(copies)]], sems.at[len(copies)])
            )
            copies[-1].start()
    for copy in copies:
        copy.wait()
    span = tile_chunks * CHUNK
    for tile, (heads, out_ref) in enumerate(zip(tiles, outs)):
        limit = meta_ref[len(copies) + 2 * tile]
        first = pl.multiple_of(meta_ref[len(copies) + 2 * tile + 1], CHUNK)
        rows = q_ref.at[pl.ds(first, CHUNK)]
        each = len(heads) // chains
        queries = [
            jnp.concatenate(
                [rows[:, h * HEAD_DIM : (h + 1) * HEAD_DIM] for h in heads[g * each : (g + 1) * each]],
                axis=0,
            )
            for g in range(chains)
        ]
        height = each * CHUNK

        def step(i, state, masked):
            here = pl.ds(i * tile_chunks, tile_chunks)
            keys = kv[here, :, :HEAD_DIM].reshape(span, HEAD_DIM)
            values = kv[here, :, HEAD_DIM:].reshape(span, HEAD_DIM)
            values = jnp.concatenate([values, jnp.ones(values.shape, values.dtype)], axis=1)
            if masked:
                column = lax.broadcasted_iota(jnp.int32, (height, span), 1) + i * span
                row = lax.broadcasted_iota(jnp.int32, (height, span), 0) % CHUNK
                visible = column <= row + (limit - 1) * CHUNK
            scores = [
                lax.dot_general(
                    query, keys, (((1,), (1,)), ((), ())), preferred_element_type=jnp.float32
                )
                for query in queries
            ]
            after = []
            for score, (highest, weighted) in zip(scores, state):
                if masked:
                    score = jnp.where(visible, score, masked_score)
                new_high = jnp.maximum(highest, jnp.max(score, axis=1, keepdims=True))
                fade = jnp.exp2((highest - new_high) * scale_log2)
                scores_here = score * scale_log2 - new_high * scale_log2
                weights = jnp.exp2(scores_here).astype(jnp.bfloat16)
                weighted = weighted * fade + jnp.dot(
                    weights, values, preferred_element_type=jnp.float32
                )
                after.append((new_high, weighted))
            return tuple(after)

        state = tuple(
            (
                jnp.full((height, 1), masked_score, jnp.float32),
                jnp.zeros((height, 2 * HEAD_DIM), jnp.float32),
            )
            for _ in range(chains)
        )
        whole = lax.div(limit - 1, jnp.int32(tile_chunks))
        state = lax.fori_loop(0, whole, functools.partial(step, masked=False), state)
        state = step(whole, state, True)
        for g, (_, weighted) in enumerate(state):
            result = (weighted[:, :HEAD_DIM] / weighted[:, HEAD_DIM:]).astype(jnp.bfloat16)
            for j in range(each):
                h = heads[g * each + j]
                out_ref[:, h * HEAD_DIM : (h + 1) * HEAD_DIM] = result[
                    j * CHUNK : (j + 1) * CHUNK
                ]


def attend(meta, queries, pieces, chunks, tiles, tile_chunks, chains, name, *earlier):
    return pl.pallas_call(
        functools.partial(attend_kernel, tiles, tile_chunks, chains, len(earlier)),
        out_shape=[jax.ShapeDtypeStruct((CHUNK, queries.shape[1]), jnp.bfloat16)] * len(tiles),
        in_specs=[SMEM, VMEM] + [HBM] * (len(pieces) + len(earlier)),
        out_specs=[VMEM] * len(tiles),
        scratch_shapes=[
            pltpu.VMEM((chunks, CHUNK, 2 * HEAD_DIM), jnp.bfloat16),
            pltpu.SemaphoreType.DMA((chunks,)),
        ],
        compiler_params=pltpu.CompilerParams(vmem_limit_bytes=32 * MIB),
        cost_estimate=pl.CostEstimate(
            flops=2_200_000_000, bytes_accessed=5_000_000, transcendentals=10_000_000
        ),
        name=name,
    )(meta, queries, *pieces, *earlier)


def ring_gather(block, again, work):
    half = block.shape[0] // 2
    below, above = block, again
    offsets, blocks, state = (0,), (block,), ()
    for hop in (1, 2, 3, 4):
        if hop == 4:
            below, above = below[:half], above[half:]
        below, above = along_z(below, 1), along_z(above, -1)
        below, above, *state = together(below, above, *work(offsets, blocks, state))
        offsets, blocks = (hop, 8 - hop), (above, below)
    return (4,), (below, above), state


def rope(value, cosine, sine):
    return value * cosine + pltpu.roll(value, HEAD_DIM // 2, axis=1) * sine


def take_blocks(offsets, refs):
    if offsets == (4,):
        return [jnp.concatenate([refs[0][...], refs[1][...]], axis=0)], refs[2:]
    return [ref[...] for ref in refs[: len(offsets)]], refs[len(offsets) :]


def project_kernel(offsets, first, z_ref, *refs):
    last = offsets == (4,)
    blocks, (gain_ref, w_ref, *refs) = take_blocks(offsets, refs)
    w_vmem, sems = refs[-2:]
    copies = []
    for i, offset in enumerate(offsets):
        source = (z_ref[0] + offset) & 7
        for y_lo in (0, 1):
            rows = pl.ds(y_lo * COLS, COLS)
            copies.append(
                pltpu.make_async_copy(
                    w_ref.at[y_lo * N_Z + source], w_vmem.at[i, rows], sems.at[len(copies)]
                )
            )
            copies[-1].start()
    if first:
        squares, total = jnp.zeros((CHUNK, 128), jnp.float32), None
    else:
        squares, total = refs[0][...], refs[1][...]
    for i, (offset, block) in enumerate(zip(offsets, blocks)):
        wide = block.astype(jnp.float32)
        for at in range(0, PAIR_COLS, 128):
            squares = squares + wide[:, at : at + 128] * wide[:, at : at + 128]
        scaled = (wide * gain_ref[offset : offset + 1]).astype(jnp.bfloat16)
        copies[2 * i].wait()
        copies[2 * i + 1].wait()
        part = jnp.dot(scaled, w_vmem[i], preferred_element_type=jnp.float32)
        total = part if total is None else total + part
    if not last:
        squares_ref, total_ref = refs[-4:-2]
        squares_ref[...], total_ref[...] = squares, total
        return
    cos_ref, sin_ref, q_ref, kv_ref = refs[2:6]
    mean = jnp.sum(squares, axis=1, keepdims=True) / (16 * COLS)
    total = total * lax.rsqrt(mean + norm_eps)
    cosine, sine = cos_ref[...], sin_ref[...]
    for h in range(GROUP):
        at = slice(h * HEAD_DIM, (h + 1) * HEAD_DIM)
        q_ref[:, at] = rope(total[:, at], cosine, sine).astype(jnp.bfloat16)
    at = GROUP * HEAD_DIM
    kv_ref[:, :HEAD_DIM] = rope(total[:, at : at + HEAD_DIM], cosine, sine).astype(jnp.bfloat16)
    kv_ref[:, HEAD_DIM:] = total[:, at + HEAD_DIM :].astype(jnp.bfloat16)


def project(z, gain, weights, rotation, offsets, blocks, state):
    width = weights.shape[2]
    shapes = ((CHUNK, 128), jnp.float32), ((CHUNK, width), jnp.float32)
    extra = ()
    if offsets == (4,):
        shapes = ((CHUNK, GROUP * HEAD_DIM), jnp.bfloat16), ((CHUNK, 2 * HEAD_DIM), jnp.bfloat16)
        extra = rotation
    return pl.pallas_call(
        functools.partial(project_kernel, offsets, not state),
        out_shape=[jax.ShapeDtypeStruct(*shape) for shape in shapes],
        in_specs=[SMEM] + [VMEM] * (len(blocks) + 1) + [HBM] + [VMEM] * (len(state) + len(extra)),
        out_specs=[VMEM] * 2,
        scratch_shapes=[
            pltpu.VMEM((len(offsets), PAIR_COLS, width), jnp.bfloat16),
            pltpu.SemaphoreType.DMA((2 * len(offsets),)),
        ],
        compiler_params=pltpu.CompilerParams(vmem_limit_bytes=16 * MIB),
        cost_estimate=pl.CostEstimate(
            flops=2 * CHUNK * PAIR_COLS * width * len(offsets),
            bytes_accessed=2 * PAIR_COLS * width * len(offsets),
            transcendentals=0,
        ),
        name="norm_project",
    )(z.reshape(1), *blocks, gain, weights, *state, *extra)


def finish_kernel(offsets, place_ref, *refs):
    last = offsets == (4,)
    blocks, (total_ref, w_ref, *outs, w_vmem, sems) = take_blocks(offsets, refs)
    copies = []
    for i, offset in enumerate(offsets):
        source = (place_ref[1] + offset) & 7
        for j in (0, 1):
            at = (place_ref[1] - 2 * source - j) & 7
            at = at + N_Z * ((source >> 2) ^ place_ref[0])
            copies.append(
                pltpu.make_async_copy(w_ref.at[:, at], w_vmem.at[i, j], sems.at[len(copies)])
            )
            copies[-1].start()
    total = total_ref[...].astype(jnp.float32)
    for i, block in enumerate(blocks):
        for j in (0, 1):
            copies[2 * i + j].wait()
            total = total + jnp.dot(
                block[:, j * 2 * HEAD_DIM : (j + 1) * 2 * HEAD_DIM],
                w_vmem[i, j].reshape(2 * HEAD_DIM, PAIR_COLS),
                preferred_element_type=jnp.float32,
            )
    if not last:
        outs[0][...] = total
        return
    own_ref, other_ref = outs
    first, second = total[:, :COLS].astype(jnp.bfloat16), total[:, COLS:].astype(jnp.bfloat16)

    @pl.when(place_ref[0] == 0)
    def _():
        own_ref[...] = first
        other_ref[...] = second

    @pl.when(place_ref[0] == 1)
    def _():
        own_ref[...] = second
        other_ref[...] = first


def finish(place, mixed, weights, offsets, blocks, state):
    shapes = [jax.ShapeDtypeStruct((CHUNK, PAIR_COLS), jnp.float32)]
    if offsets == (4,):
        shapes = [jax.ShapeDtypeStruct((CHUNK, COLS), jnp.bfloat16)] * 2
    return pl.pallas_call(
        functools.partial(finish_kernel, offsets),
        out_shape=shapes,
        in_specs=[SMEM] + [VMEM] * (len(blocks) + 1) + [HBM],
        out_specs=[VMEM] * len(shapes),
        scratch_shapes=[
            pltpu.VMEM((len(offsets), 2, N_CTX, weights.shape[2], PAIR_COLS), jnp.bfloat16),
            pltpu.SemaphoreType.DMA((2 * len(offsets),)),
        ],
        compiler_params=pltpu.CompilerParams(vmem_limit_bytes=16 * MIB),
        cost_estimate=pl.CostEstimate(
            flops=2 * CHUNK * PAIR_COLS * 4 * HEAD_DIM * len(offsets),
            bytes_accessed=8 * PAIR_COLS * HEAD_DIM * len(offsets),
            transcendentals=0,
        ),
        name="project_out",
    )(place, *blocks, *(state or (mixed,)), weights)


def in_order(first, own, other, axis):
    return jnp.where(
        first, jnp.concatenate([own, other], axis=axis), jnp.concatenate([other, own], axis=axis)
    )


def per_device(
    residual,
    global_q,
    global_k,
    global_v,
    global_wo,
    norm_gain,
    stretch_wq,
    stretch_wk,
    stretch_wv,
    stretch_wo,
):
    me = lax.axis_index("ctx")
    place = lax.axis_index("tp")
    y_lo, z = place // N_Z, place % N_Z
    lower = y_lo == 0
    core = me & 1

    place_pair = jnp.stack([y_lo, z]).astype(jnp.int32)

    class_kv = gather_class(take_kv(place // 2, global_k, global_v))
    ctx_order = [2 * k + side for side in (core, 1 - core) for k in range(N_CTX // 2)]
    slots = [slot for c in ctx_order for slot in (c, 2 * N_CTX - 1 - c)]
    limits = jnp.where(lower, me + 1, 2 * N_CTX - me), jnp.where(lower, 2 * N_CTX - me, me + 1)
    ends = limits[0], y_lo * CHUNK, limits[1], (1 - y_lo) * CHUNK
    meta = jnp.stack([*slots, *ends]).astype(jnp.int32)

    first_weights, mine_a, mine_b = arrange(
        z, jnp.int32(0), core, global_wo, global_wo.shape[0]
    )
    rows = stretch_wo.shape[0] // N_CTX
    (share,) = arrange(z, me * rows, None, stretch_wo, rows)
    share = share.reshape(2, 2, 2, rows, PAIR_COLS)
    residual_kept, residual_given = split(place_pair, residual)
    own_wq, mine_a, came = together(
        permute(stretch_wq, "tp", lambda t: 8 * (t % 2) + t // 2),
        to_other_y_lo(mine_a),
        along_z(share[:, :, 1], 1),
    )
    share = jnp.stack([share[:, :, 0], came], axis=2)
    other_wq, mine_b, came = together(
        to_other_y_lo(own_wq), to_other_y_lo(mine_b), along_z(share[:, 1], 2)
    )
    share = jnp.stack([share[:, 0], came], axis=1)
    weights = pack(place_pair, stretch_wk, stretch_wv, own_wq, other_wq)
    other_a, other_b, residual_came, came, weights = together(
        to_other_core(mine_a),
        to_other_core(mine_b),
        to_other_y_lo(residual_given),
        along_z(share[1], 4),
        weights,
    )
    share = jnp.stack([share[0], came], axis=0).reshape(N_Z, rows, PAIR_COLS)
    share = jnp.concatenate([share, to_other_y_lo(share)], axis=0)

    weights, share, _ = together(weights, share, class_kv[0, :16, :HEAD_DIM])
    gathered_weights = lax.all_gather(weights, "ctx", axis=0, tiled=False)
    last_weights = lax.all_gather(share, "ctx", axis=0, tiled=False)

    kept, given = attend(
        meta,
        global_q,
        [class_kv, to_other_core(class_kv)],
        2 * N_CTX,
        ((0, 1), (0, 1)),
        8,
        2,
        "attend_all",
        other_a,
        residual_came,
    )
    parts = first_weights, mine_a, mine_b, other_a, other_b
    operands = core, kept, to_other_y_lo(given), parts
    mixed, again = ring_reduce(operands, place_pair, (residual_kept, residual_came))

    gain = norm_gain.reshape(2, N_Z, COLS).transpose(1, 0, 2).reshape(N_Z, PAIR_COLS)
    gain = lax.dynamic_slice_in_dim(jnp.concatenate([gain, gain], axis=0), z, N_Z, 0)
    chunk = jnp.where(lower, me, 2 * N_CTX - 1 - me)
    positions = (chunk * CHUNK + jnp.arange(CHUNK, dtype=jnp.int32)).astype(jnp.float32)
    half_dim = HEAD_DIM // 2
    inv_freq = rope_base ** (-(jnp.arange(half_dim).astype(jnp.float32) * 2.0 / HEAD_DIM))
    angles = positions[:, None] * inv_freq[None, :]
    cosine, sine = jnp.cos(angles), jnp.sin(angles)
    rotation = (
        jnp.concatenate([cosine, cosine], axis=1),
        jnp.concatenate([-sine, sine], axis=1),
    )
    work = functools.partial(project, z, gain, gathered_weights, rotation)
    stretch_q, stretch_kv = work(*ring_gather(mixed, again, work))
    pieces = gather_ctx(stretch_kv)
    slots = [jnp.where(lower, c, N_CTX - 1 - c) for c in owners()]
    limit = jnp.where(lower, me + 1, N_CTX - me)
    meta = jnp.stack(slots + [limit, 0]).astype(jnp.int32)
    (attended,) = attend(
        meta, stretch_q, pieces, N_CTX, ((0, 1, 2, 3),), 8, 4, "attend_window"
    )
    work = functools.partial(finish, place_pair, mixed, last_weights)
    own, other = work(*ring_gather(attended, attended, work))
    return in_order(lower, own, to_other_y_lo(other), 0)


def solution(mesh):
    in_specs = (
        P("ctx", "tp"),
        P("ctx", "tp"),
        P("ctx", None),
        P("ctx", None),
        P("tp", None),
        P(),
        P("ctx", "tp"),
        P("ctx", None),
        P("ctx", None),
        P("tp", None),
    )
    return jax.shard_map(
        per_device, mesh=mesh, in_specs=in_specs, out_specs=P("ctx", "tp"), check_vma=False
    )
```

```python
import functools

import jax
import jax.numpy as jnp
from jax import lax
from jax.experimental import pallas as pl
from jax.experimental.pallas import tpu as pltpu
from jax.sharding import PartitionSpec as P

HEAD_DIM = 128
GROUP = 4
CHUNK = 256
N_CTX = 16
N_Z = 8
COLS = 320
PAIR_COLS = 2 * COLS
rope_base = 500000.0
norm_eps = 1e-05
masked_score = -1e30
scale_log2 = 1.4426950408889634 * HEAD_DIM**-0.5
MIB = 1024 * 1024
SMEM = pl.BlockSpec(memory_space=pltpu.SMEM)
VMEM = pl.BlockSpec(memory_space=pltpu.VMEM)
HBM = pl.BlockSpec(memory_space=pltpu.HBM)


def permute(value, axis, target):
    return lax.ppermute(value, axis, [(place, target(place)) for place in range(16)])


def to_other_core(value):
    return permute(value, "ctx", lambda c: c ^ 1)


def to_other_y_hi(value):
    return permute(value, "ctx", lambda c: c ^ 8)


def along_x(value, step):
    return permute(value, "ctx", lambda c: (c & 9) | ((c + 2 * step) & 6))


def to_other_y_lo(value):
    return permute(value, "tp", lambda t: t ^ 8)


def along_z(value, step):
    return permute(value, "tp", lambda t: (t & 8) | ((t + step) & 7))


def together_kernel(*refs):
    pass


def together(*values):
    return pl.pallas_call(
        together_kernel,
        out_shape=[jax.ShapeDtypeStruct(value.shape, value.dtype) for value in values],
        in_specs=[HBM] * len(values),
        out_specs=[HBM] * len(values),
        input_output_aliases={i: i for i in range(len(values))},
        compiler_params=pltpu.CompilerParams(vmem_limit_bytes=MIB),
        name="together",
    )(*values)


def arrange_kernel(row_count, place_ref, source, *rest):
    outs, (rows, sem) = rest[:-2], rest[-2:]
    first = pl.multiple_of(place_ref[1], 16)
    copy = pltpu.make_async_copy(source.at[pl.ds(first, row_count)], rows, sem)
    copy.start()
    copy.wait()
    for z in range(N_Z):
        offset = (z - place_ref[0]) & 7
        for y_lo in (0, 1):
            at = (y_lo * N_Z + z) * COLS
            outs[0][offset, :, y_lo * COLS : (y_lo + 1) * COLS] = rows[:, at : at + COLS]
    for i, out in enumerate(outs[1:]):
        count, height = out.shape[:2]
        half = pl.ds(pl.multiple_of(place_ref[2], height), height)
        out[...] = outs[0][i * count : (i + 1) * count, half, :]


def arrange(z, first, half, weights, row_count):
    shapes = [jax.ShapeDtypeStruct((N_Z, row_count, PAIR_COLS), jnp.bfloat16)]
    place = [z, first]
    if half is not None:
        shapes += [
            jax.ShapeDtypeStruct((N_Z // 2, row_count // 2, PAIR_COLS), jnp.bfloat16)
        ] * 2
        place.append(half * (row_count // 2))
    return pl.pallas_call(
        functools.partial(arrange_kernel, row_count),
        out_shape=shapes,
        in_specs=[SMEM, HBM],
        out_specs=[VMEM] * len(shapes),
        scratch_shapes=[
            pltpu.VMEM((row_count, weights.shape[1]), jnp.bfloat16),
            pltpu.SemaphoreType.DMA,
        ],
        compiler_params=pltpu.CompilerParams(vmem_limit_bytes=20 * MIB),
        name="arrange",
    )(jnp.stack(place).astype(jnp.int32), weights)


def pack_kernel(place_ref, k_ref, v_ref, own_ref, other_ref, out_ref, sems):
    def columns(first, width):
        return pl.ds(pl.multiple_of(first, HEAD_DIM), width)

    wide = own_ref.shape[1]
    head = columns(place_ref[1] * HEAD_DIM, HEAD_DIM)
    moves = (
        (own_ref, columns(place_ref[0] * wide, wide)),
        (other_ref, columns((1 - place_ref[0]) * wide, wide)),
        (k_ref.at[:, head], pl.ds(2 * wide, HEAD_DIM)),
        (v_ref.at[:, head], pl.ds(2 * wide + HEAD_DIM, HEAD_DIM)),
    )
    copies = [
        pltpu.make_async_copy(source, out_ref.at[:, target], sems.at[i])
        for i, (source, target) in enumerate(moves)
    ]
    for copy in copies:
        copy.start()
    for copy in copies:
        copy.wait()


def pack(place, keys, values, own, other):
    rows, wide = own.shape
    return pl.pallas_call(
        pack_kernel,
        out_shape=jax.ShapeDtypeStruct((rows, 2 * (wide + HEAD_DIM)), jnp.bfloat16),
        in_specs=[SMEM] + [HBM] * 4,
        out_specs=HBM,
        scratch_shapes=[pltpu.SemaphoreType.DMA((4,))],
        compiler_params=pltpu.CompilerParams(vmem_limit_bytes=MIB),
        name="pack",
    )(place, keys, values, own, other)


def split_kernel(place_ref, value_ref, *rest):
    outs, sems = rest[-3:-1], rest[-1]
    copies = []
    for i, half in enumerate((place_ref[0], 1 - place_ref[0])):
        rows = pl.ds(pl.multiple_of(half * CHUNK, CHUNK), CHUNK)
        copies.append(pltpu.make_async_copy(value_ref.at[rows], outs[i], sems.at[i]))
        copies[-1].start()
    for copy in copies:
        copy.wait()


def split(place, value):
    half = jax.ShapeDtypeStruct((CHUNK, value.shape[1]), value.dtype)
    return pl.pallas_call(
        split_kernel,
        out_shape=(half, half),
        in_specs=[SMEM, HBM],
        out_specs=(VMEM, VMEM),
        scratch_shapes=[pltpu.SemaphoreType.DMA((2,))],
        compiler_params=pltpu.CompilerParams(vmem_limit_bytes=MIB),
        name="split",
    )(place, value)


def own_terms(offsets, core_ref, kept_ref, received_ref, weights, others, refs):
    buffer, landing, sems = refs
    half = CHUNK // 2
    copies = []
    for i, offset in enumerate(offsets):
        late, at = offset // 4, offset % 4
        sources = weights[0].at[offset], weights[1 + late].at[at], weights[3 + late].at[at]
        for j, (first, rows) in enumerate(((0, CHUNK), (CHUNK, half), (CHUNK + half, half))):
            target = buffer.at[i, pl.ds(first, rows)]
            copies.append(pltpu.make_async_copy(sources[j], target, sems.at[3 * i + j]))
            copies[-1].start()
    landed = []
    for i, other in enumerate(others):
        target = landing.at[i, pl.ds(0, other.shape[0]), pl.ds(0, other.shape[1])]
        copies.append(pltpu.make_async_copy(other, target, sems.at[len(copies)]))
        copies[-1].start()
    received = received_ref[...]
    low, high = received[:, :half], received[:, half:]
    first = jnp.full(low.shape, core_ref[0], jnp.int32) == 0
    rows = jnp.concatenate(
        [kept_ref[...], jnp.where(first, low, high), jnp.where(first, high, low)], axis=1
    )
    for copy in copies:
        copy.wait()
    for i, other in enumerate(others):
        landed.append(landing[i, : other.shape[0]].astype(jnp.float32))
    parts = [
        jnp.dot(rows, buffer[i], preferred_element_type=jnp.float32) for i in range(len(offsets))
    ]
    return parts, landed


def terms_kernel(offsets, core_ref, kept_ref, received_ref, *refs):
    weights, (*outs, buffer, landing, sems) = refs[:5], refs[5:]
    scratch = buffer, landing, sems
    parts, _ = own_terms(offsets, core_ref, kept_ref, received_ref, weights, (), scratch)
    if offsets == (4,):
        parts = parts[0][: CHUNK // 2], parts[0][CHUNK // 2 :]
    for part, out in zip(parts, outs):
        out[...] = part.astype(jnp.bfloat16)


def hop_kernel(up_ref, down_ref, up_term_ref, down_term_ref, up_out_ref, down_out_ref):
    came = up_ref.shape[0]
    rest = CHUNK - came
    up, down = up_term_ref[:came].astype(jnp.float32), down_term_ref[rest:].astype(jnp.float32)
    up_out_ref[:came] = (up + up_ref[...].astype(jnp.float32)).astype(jnp.bfloat16)
    down_out_ref[rest:] = (down + down_ref[...].astype(jnp.float32)).astype(jnp.bfloat16)
    if rest:
        up_out_ref[came:] = up_term_ref[came:]
        down_out_ref[:rest] = down_term_ref[:rest]


def mix_kernel(up_ref, down_ref, term_ref, place_ref, *refs):
    *residual, out_ref, again_ref = refs
    total = sum(ref[...].astype(jnp.float32) for ref in (up_ref, down_ref, term_ref))

    def put(first, second):
        out_ref[:, :COLS] = (total[:, :COLS] + first[...].astype(jnp.float32)).astype(jnp.bfloat16)
        out_ref[:, COLS:] = (total[:, COLS:] + second[...].astype(jnp.float32)).astype(jnp.bfloat16)

    pl.when(place_ref[0] == 0)(lambda: put(*residual))
    pl.when(place_ref[0] == 1)(lambda: put(*residual[::-1]))
    again_ref[...] = out_ref[...]


def terms(offsets, core, kept, received, weights):
    count = len(offsets)
    shapes = [(CHUNK, PAIR_COLS)] * count if offsets != (4,) else [(CHUNK // 2, PAIR_COLS)] * 2
    return pl.pallas_call(
        functools.partial(terms_kernel, offsets),
        out_shape=[jax.ShapeDtypeStruct(shape, jnp.bfloat16) for shape in shapes],
        in_specs=[SMEM, VMEM, VMEM] + [HBM] * 5,
        out_specs=[VMEM] * len(shapes),
        scratch_shapes=[
            pltpu.VMEM((count, 2 * CHUNK, PAIR_COLS), jnp.bfloat16),
            pltpu.VMEM((1, 16, 128), jnp.bfloat16),
            pltpu.SemaphoreType.DMA((3 * count,)),
        ],
        compiler_params=pltpu.CompilerParams(vmem_limit_bytes=24 * MIB),
        name="terms",
    )(core.reshape(1), kept, received, *weights)


def ring_step(kernel, name, *operands):
    specs = [SMEM if operand.ndim == 1 else VMEM for operand in operands]
    return pl.pallas_call(
        kernel,
        out_shape=[jax.ShapeDtypeStruct((CHUNK, PAIR_COLS), jnp.bfloat16)] * 2,
        in_specs=specs,
        out_specs=[VMEM] * 2,
        compiler_params=pltpu.CompilerParams(vmem_limit_bytes=8 * MIB),
        name=name,
    )(*operands)


def ring_reduce(operands, place, residual):
    up, down = terms((4,), *operands)
    up, down = along_z(up, 1), along_z(down, -1)
    offsets = (3, 5, 2, 6, 1, 7, 0)
    term = dict(zip(offsets, terms(offsets, *operands)))
    for hop in (3, 2, 1):
        up, down = ring_step(hop_kernel, "hop", up, down, term[hop], term[N_Z - hop])
        up, down = along_z(up, 1), along_z(down, -1)
    return ring_step(mix_kernel, "mix", up, down, term[0], place, *residual)


GATHER_OFFSETS = [
    (dy, dx, core)
    for core in (0, 1)
    for dy, dx in ((0, 0), (1, 0), (0, 3), (0, 1), (0, 2), (1, 3), (1, 1), (1, 2))
]


def gather_ctx(block):
    other = to_other_y_hi(block)
    left, right = along_x(block, 1), along_x(block, -1)
    far = along_x(left, 1)
    left_other, right_other = along_x(other, 1), along_x(other, -1)
    far_other = along_x(right_other, -1)
    mine = [block, other, left, right, far, left_other, right_other, far_other]
    return mine + [
        to_other_core(jnp.stack(mine[:4])),
        to_other_core(jnp.stack(mine[4:7])),
        to_other_core(far_other),
    ]


CLASSES = [list(range(0, N_CTX, 2)), list(range(1, N_CTX, 2))]


def gather_class(block):
    return lax.all_gather(block, "ctx", axis=0, tiled=False, axis_index_groups=CLASSES)


def owners():
    me = lax.axis_index("ctx")
    return [
        ((me & 8) ^ (8 * dy)) | ((me + 2 * dx) & 6) | ((me & 1) ^ dc)
        for dy, dx, dc in GATHER_OFFSETS
    ]


def take_kernel(place_ref, k_ref, v_ref, out_ref, sems):
    columns = pl.ds(pl.multiple_of(place_ref[0] * HEAD_DIM, HEAD_DIM), HEAD_DIM)
    copies = [
        pltpu.make_async_copy(src.at[:, columns], out_ref.at[:, pl.ds(i * HEAD_DIM, HEAD_DIM)], sems.at[i])
        for i, src in enumerate((k_ref, v_ref))
    ]
    for copy in copies:
        copy.start()
    for copy in copies:
        copy.wait()


def take_kv(place, keys, values):
    rows = keys.shape[0]
    return pl.pallas_call(
        take_kernel,
        out_shape=jax.ShapeDtypeStruct((rows, 2 * HEAD_DIM), jnp.bfloat16),
        in_specs=[SMEM, HBM, HBM],
        out_specs=VMEM,
        scratch_shapes=[pltpu.SemaphoreType.DMA((2,))],
        compiler_params=pltpu.CompilerParams(vmem_limit_bytes=60 * MIB),
        name="take_kv",
    )(place.reshape(1), keys, values)


def attend_kernel(tiles, tile_chunks, chains, earlier, meta_ref, q_ref, *rest):
    pieces, outs, (kv, sems) = rest[: -2 - len(tiles) - earlier], rest[-2 - len(tiles) : -2], rest[-2:]
    blocks = []
    for piece in pieces:
        blocks += [piece] if len(piece.shape) == 2 else [piece.at[b] for b in range(piece.shape[0])]
    copies = []
    for block in blocks:
        for part in range(block.shape[0] // CHUNK):
            source = block.at[pl.ds(part * CHUNK, CHUNK)]
            copies.append(
                pltpu.make_async_copy(source, kv.at[meta_ref[len(copies)]], sems.at[len(copies)])
            )
            copies[-1].start()
    for copy in copies:
        copy.wait()
    span = tile_chunks * CHUNK
    for tile, (heads, out_ref) in enumerate(zip(tiles, outs)):
        limit = meta_ref[len(copies) + 2 * tile]
        first = pl.multiple_of(meta_ref[len(copies) + 2 * tile + 1], CHUNK)
        rows = q_ref.at[pl.ds(first, CHUNK)]
        each = len(heads) // chains
        queries = [
            jnp.concatenate(
                [rows[:, h * HEAD_DIM : (h + 1) * HEAD_DIM] for h in heads[g * each : (g + 1) * each]],
                axis=0,
            )
            for g in range(chains)
        ]
        height = each * CHUNK

        def step(i, state, masked):
            here = pl.ds(i * tile_chunks, tile_chunks)
            keys = kv[here, :, :HEAD_DIM].reshape(span, HEAD_DIM)
            values = kv[here, :, HEAD_DIM:].reshape(span, HEAD_DIM)
            values = jnp.concatenate([values, jnp.ones(values.shape, values.dtype)], axis=1)
            if masked:
                column = lax.broadcasted_iota(jnp.int32, (height, span), 1) + i * span
                row = lax.broadcasted_iota(jnp.int32, (height, span), 0) % CHUNK
                visible = column <= row + (limit - 1) * CHUNK
            scores = [
                lax.dot_general(
                    query, keys, (((1,), (1,)), ((), ())), preferred_element_type=jnp.float32
                )
                for query in queries
            ]
            after = []
            for score, (highest, weighted) in zip(scores, state):
                if masked:
                    score = jnp.where(visible, score, masked_score)
                new_high = jnp.maximum(highest, jnp.max(score, axis=1, keepdims=True))
                fade = jnp.exp2((highest - new_high) * scale_log2)
                scores_here = score * scale_log2 - new_high * scale_log2
                weights = jnp.exp2(scores_here).astype(jnp.bfloat16)
                weighted = weighted * fade + jnp.dot(
                    weights, values, preferred_element_type=jnp.float32
                )
                after.append((new_high, weighted))
            return tuple(after)

        state = tuple(
            (
                jnp.full((height, 1), masked_score, jnp.float32),
                jnp.zeros((height, 2 * HEAD_DIM), jnp.float32),
            )
            for _ in range(chains)
        )
        whole = lax.div(limit - 1, jnp.int32(tile_chunks))
        state = lax.fori_loop(0, whole, functools.partial(step, masked=False), state)
        state = step(whole, state, True)
        for g, (_, weighted) in enumerate(state):
            result = (weighted[:, :HEAD_DIM] / weighted[:, HEAD_DIM:]).astype(jnp.bfloat16)
            for j in range(each):
                h = heads[g * each + j]
                out_ref[:, h * HEAD_DIM : (h + 1) * HEAD_DIM] = result[
                    j * CHUNK : (j + 1) * CHUNK
                ]


def attend(meta, queries, pieces, chunks, tiles, tile_chunks, chains, name, *earlier):
    return pl.pallas_call(
        functools.partial(attend_kernel, tiles, tile_chunks, chains, len(earlier)),
        out_shape=[jax.ShapeDtypeStruct((CHUNK, queries.shape[1]), jnp.bfloat16)] * len(tiles),
        in_specs=[SMEM, VMEM] + [HBM] * (len(pieces) + len(earlier)),
        out_specs=[VMEM] * len(tiles),
        scratch_shapes=[
            pltpu.VMEM((chunks, CHUNK, 2 * HEAD_DIM), jnp.bfloat16),
            pltpu.SemaphoreType.DMA((chunks,)),
        ],
        compiler_params=pltpu.CompilerParams(vmem_limit_bytes=32 * MIB),
        cost_estimate=pl.CostEstimate(
            flops=2_200_000_000, bytes_accessed=5_000_000, transcendentals=10_000_000
        ),
        name=name,
    )(meta, queries, *pieces, *earlier)


def ring_gather(block, again, work, first_hop):
    half = block.shape[0] // 2
    below, above = block, again
    offsets, blocks, state = (0,), (block,), ()
    if first_hop == 2:
        below, above = along_z(block, 1), along_z(again, -1)
        offsets, blocks = (0, 1, 7), (block, above, below)
    for hop in range(first_hop, 5):
        if hop == 4:
            below, above = below[:half], above[half:]
        below, above = along_z(below, 1), along_z(above, -1)
        below, above, *state = together(below, above, *work(offsets, blocks, state))
        offsets, blocks = (hop, 8 - hop), (above, below)
    return (4,), (below, above), state


def rope(value, cosine, sine):
    return value * cosine + pltpu.roll(value, HEAD_DIM // 2, axis=1) * sine


def take_blocks(offsets, refs):
    if offsets == (4,):
        return [jnp.concatenate([refs[0][...], refs[1][...]], axis=0)], refs[2:]
    return [ref[...] for ref in refs[: len(offsets)]], refs[len(offsets) :]


def project_kernel(offsets, first, z_ref, *refs):
    last = offsets == (4,)
    blocks, (gain_ref, w_ref, *refs) = take_blocks(offsets, refs)
    w_vmem, sems = refs[-2:]
    copies = []
    for i, offset in enumerate(offsets):
        source = (z_ref[0] + offset) & 7
        for y_lo in (0, 1):
            rows = pl.ds(y_lo * COLS, COLS)
            copies.append(
                pltpu.make_async_copy(
                    w_ref.at[y_lo * N_Z + source], w_vmem.at[i, rows], sems.at[len(copies)]
                )
            )
            copies[-1].start()
    if first:
        squares, total = jnp.zeros((CHUNK, 128), jnp.float32), None
    else:
        squares, total = refs[0][...], refs[1][...]
    for i, (offset, block) in enumerate(zip(offsets, blocks)):
        wide = block.astype(jnp.float32)
        for at in range(0, PAIR_COLS, 128):
            squares = squares + wide[:, at : at + 128] * wide[:, at : at + 128]
        scaled = (wide * gain_ref[offset : offset + 1]).astype(jnp.bfloat16)
        copies[2 * i].wait()
        copies[2 * i + 1].wait()
        part = jnp.dot(scaled, w_vmem[i], preferred_element_type=jnp.float32)
        total = part if total is None else total + part
    if not last:
        squares_ref, total_ref = refs[-4:-2]
        squares_ref[...], total_ref[...] = squares, total
        return
    cos_ref, sin_ref, q_ref, kv_ref = refs[2:6]
    mean = jnp.sum(squares, axis=1, keepdims=True) / (16 * COLS)
    total = total * lax.rsqrt(mean + norm_eps)
    cosine, sine = cos_ref[...], sin_ref[...]
    for h in range(GROUP):
        at = slice(h * HEAD_DIM, (h + 1) * HEAD_DIM)
        q_ref[:, at] = rope(total[:, at], cosine, sine).astype(jnp.bfloat16)
    at = GROUP * HEAD_DIM
    kv_ref[:, :HEAD_DIM] = rope(total[:, at : at + HEAD_DIM], cosine, sine).astype(jnp.bfloat16)
    kv_ref[:, HEAD_DIM:] = total[:, at + HEAD_DIM :].astype(jnp.bfloat16)


def project(z, gain, weights, rotation, offsets, blocks, state):
    width = weights.shape[2]
    shapes = ((CHUNK, 128), jnp.float32), ((CHUNK, width), jnp.float32)
    extra = ()
    if offsets == (4,):
        shapes = ((CHUNK, GROUP * HEAD_DIM), jnp.bfloat16), ((CHUNK, 2 * HEAD_DIM), jnp.bfloat16)
        extra = rotation
    return pl.pallas_call(
        functools.partial(project_kernel, offsets, not state),
        out_shape=[jax.ShapeDtypeStruct(*shape) for shape in shapes],
        in_specs=[SMEM] + [VMEM] * (len(blocks) + 1) + [HBM] + [VMEM] * (len(state) + len(extra)),
        out_specs=[VMEM] * 2,
        scratch_shapes=[
            pltpu.VMEM((len(offsets), PAIR_COLS, width), jnp.bfloat16),
            pltpu.SemaphoreType.DMA((2 * len(offsets),)),
        ],
        compiler_params=pltpu.CompilerParams(vmem_limit_bytes=16 * MIB),
        cost_estimate=pl.CostEstimate(
            flops=2 * CHUNK * PAIR_COLS * width * len(offsets),
            bytes_accessed=2 * PAIR_COLS * width * len(offsets),
            transcendentals=0,
        ),
        name="norm_project",
    )(z.reshape(1), *blocks, gain, weights, *state, *extra)


def finish_kernel(offsets, place_ref, *refs):
    last = offsets == (4,)
    blocks, (total_ref, w_ref, *outs, w_vmem, sems) = take_blocks(offsets, refs)
    copies = []
    for i, offset in enumerate(offsets):
        source = (place_ref[1] + offset) & 7
        for j in (0, 1):
            at = (place_ref[1] - 2 * source - j) & 7
            at = at + N_Z * ((source >> 2) ^ place_ref[0])
            copies.append(
                pltpu.make_async_copy(w_ref.at[:, at], w_vmem.at[i, j], sems.at[len(copies)])
            )
            copies[-1].start()
    total = total_ref[...].astype(jnp.float32)
    for i, block in enumerate(blocks):
        for j in (0, 1):
            copies[2 * i + j].wait()
            total = total + jnp.dot(
                block[:, j * 2 * HEAD_DIM : (j + 1) * 2 * HEAD_DIM],
                w_vmem[i, j].reshape(2 * HEAD_DIM, PAIR_COLS),
                preferred_element_type=jnp.float32,
            )
    if not last:
        outs[0][...] = total
        return
    own_ref, other_ref = outs
    first, second = total[:, :COLS].astype(jnp.bfloat16), total[:, COLS:].astype(jnp.bfloat16)

    @pl.when(place_ref[0] == 0)
    def _():
        own_ref[...] = first
        other_ref[...] = second

    @pl.when(place_ref[0] == 1)
    def _():
        own_ref[...] = second
        other_ref[...] = first


def finish(place, mixed, weights, offsets, blocks, state):
    shapes = [jax.ShapeDtypeStruct((CHUNK, PAIR_COLS), jnp.float32)]
    if offsets == (4,):
        shapes = [jax.ShapeDtypeStruct((CHUNK, COLS), jnp.bfloat16)] * 2
    return pl.pallas_call(
        functools.partial(finish_kernel, offsets),
        out_shape=shapes,
        in_specs=[SMEM] + [VMEM] * (len(blocks) + 1) + [HBM],
        out_specs=[VMEM] * len(shapes),
        scratch_shapes=[
            pltpu.VMEM((len(offsets), 2, N_CTX, weights.shape[2], PAIR_COLS), jnp.bfloat16),
            pltpu.SemaphoreType.DMA((2 * len(offsets),)),
        ],
        compiler_params=pltpu.CompilerParams(vmem_limit_bytes=16 * MIB),
        cost_estimate=pl.CostEstimate(
            flops=2 * CHUNK * PAIR_COLS * 4 * HEAD_DIM * len(offsets),
            bytes_accessed=8 * PAIR_COLS * HEAD_DIM * len(offsets),
            transcendentals=0,
        ),
        name="project_out",
    )(place, *blocks, *(state or (mixed,)), weights)


def in_order(first, own, other, axis):
    return jnp.where(
        first, jnp.concatenate([own, other], axis=axis), jnp.concatenate([other, own], axis=axis)
    )


def per_device(
    residual,
    global_q,
    global_k,
    global_v,
    global_wo,
    norm_gain,
    stretch_wq,
    stretch_wk,
    stretch_wv,
    stretch_wo,
):
    me = lax.axis_index("ctx")
    place = lax.axis_index("tp")
    y_lo, z = place // N_Z, place % N_Z
    lower = y_lo == 0
    core = me & 1

    place_pair = jnp.stack([y_lo, z]).astype(jnp.int32)

    class_kv = gather_class(take_kv(place // 2, global_k, global_v))
    ctx_order = [2 * k + side for side in (core, 1 - core) for k in range(N_CTX // 2)]
    slots = [slot for c in ctx_order for slot in (c, 2 * N_CTX - 1 - c)]
    limits = jnp.where(lower, me + 1, 2 * N_CTX - me), jnp.where(lower, 2 * N_CTX - me, me + 1)
    ends = limits[0], y_lo * CHUNK, limits[1], (1 - y_lo) * CHUNK
    meta = jnp.stack([*slots, *ends]).astype(jnp.int32)

    first_weights, mine_a, mine_b = arrange(
        z, jnp.int32(0), core, global_wo, global_wo.shape[0]
    )
    rows = stretch_wo.shape[0] // N_CTX
    (share,) = arrange(z, me * rows, None, stretch_wo, rows)
    share = share.reshape(2, 2, 2, rows, PAIR_COLS)
    residual_kept, residual_given = split(place_pair, residual)
    own_wq, mine_a, came = together(
        permute(stretch_wq, "tp", lambda t: 8 * (t % 2) + t // 2),
        to_other_y_lo(mine_a),
        along_z(share[:, :, 1], 1),
    )
    share = jnp.stack([share[:, :, 0], came], axis=2)
    other_wq, mine_b, came = together(
        to_other_y_lo(own_wq), to_other_y_lo(mine_b), along_z(share[:, 1], 2)
    )
    share = jnp.stack([share[:, 0], came], axis=1)
    weights = pack(place_pair, stretch_wk, stretch_wv, own_wq, other_wq)
    other_a, other_b, residual_came, came, weights = together(
        to_other_core(mine_a),
        to_other_core(mine_b),
        to_other_y_lo(residual_given),
        along_z(share[1], 4),
        weights,
    )
    share = jnp.stack([share[0], came], axis=0).reshape(N_Z, rows, PAIR_COLS)
    share = jnp.concatenate([share, to_other_y_lo(share)], axis=0)

    weights, share, _ = together(weights, share, class_kv[0, :16, :HEAD_DIM])
    gathered_weights = lax.all_gather(weights, "ctx", axis=0, tiled=False)
    last_weights = lax.all_gather(share, "ctx", axis=0, tiled=False)

    kept, given = attend(
        meta,
        global_q,
        [class_kv, to_other_core(class_kv)],
        2 * N_CTX,
        ((0, 1), (0, 1)),
        8,
        2,
        "attend_all",
        other_a,
        residual_came,
    )
    parts = first_weights, mine_a, mine_b, other_a, other_b
    operands = core, kept, to_other_y_lo(given), parts
    mixed, again = ring_reduce(operands, place_pair, (residual_kept, residual_came))

    gain = norm_gain.reshape(2, N_Z, COLS).transpose(1, 0, 2).reshape(N_Z, PAIR_COLS)
    gain = lax.dynamic_slice_in_dim(jnp.concatenate([gain, gain], axis=0), z, N_Z, 0)
    chunk = jnp.where(lower, me, 2 * N_CTX - 1 - me)
    positions = (chunk * CHUNK + jnp.arange(CHUNK, dtype=jnp.int32)).astype(jnp.float32)
    half_dim = HEAD_DIM // 2
    inv_freq = rope_base ** (-(jnp.arange(half_dim).astype(jnp.float32) * 2.0 / HEAD_DIM))
    angles = positions[:, None] * inv_freq[None, :]
    cosine, sine = jnp.cos(angles), jnp.sin(angles)
    rotation = (
        jnp.concatenate([cosine, cosine], axis=1),
        jnp.concatenate([-sine, sine], axis=1),
    )
    work = functools.partial(project, z, gain, gathered_weights, rotation)
    stretch_q, stretch_kv = work(*ring_gather(mixed, again, work, 2))
    pieces = gather_ctx(stretch_kv)
    slots = [jnp.where(lower, c, N_CTX - 1 - c) for c in owners()]
    limit = jnp.where(lower, me + 1, N_CTX - me)
    meta = jnp.stack(slots + [limit, 0]).astype(jnp.int32)
    (attended,) = attend(
        meta, stretch_q, pieces, N_CTX, ((0, 1, 2, 3),), 8, 4, "attend_window"
    )
    work = functools.partial(finish, place_pair, mixed, last_weights)
    own, other = work(*ring_gather(attended, attended, work, 1))
    return in_order(lower, own, to_other_y_lo(other), 0)


def solution(mesh):
    in_specs = (
        P("ctx", "tp"),
        P("ctx", "tp"),
        P("ctx", None),
        P("ctx", None),
        P("tp", None),
        P(),
        P("ctx", "tp"),
        P("ctx", None),
        P("ctx", None),
        P("tp", None),
    )
    return jax.shard_map(
        per_device, mesh=mesh, in_specs=in_specs, out_specs=P("ctx", "tp"), check_vma=False
    )
```

```python
import functools

import jax
import jax.numpy as jnp
from jax import lax
from jax.experimental import pallas as pl
from jax.experimental.pallas import tpu as pltpu
from jax.sharding import PartitionSpec as P

HEAD_DIM = 128
GROUP = 4
CHUNK = 256
N_CTX = 16
N_Z = 8
COLS = 320
PAIR_COLS = 2 * COLS
rope_base = 500000.0
norm_eps = 1e-05
masked_score = -1e30
scale_log2 = 1.4426950408889634 * HEAD_DIM**-0.5
MIB = 1024 * 1024
SMEM = pl.BlockSpec(memory_space=pltpu.SMEM)
VMEM = pl.BlockSpec(memory_space=pltpu.VMEM)
HBM = pl.BlockSpec(memory_space=pltpu.HBM)


def permute(value, axis, target):
    return lax.ppermute(value, axis, [(place, target(place)) for place in range(16)])


def to_other_core(value):
    return permute(value, "ctx", lambda c: c ^ 1)


def to_other_y_hi(value):
    return permute(value, "ctx", lambda c: c ^ 8)


def along_x(value, step):
    return permute(value, "ctx", lambda c: (c & 9) | ((c + 2 * step) & 6))


def to_other_y_lo(value):
    return permute(value, "tp", lambda t: t ^ 8)


def along_z(value, step):
    return permute(value, "tp", lambda t: (t & 8) | ((t + step) & 7))


def together_kernel(*refs):
    pass


def together(*values):
    return pl.pallas_call(
        together_kernel,
        out_shape=[jax.ShapeDtypeStruct(value.shape, value.dtype) for value in values],
        in_specs=[HBM] * len(values),
        out_specs=[HBM] * len(values),
        input_output_aliases={i: i for i in range(len(values))},
        compiler_params=pltpu.CompilerParams(vmem_limit_bytes=MIB),
        name="together",
    )(*values)


def copy_kernel(source, out, sem):
    copy = pltpu.make_async_copy(source, out, sem)
    copy.start()
    copy.wait()


def in_vmem(value):
    return pl.pallas_call(
        copy_kernel,
        out_shape=jax.ShapeDtypeStruct(value.shape, value.dtype),
        in_specs=[HBM],
        out_specs=VMEM,
        scratch_shapes=[pltpu.SemaphoreType.DMA],
        compiler_params=pltpu.CompilerParams(vmem_limit_bytes=8 * MIB),
        name="in_vmem",
    )(value)


def arrange_kernel(row_count, place_ref, source, *rest):
    outs, (rows, sem) = rest[:-2], rest[-2:]
    first = pl.multiple_of(place_ref[1], 16)
    copy = pltpu.make_async_copy(source.at[pl.ds(first, row_count)], rows, sem)
    copy.start()
    copy.wait()
    for z in range(N_Z):
        offset = (z - place_ref[0]) & 7
        for y_lo in (0, 1):
            at = (y_lo * N_Z + z) * COLS
            outs[0][offset, :, y_lo * COLS : (y_lo + 1) * COLS] = rows[:, at : at + COLS]
    for i, out in enumerate(outs[1:]):
        count, height = out.shape[:2]
        half = pl.ds(pl.multiple_of(place_ref[2], height), height)
        out[...] = outs[0][i * count : (i + 1) * count, half, :]


def arrange(z, first, half, weights, row_count):
    shapes = [jax.ShapeDtypeStruct((N_Z, row_count, PAIR_COLS), jnp.bfloat16)]
    place = [z, first]
    if half is not None:
        shapes += [
            jax.ShapeDtypeStruct((N_Z // 2, row_count // 2, PAIR_COLS), jnp.bfloat16)
        ] * 2
        place.append(half * (row_count // 2))
    return pl.pallas_call(
        functools.partial(arrange_kernel, row_count),
        out_shape=shapes,
        in_specs=[SMEM, HBM],
        out_specs=[VMEM] * len(shapes),
        scratch_shapes=[
            pltpu.VMEM((row_count, weights.shape[1]), jnp.bfloat16),
            pltpu.SemaphoreType.DMA,
        ],
        compiler_params=pltpu.CompilerParams(vmem_limit_bytes=20 * MIB),
        name="arrange",
    )(jnp.stack(place).astype(jnp.int32), weights)


def pack_kernel(place_ref, k_ref, v_ref, own_ref, other_ref, out_ref, sems):
    def columns(first, width):
        return pl.ds(pl.multiple_of(first, HEAD_DIM), width)

    wide = own_ref.shape[1]
    head = columns(place_ref[1] * HEAD_DIM, HEAD_DIM)
    moves = (
        (own_ref, columns(place_ref[0] * wide, wide)),
        (other_ref, columns((1 - place_ref[0]) * wide, wide)),
        (k_ref.at[:, head], pl.ds(2 * wide, HEAD_DIM)),
        (v_ref.at[:, head], pl.ds(2 * wide + HEAD_DIM, HEAD_DIM)),
    )
    copies = [
        pltpu.make_async_copy(source, out_ref.at[:, target], sems.at[i])
        for i, (source, target) in enumerate(moves)
    ]
    for copy in copies:
        copy.start()
    for copy in copies:
        copy.wait()


def pack(place, keys, values, own, other):
    rows, wide = own.shape
    return pl.pallas_call(
        pack_kernel,
        out_shape=jax.ShapeDtypeStruct((rows, 2 * (wide + HEAD_DIM)), jnp.bfloat16),
        in_specs=[SMEM] + [HBM] * 4,
        out_specs=HBM,
        scratch_shapes=[pltpu.SemaphoreType.DMA((4,))],
        compiler_params=pltpu.CompilerParams(vmem_limit_bytes=MIB),
        name="pack",
    )(place, keys, values, own, other)


def split_kernel(place_ref, value_ref, *rest):
    outs, sems = rest[-3:-1], rest[-1]
    copies = []
    for i, half in enumerate((place_ref[0], 1 - place_ref[0])):
        rows = pl.ds(pl.multiple_of(half * CHUNK, CHUNK), CHUNK)
        copies.append(pltpu.make_async_copy(value_ref.at[rows], outs[i], sems.at[i]))
        copies[-1].start()
    for copy in copies:
        copy.wait()


def split(place, value):
    half = jax.ShapeDtypeStruct((CHUNK, value.shape[1]), value.dtype)
    return pl.pallas_call(
        split_kernel,
        out_shape=(half, half),
        in_specs=[SMEM, HBM],
        out_specs=(VMEM, VMEM),
        scratch_shapes=[pltpu.SemaphoreType.DMA((2,))],
        compiler_params=pltpu.CompilerParams(vmem_limit_bytes=MIB),
        name="split",
    )(place, value)


def own_terms(offsets, core_ref, kept_ref, received_ref, weights, others, refs):
    buffer, landing, sems = refs
    half = CHUNK // 2
    copies = []
    for i, offset in enumerate(offsets):
        late, at = offset // 4, offset % 4
        sources = weights[0].at[offset], weights[1 + late].at[at], weights[3 + late].at[at]
        for j, (first, rows) in enumerate(((0, CHUNK), (CHUNK, half), (CHUNK + half, half))):
            target = buffer.at[i, pl.ds(first, rows)]
            copies.append(pltpu.make_async_copy(sources[j], target, sems.at[3 * i + j]))
            copies[-1].start()
    landed = []
    for i, other in enumerate(others):
        target = landing.at[i, pl.ds(0, other.shape[0]), pl.ds(0, other.shape[1])]
        copies.append(pltpu.make_async_copy(other, target, sems.at[len(copies)]))
        copies[-1].start()
    received = received_ref[...]
    low, high = received[:, :half], received[:, half:]
    first = jnp.full(low.shape, core_ref[0], jnp.int32) == 0
    rows = jnp.concatenate(
        [kept_ref[...], jnp.where(first, low, high), jnp.where(first, high, low)], axis=1
    )
    for copy in copies:
        copy.wait()
    for i, other in enumerate(others):
        landed.append(landing[i, : other.shape[0]].astype(jnp.float32))
    parts = [
        jnp.dot(rows, buffer[i], preferred_element_type=jnp.float32) for i in range(len(offsets))
    ]
    return parts, landed


def terms_kernel(offsets, core_ref, kept_ref, received_ref, *refs):
    weights, (*outs, buffer, landing, sems) = refs[:5], refs[5:]
    scratch = buffer, landing, sems
    parts, _ = own_terms(offsets, core_ref, kept_ref, received_ref, weights, (), scratch)
    if offsets == (4,):
        parts = parts[0][: CHUNK // 2], parts[0][CHUNK // 2 :]
    for part, out in zip(parts, outs):
        out[...] = part.astype(jnp.bfloat16)


def hop_kernel(up_ref, down_ref, up_term_ref, down_term_ref, up_out_ref, down_out_ref):
    came = up_ref.shape[0]
    rest = CHUNK - came
    up, down = up_term_ref[:came].astype(jnp.float32), down_term_ref[rest:].astype(jnp.float32)
    up_out_ref[:came] = (up + up_ref[...].astype(jnp.float32)).astype(jnp.bfloat16)
    down_out_ref[rest:] = (down + down_ref[...].astype(jnp.float32)).astype(jnp.bfloat16)
    if rest:
        up_out_ref[came:] = up_term_ref[came:]
        down_out_ref[:rest] = down_term_ref[:rest]


def mix_kernel(up_ref, down_ref, term_ref, place_ref, *refs):
    *residual, out_ref, again_ref = refs
    total = sum(ref[...].astype(jnp.float32) for ref in (up_ref, down_ref, term_ref))

    def put(first, second):
        out_ref[:, :COLS] = (total[:, :COLS] + first[...].astype(jnp.float32)).astype(jnp.bfloat16)
        out_ref[:, COLS:] = (total[:, COLS:] + second[...].astype(jnp.float32)).astype(jnp.bfloat16)

    pl.when(place_ref[0] == 0)(lambda: put(*residual))
    pl.when(place_ref[0] == 1)(lambda: put(*residual[::-1]))
    again_ref[...] = out_ref[...]


def terms(offsets, core, kept, received, weights):
    count = len(offsets)
    shapes = [(CHUNK, PAIR_COLS)] * count if offsets != (4,) else [(CHUNK // 2, PAIR_COLS)] * 2
    return pl.pallas_call(
        functools.partial(terms_kernel, offsets),
        out_shape=[jax.ShapeDtypeStruct(shape, jnp.bfloat16) for shape in shapes],
        in_specs=[SMEM, VMEM, VMEM] + [HBM] * 5,
        out_specs=[VMEM] * len(shapes),
        scratch_shapes=[
            pltpu.VMEM((count, 2 * CHUNK, PAIR_COLS), jnp.bfloat16),
            pltpu.VMEM((1, 16, 128), jnp.bfloat16),
            pltpu.SemaphoreType.DMA((3 * count,)),
        ],
        compiler_params=pltpu.CompilerParams(vmem_limit_bytes=24 * MIB),
        name="terms",
    )(core.reshape(1), kept, received, *weights)


def ring_step(kernel, name, *operands):
    specs = [SMEM if operand.ndim == 1 else VMEM for operand in operands]
    return pl.pallas_call(
        kernel,
        out_shape=[jax.ShapeDtypeStruct((CHUNK, PAIR_COLS), jnp.bfloat16)] * 2,
        in_specs=specs,
        out_specs=[VMEM] * 2,
        compiler_params=pltpu.CompilerParams(vmem_limit_bytes=8 * MIB),
        name=name,
    )(*operands)


def ring_reduce(operands, place, residual):
    up, down = terms((4,), *operands)
    up, down = along_z(up, 1), along_z(down, -1)
    offsets = (3, 5, 2, 6, 1, 7, 0)
    term = dict(zip(offsets, terms(offsets, *operands)))
    for hop in (3, 2, 1):
        up, down = ring_step(hop_kernel, "hop", up, down, term[hop], term[N_Z - hop])
        up, down = along_z(up, 1), along_z(down, -1)
    return ring_step(mix_kernel, "mix", up, down, term[0], place, *residual)


GATHER_OFFSETS = [
    (dy, dx, core)
    for core in (0, 1)
    for dy, dx in ((0, 0), (1, 0), (0, 3), (0, 1), (0, 2), (1, 3), (1, 1), (1, 2))
]


def gather_ctx(block):
    other = to_other_y_hi(block)
    left, right = along_x(block, 1), along_x(block, -1)
    far = along_x(left, 1)
    left_other, right_other = along_x(other, 1), along_x(other, -1)
    far_other = along_x(right_other, -1)
    mine = [block, other, left, right, far, left_other, right_other, far_other]
    return mine + [
        to_other_core(jnp.stack(mine[:4])),
        to_other_core(jnp.stack(mine[4:7])),
        to_other_core(far_other),
    ]


CLASSES = [list(range(0, N_CTX, 2)), list(range(1, N_CTX, 2))]


def gather_class(block):
    return lax.all_gather(block, "ctx", axis=0, tiled=False, axis_index_groups=CLASSES)


def owners():
    me = lax.axis_index("ctx")
    return [
        ((me & 8) ^ (8 * dy)) | ((me + 2 * dx) & 6) | ((me & 1) ^ dc)
        for dy, dx, dc in GATHER_OFFSETS
    ]


def take_kernel(place_ref, k_ref, v_ref, out_ref, sems):
    columns = pl.ds(pl.multiple_of(place_ref[0] * HEAD_DIM, HEAD_DIM), HEAD_DIM)
    copies = [
        pltpu.make_async_copy(src.at[:, columns], out_ref.at[:, pl.ds(i * HEAD_DIM, HEAD_DIM)], sems.at[i])
        for i, src in enumerate((k_ref, v_ref))
    ]
    for copy in copies:
        copy.start()
    for copy in copies:
        copy.wait()


def take_kv(place, keys, values):
    rows = keys.shape[0]
    return pl.pallas_call(
        take_kernel,
        out_shape=jax.ShapeDtypeStruct((rows, 2 * HEAD_DIM), jnp.bfloat16),
        in_specs=[SMEM, HBM, HBM],
        out_specs=VMEM,
        scratch_shapes=[pltpu.SemaphoreType.DMA((2,))],
        compiler_params=pltpu.CompilerParams(vmem_limit_bytes=60 * MIB),
        name="take_kv",
    )(place.reshape(1), keys, values)


def attend_kernel(tiles, tile_chunks, chains, earlier, meta_ref, q_ref, *rest):
    pieces, outs, (kv, sems) = rest[: -2 - len(tiles) - earlier], rest[-2 - len(tiles) : -2], rest[-2:]
    blocks = []
    for piece in pieces:
        blocks += [piece] if len(piece.shape) == 2 else [piece.at[b] for b in range(piece.shape[0])]
    copies = []
    for block in blocks:
        for part in range(block.shape[0] // CHUNK):
            source = block.at[pl.ds(part * CHUNK, CHUNK)]
            copies.append(
                pltpu.make_async_copy(source, kv.at[meta_ref[len(copies)]], sems.at[len(copies)])
            )
            copies[-1].start()
    for copy in copies:
        copy.wait()
    span = tile_chunks * CHUNK
    for tile, (heads, out_ref) in enumerate(zip(tiles, outs)):
        limit = meta_ref[len(copies) + 2 * tile]
        first = pl.multiple_of(meta_ref[len(copies) + 2 * tile + 1], CHUNK)
        rows = q_ref.at[pl.ds(first, CHUNK)]
        each = len(heads) // chains
        queries = [
            jnp.concatenate(
                [rows[:, h * HEAD_DIM : (h + 1) * HEAD_DIM] for h in heads[g * each : (g + 1) * each]],
                axis=0,
            )
            for g in range(chains)
        ]
        height = each * CHUNK

        def step(i, state, masked):
            here = pl.ds(i * tile_chunks, tile_chunks)
            keys = kv[here, :, :HEAD_DIM].reshape(span, HEAD_DIM)
            values = kv[here, :, HEAD_DIM:].reshape(span, HEAD_DIM)
            values = jnp.concatenate([values, jnp.ones(values.shape, values.dtype)], axis=1)
            if masked:
                column = lax.broadcasted_iota(jnp.int32, (height, span), 1) + i * span
                row = lax.broadcasted_iota(jnp.int32, (height, span), 0) % CHUNK
                visible = column <= row + (limit - 1) * CHUNK
            scores = [
                lax.dot_general(
                    query, keys, (((1,), (1,)), ((), ())), preferred_element_type=jnp.float32
                )
                for query in queries
            ]
            after = []
            for score, (highest, weighted) in zip(scores, state):
                if masked:
                    score = jnp.where(visible, score, masked_score)
                new_high = jnp.maximum(highest, jnp.max(score, axis=1, keepdims=True))
                fade = jnp.exp2((highest - new_high) * scale_log2)
                scores_here = score * scale_log2 - new_high * scale_log2
                weights = jnp.exp2(scores_here).astype(jnp.bfloat16)
                weighted = weighted * fade + jnp.dot(
                    weights, values, preferred_element_type=jnp.float32
                )
                after.append((new_high, weighted))
            return tuple(after)

        state = tuple(
            (
                jnp.full((height, 1), masked_score, jnp.float32),
                jnp.zeros((height, 2 * HEAD_DIM), jnp.float32),
            )
            for _ in range(chains)
        )
        whole = lax.div(limit - 1, jnp.int32(tile_chunks))
        state = lax.fori_loop(0, whole, functools.partial(step, masked=False), state)
        state = step(whole, state, True)
        for g, (_, weighted) in enumerate(state):
            result = (weighted[:, :HEAD_DIM] / weighted[:, HEAD_DIM:]).astype(jnp.bfloat16)
            for j in range(each):
                h = heads[g * each + j]
                out_ref[:, h * HEAD_DIM : (h + 1) * HEAD_DIM] = result[
                    j * CHUNK : (j + 1) * CHUNK
                ]


def attend(meta, queries, pieces, chunks, tiles, tile_chunks, chains, name, *earlier):
    return pl.pallas_call(
        functools.partial(attend_kernel, tiles, tile_chunks, chains, len(earlier)),
        out_shape=[jax.ShapeDtypeStruct((CHUNK, queries.shape[1]), jnp.bfloat16)] * len(tiles),
        in_specs=[SMEM, VMEM] + [HBM] * (len(pieces) + len(earlier)),
        out_specs=[VMEM] * len(tiles),
        scratch_shapes=[
            pltpu.VMEM((chunks, CHUNK, 2 * HEAD_DIM), jnp.bfloat16),
            pltpu.SemaphoreType.DMA((chunks,)),
        ],
        compiler_params=pltpu.CompilerParams(vmem_limit_bytes=32 * MIB),
        cost_estimate=pl.CostEstimate(
            flops=2_200_000_000, bytes_accessed=5_000_000, transcendentals=10_000_000
        ),
        name=name,
    )(meta, queries, *pieces, *earlier)


def ring_gather(block, again, work, first_hop):
    half = block.shape[0] // 2
    below, above = block, again
    offsets, blocks, state = (0,), (block,), ()
    if first_hop == 2:
        below, above = along_z(block, 1), along_z(again, -1)
        offsets, blocks = (0, 1, 7), (block, above, below)
    for hop in range(first_hop, 5):
        if hop == 4:
            below, above = below[:half], above[half:]
        below, above = along_z(below, 1), along_z(above, -1)
        below, above, *state = together(below, above, *work(offsets, blocks, state))
        offsets, blocks = (hop, 8 - hop), (above, below)
    return (4,), (below, above), state


def rope(value, cosine, sine):
    return value * cosine + pltpu.roll(value, HEAD_DIM // 2, axis=1) * sine


def take_blocks(offsets, refs):
    if offsets == (4,):
        return [jnp.concatenate([refs[0][...], refs[1][...]], axis=0)], refs[2:]
    return [ref[...] for ref in refs[: len(offsets)]], refs[len(offsets) :]


def project_kernel(offsets, first, z_ref, *refs):
    last = offsets == (4,)
    blocks, (gain_ref, w_ref, *refs) = take_blocks(offsets, refs)
    w_vmem, sems = refs[-2:]
    copies = []
    for i, offset in enumerate(offsets):
        source = (z_ref[0] + offset) & 7
        for y_lo in (0, 1):
            rows = pl.ds(y_lo * COLS, COLS)
            copies.append(
                pltpu.make_async_copy(
                    w_ref.at[y_lo * N_Z + source], w_vmem.at[i, rows], sems.at[len(copies)]
                )
            )
            copies[-1].start()
    if first:
        squares, total = jnp.zeros((CHUNK, 128), jnp.float32), None
    else:
        squares, total = refs[0][...], refs[1][...]
    for i, (offset, block) in enumerate(zip(offsets, blocks)):
        wide = block.astype(jnp.float32)
        for at in range(0, PAIR_COLS, 128):
            squares = squares + wide[:, at : at + 128] * wide[:, at : at + 128]
        scaled = (wide * gain_ref[offset : offset + 1]).astype(jnp.bfloat16)
        copies[2 * i].wait()
        copies[2 * i + 1].wait()
        part = jnp.dot(scaled, w_vmem[i], preferred_element_type=jnp.float32)
        total = part if total is None else total + part
    if not last:
        squares_ref, total_ref = refs[-4:-2]
        squares_ref[...], total_ref[...] = squares, total
        return
    cos_ref, sin_ref, q_ref, kv_ref = refs[2:6]
    mean = jnp.sum(squares, axis=1, keepdims=True) / (16 * COLS)
    total = total * lax.rsqrt(mean + norm_eps)
    cosine, sine = cos_ref[...], sin_ref[...]
    for h in range(GROUP):
        at = slice(h * HEAD_DIM, (h + 1) * HEAD_DIM)
        q_ref[:, at] = rope(total[:, at], cosine, sine).astype(jnp.bfloat16)
    at = GROUP * HEAD_DIM
    kv_ref[:, :HEAD_DIM] = rope(total[:, at : at + HEAD_DIM], cosine, sine).astype(jnp.bfloat16)
    kv_ref[:, HEAD_DIM:] = total[:, at + HEAD_DIM :].astype(jnp.bfloat16)


def project(z, gain, weights, rotation, offsets, blocks, state):
    width = weights.shape[2]
    shapes = ((CHUNK, 128), jnp.float32), ((CHUNK, width), jnp.float32)
    extra = ()
    if offsets == (4,):
        shapes = ((CHUNK, GROUP * HEAD_DIM), jnp.bfloat16), ((CHUNK, 2 * HEAD_DIM), jnp.bfloat16)
        extra = rotation
    return pl.pallas_call(
        functools.partial(project_kernel, offsets, not state),
        out_shape=[jax.ShapeDtypeStruct(*shape) for shape in shapes],
        in_specs=[SMEM] + [VMEM] * (len(blocks) + 1) + [HBM] + [VMEM] * (len(state) + len(extra)),
        out_specs=[VMEM] * 2,
        scratch_shapes=[
            pltpu.VMEM((len(offsets), PAIR_COLS, width), jnp.bfloat16),
            pltpu.SemaphoreType.DMA((2 * len(offsets),)),
        ],
        compiler_params=pltpu.CompilerParams(vmem_limit_bytes=16 * MIB),
        cost_estimate=pl.CostEstimate(
            flops=2 * CHUNK * PAIR_COLS * width * len(offsets),
            bytes_accessed=2 * PAIR_COLS * width * len(offsets),
            transcendentals=0,
        ),
        name="norm_project",
    )(z.reshape(1), *blocks, gain, weights, *state, *extra)


def finish_kernel(offsets, place_ref, *refs):
    last = offsets == (4,)
    blocks, (total_ref, w_ref, *outs, w_vmem, sems) = take_blocks(offsets, refs)
    copies = []
    for i, offset in enumerate(offsets):
        source = (place_ref[1] + offset) & 7
        for j in (0, 1):
            at = (place_ref[1] - 2 * source - j) & 7
            at = at + N_Z * ((source >> 2) ^ place_ref[0])
            copies.append(
                pltpu.make_async_copy(w_ref.at[:, at], w_vmem.at[i, j], sems.at[len(copies)])
            )
            copies[-1].start()
    total = total_ref[...].astype(jnp.float32)
    for i, block in enumerate(blocks):
        for j in (0, 1):
            copies[2 * i + j].wait()
            total = total + jnp.dot(
                block[:, j * 2 * HEAD_DIM : (j + 1) * 2 * HEAD_DIM],
                w_vmem[i, j].reshape(2 * HEAD_DIM, PAIR_COLS),
                preferred_element_type=jnp.float32,
            )
    if not last:
        outs[0][...] = total
        return
    own_ref, other_ref = outs
    first, second = total[:, :COLS].astype(jnp.bfloat16), total[:, COLS:].astype(jnp.bfloat16)

    @pl.when(place_ref[0] == 0)
    def _():
        own_ref[...] = first
        other_ref[...] = second

    @pl.when(place_ref[0] == 1)
    def _():
        own_ref[...] = second
        other_ref[...] = first


def finish(place, mixed, weights, offsets, blocks, state):
    shapes = [jax.ShapeDtypeStruct((CHUNK, PAIR_COLS), jnp.float32)]
    if offsets == (4,):
        shapes = [jax.ShapeDtypeStruct((CHUNK, COLS), jnp.bfloat16)] * 2
    return pl.pallas_call(
        functools.partial(finish_kernel, offsets),
        out_shape=shapes,
        in_specs=[SMEM] + [VMEM] * (len(blocks) + 1) + [HBM],
        out_specs=[VMEM] * len(shapes),
        scratch_shapes=[
            pltpu.VMEM((len(offsets), 2, N_CTX, weights.shape[2], PAIR_COLS), jnp.bfloat16),
            pltpu.SemaphoreType.DMA((2 * len(offsets),)),
        ],
        compiler_params=pltpu.CompilerParams(vmem_limit_bytes=16 * MIB),
        cost_estimate=pl.CostEstimate(
            flops=2 * CHUNK * PAIR_COLS * 4 * HEAD_DIM * len(offsets),
            bytes_accessed=8 * PAIR_COLS * HEAD_DIM * len(offsets),
            transcendentals=0,
        ),
        name="project_out",
    )(place, *blocks, *(state or (mixed,)), weights)


def in_order(first, own, other, axis):
    return jnp.where(
        first, jnp.concatenate([own, other], axis=axis), jnp.concatenate([other, own], axis=axis)
    )


def per_device(
    residual,
    global_q,
    global_k,
    global_v,
    global_wo,
    norm_gain,
    stretch_wq,
    stretch_wk,
    stretch_wv,
    stretch_wo,
):
    me = lax.axis_index("ctx")
    place = lax.axis_index("tp")
    y_lo, z = place // N_Z, place % N_Z
    lower = y_lo == 0
    core = me & 1

    place_pair = jnp.stack([y_lo, z]).astype(jnp.int32)

    class_kv = gather_class(take_kv(place // 2, global_k, global_v))
    ctx_order = [2 * k + side for side in (core, 1 - core) for k in range(N_CTX // 2)]
    slots = [slot for c in ctx_order for slot in (c, 2 * N_CTX - 1 - c)]
    limits = jnp.where(lower, me + 1, 2 * N_CTX - me), jnp.where(lower, 2 * N_CTX - me, me + 1)
    ends = limits[0], y_lo * CHUNK, limits[1], (1 - y_lo) * CHUNK
    meta = jnp.stack([*slots, *ends]).astype(jnp.int32)

    first_weights, mine_a, mine_b = arrange(
        z, jnp.int32(0), core, global_wo, global_wo.shape[0]
    )
    rows = stretch_wo.shape[0] // N_CTX
    (share,) = arrange(z, me * rows, None, stretch_wo, rows)
    share = share.reshape(2, 2, 2, rows, PAIR_COLS)
    residual_kept, residual_given = split(place_pair, residual)
    own_wq, mine_a, came = together(
        permute(stretch_wq, "tp", lambda t: 8 * (t % 2) + t // 2),
        to_other_y_lo(mine_a),
        along_z(share[:, :, 1], 1),
    )
    share = jnp.stack([share[:, :, 0], came], axis=2)
    other_wq, mine_b, came = together(
        to_other_y_lo(own_wq), to_other_y_lo(mine_b), along_z(share[:, 1], 2)
    )
    share = jnp.stack([share[:, 0], came], axis=1)
    weights = pack(place_pair, stretch_wk, stretch_wv, own_wq, other_wq)
    other_a, other_b, residual_came, came, weights = together(
        to_other_core(mine_a),
        to_other_core(mine_b),
        to_other_y_lo(residual_given),
        along_z(share[1], 4),
        weights,
    )
    share = jnp.stack([share[0], came], axis=0).reshape(N_Z, rows, PAIR_COLS)
    share = jnp.concatenate([share, to_other_y_lo(share)], axis=0)

    weights, share, _ = together(weights, share, class_kv[0, :16, :HEAD_DIM])
    gathered_weights = lax.all_gather(weights, "ctx", axis=0, tiled=False)
    last_weights = lax.all_gather(share, "ctx", axis=0, tiled=False)

    kept, given = attend(
        meta,
        global_q,
        [in_vmem(class_kv), to_other_core(class_kv)],
        2 * N_CTX,
        ((0, 1), (0, 1)),
        8,
        2,
        "attend_all",
        other_a,
        residual_came,
    )
    parts = first_weights, mine_a, mine_b, other_a, other_b
    operands = core, kept, to_other_y_lo(given), parts
    mixed, again = ring_reduce(operands, place_pair, (residual_kept, residual_came))

    gain = norm_gain.reshape(2, N_Z, COLS).transpose(1, 0, 2).reshape(N_Z, PAIR_COLS)
    gain = lax.dynamic_slice_in_dim(jnp.concatenate([gain, gain], axis=0), z, N_Z, 0)
    chunk = jnp.where(lower, me, 2 * N_CTX - 1 - me)
    positions = (chunk * CHUNK + jnp.arange(CHUNK, dtype=jnp.int32)).astype(jnp.float32)
    half_dim = HEAD_DIM // 2
    inv_freq = rope_base ** (-(jnp.arange(half_dim).astype(jnp.float32) * 2.0 / HEAD_DIM))
    angles = positions[:, None] * inv_freq[None, :]
    cosine, sine = jnp.cos(angles), jnp.sin(angles)
    rotation = (
        jnp.concatenate([cosine, cosine], axis=1),
        jnp.concatenate([-sine, sine], axis=1),
    )
    work = functools.partial(project, z, gain, gathered_weights, rotation)
    stretch_q, stretch_kv = work(*ring_gather(mixed, again, work, 2))
    pieces = gather_ctx(stretch_kv)
    slots = [jnp.where(lower, c, N_CTX - 1 - c) for c in owners()]
    limit = jnp.where(lower, me + 1, N_CTX - me)
    meta = jnp.stack(slots + [limit, 0]).astype(jnp.int32)
    (attended,) = attend(
        meta, stretch_q, pieces, N_CTX, ((0, 1, 2, 3),), 8, 4, "attend_window"
    )
    work = functools.partial(finish, place_pair, mixed, last_weights)
    own, other = work(*ring_gather(attended, attended, work, 2))
    return in_order(lower, own, to_other_y_lo(other), 0)


def solution(mesh):
    in_specs = (
        P("ctx", "tp"),
        P("ctx", "tp"),
        P("ctx", None),
        P("ctx", None),
        P("tp", None),
        P(),
        P("ctx", "tp"),
        P("ctx", None),
        P("ctx", None),
        P("tp", None),
    )
    return jax.shard_map(
        per_device, mesh=mesh, in_specs=in_specs, out_specs=P("ctx", "tp"), check_vma=False
    )
```

```python
import functools

import jax
import jax.numpy as jnp
from jax import lax
from jax.experimental import pallas as pl
from jax.experimental.pallas import tpu as pltpu
from jax.sharding import PartitionSpec as P

HEAD_DIM = 128
GROUP = 4
CHUNK = 256
N_CTX = 16
N_Z = 8
COLS = 320
PAIR_COLS = 2 * COLS
rope_base = 500000.0
norm_eps = 1e-05
masked_score = -1e30
scale_log2 = 1.4426950408889634 * HEAD_DIM**-0.5
MIB = 1024 * 1024
SMEM = pl.BlockSpec(memory_space=pltpu.SMEM)
VMEM = pl.BlockSpec(memory_space=pltpu.VMEM)
HBM = pl.BlockSpec(memory_space=pltpu.HBM)


def permute(value, axis, target):
    return lax.ppermute(value, axis, [(place, target(place)) for place in range(16)])


def to_other_core(value):
    return permute(value, "ctx", lambda c: c ^ 1)


def to_other_y_hi(value):
    return permute(value, "ctx", lambda c: c ^ 8)


def along_x(value, step):
    return permute(value, "ctx", lambda c: (c & 9) | ((c + 2 * step) & 6))


def to_other_y_lo(value):
    return permute(value, "tp", lambda t: t ^ 8)


def along_z(value, step):
    return permute(value, "tp", lambda t: (t & 8) | ((t + step) & 7))


def together_kernel(*refs):
    pass


def together(*values):
    return pl.pallas_call(
        together_kernel,
        out_shape=[jax.ShapeDtypeStruct(value.shape, value.dtype) for value in values],
        in_specs=[HBM] * len(values),
        out_specs=[HBM] * len(values),
        input_output_aliases={i: i for i in range(len(values))},
        compiler_params=pltpu.CompilerParams(vmem_limit_bytes=MIB),
        name="together",
    )(*values)


def copy_kernel(source, out, sem):
    copy = pltpu.make_async_copy(source, out, sem)
    copy.start()
    copy.wait()


def in_vmem(value):
    return pl.pallas_call(
        copy_kernel,
        out_shape=jax.ShapeDtypeStruct(value.shape, value.dtype),
        in_specs=[HBM],
        out_specs=VMEM,
        scratch_shapes=[pltpu.SemaphoreType.DMA],
        compiler_params=pltpu.CompilerParams(vmem_limit_bytes=8 * MIB),
        name="in_vmem",
    )(value)


def arrange_kernel(row_count, place_ref, source, *rest):
    outs, (rows, sem) = rest[:-2], rest[-2:]
    first = pl.multiple_of(place_ref[1], 16)
    copy = pltpu.make_async_copy(source.at[pl.ds(first, row_count)], rows, sem)
    copy.start()
    copy.wait()
    for z in range(N_Z):
        offset = (z - place_ref[0]) & 7
        for y_lo in (0, 1):
            at = (y_lo * N_Z + z) * COLS
            outs[0][offset, :, y_lo * COLS : (y_lo + 1) * COLS] = rows[:, at : at + COLS]
    for i, out in enumerate(outs[1:]):
        count, height = out.shape[:2]
        half = pl.ds(pl.multiple_of(place_ref[2], height), height)
        out[...] = outs[0][i * count : (i + 1) * count, half, :]


def arrange(z, first, half, weights, row_count):
    shapes = [jax.ShapeDtypeStruct((N_Z, row_count, PAIR_COLS), jnp.bfloat16)]
    place = [z, first]
    if half is not None:
        shapes += [
            jax.ShapeDtypeStruct((N_Z // 2, row_count // 2, PAIR_COLS), jnp.bfloat16)
        ] * 2
        place.append(half * (row_count // 2))
    return pl.pallas_call(
        functools.partial(arrange_kernel, row_count),
        out_shape=shapes,
        in_specs=[SMEM, HBM],
        out_specs=[VMEM] * len(shapes),
        scratch_shapes=[
            pltpu.VMEM((row_count, weights.shape[1]), jnp.bfloat16),
            pltpu.SemaphoreType.DMA,
        ],
        compiler_params=pltpu.CompilerParams(vmem_limit_bytes=20 * MIB),
        name="arrange",
    )(jnp.stack(place).astype(jnp.int32), weights)


def pack_kernel(place_ref, k_ref, v_ref, own_ref, other_ref, out_ref, sems):
    def columns(first, width):
        return pl.ds(pl.multiple_of(first, HEAD_DIM), width)

    wide = own_ref.shape[1]
    head = columns(place_ref[1] * HEAD_DIM, HEAD_DIM)
    moves = (
        (own_ref, columns(place_ref[0] * wide, wide)),
        (other_ref, columns((1 - place_ref[0]) * wide, wide)),
        (k_ref.at[:, head], pl.ds(2 * wide, HEAD_DIM)),
        (v_ref.at[:, head], pl.ds(2 * wide + HEAD_DIM, HEAD_DIM)),
    )
    copies = [
        pltpu.make_async_copy(source, out_ref.at[:, target], sems.at[i])
        for i, (source, target) in enumerate(moves)
    ]
    for copy in copies:
        copy.start()
    for copy in copies:
        copy.wait()


def pack(place, keys, values, own, other):
    rows, wide = own.shape
    return pl.pallas_call(
        pack_kernel,
        out_shape=jax.ShapeDtypeStruct((rows, 2 * (wide + HEAD_DIM)), jnp.bfloat16),
        in_specs=[SMEM] + [HBM] * 4,
        out_specs=HBM,
        scratch_shapes=[pltpu.SemaphoreType.DMA((4,))],
        compiler_params=pltpu.CompilerParams(vmem_limit_bytes=MIB),
        name="pack",
    )(place, keys, values, own, other)


def split_kernel(place_ref, value_ref, *rest):
    outs, sems = rest[-3:-1], rest[-1]
    copies = []
    for i, half in enumerate((place_ref[0], 1 - place_ref[0])):
        rows = pl.ds(pl.multiple_of(half * CHUNK, CHUNK), CHUNK)
        copies.append(pltpu.make_async_copy(value_ref.at[rows], outs[i], sems.at[i]))
        copies[-1].start()
    for copy in copies:
        copy.wait()


def split(place, value):
    half = jax.ShapeDtypeStruct((CHUNK, value.shape[1]), value.dtype)
    return pl.pallas_call(
        split_kernel,
        out_shape=(half, half),
        in_specs=[SMEM, HBM],
        out_specs=(VMEM, VMEM),
        scratch_shapes=[pltpu.SemaphoreType.DMA((2,))],
        compiler_params=pltpu.CompilerParams(vmem_limit_bytes=MIB),
        name="split",
    )(place, value)


def own_terms(offsets, core_ref, kept_ref, received_ref, weights, others, refs):
    buffer, landing, sems = refs
    half = CHUNK // 2
    copies = []
    for i, offset in enumerate(offsets):
        late, at = offset // 4, offset % 4
        sources = weights[0].at[offset], weights[1 + late].at[at], weights[3 + late].at[at]
        for j, (first, rows) in enumerate(((0, CHUNK), (CHUNK, half), (CHUNK + half, half))):
            target = buffer.at[i, pl.ds(first, rows)]
            copies.append(pltpu.make_async_copy(sources[j], target, sems.at[3 * i + j]))
            copies[-1].start()
    landed = []
    for i, other in enumerate(others):
        target = landing.at[i, pl.ds(0, other.shape[0]), pl.ds(0, other.shape[1])]
        copies.append(pltpu.make_async_copy(other, target, sems.at[len(copies)]))
        copies[-1].start()
    received = received_ref[...]
    low, high = received[:, :half], received[:, half:]
    first = jnp.full(low.shape, core_ref[0], jnp.int32) == 0
    rows = jnp.concatenate(
        [kept_ref[...], jnp.where(first, low, high), jnp.where(first, high, low)], axis=1
    )
    for copy in copies:
        copy.wait()
    for i, other in enumerate(others):
        landed.append(landing[i, : other.shape[0]].astype(jnp.float32))
    parts = [
        jnp.dot(rows, buffer[i], preferred_element_type=jnp.float32) for i in range(len(offsets))
    ]
    return parts, landed


def terms_kernel(offsets, core_ref, kept_ref, received_ref, *refs):
    weights, (*outs, buffer, landing, sems) = refs[:5], refs[5:]
    scratch = buffer, landing, sems
    parts, _ = own_terms(offsets, core_ref, kept_ref, received_ref, weights, (), scratch)
    if offsets == (4,):
        parts = parts[0][: CHUNK // 2], parts[0][CHUNK // 2 :]
    for part, out in zip(parts, outs):
        out[...] = part.astype(jnp.bfloat16)


def hop_kernel(up_ref, down_ref, up_term_ref, down_term_ref, up_out_ref, down_out_ref):
    came = up_ref.shape[0]
    rest = CHUNK - came
    up, down = up_term_ref[:came].astype(jnp.float32), down_term_ref[rest:].astype(jnp.float32)
    up_out_ref[:came] = (up + up_ref[...].astype(jnp.float32)).astype(jnp.bfloat16)
    down_out_ref[rest:] = (down + down_ref[...].astype(jnp.float32)).astype(jnp.bfloat16)
    if rest:
        up_out_ref[came:] = up_term_ref[came:]
        down_out_ref[:rest] = down_term_ref[:rest]


def mix_kernel(up_ref, down_ref, term_ref, place_ref, *refs):
    *residual, out_ref, again_ref = refs
    total = sum(ref[...].astype(jnp.float32) for ref in (up_ref, down_ref, term_ref))

    def put(first, second):
        out_ref[:, :COLS] = (total[:, :COLS] + first[...].astype(jnp.float32)).astype(jnp.bfloat16)
        out_ref[:, COLS:] = (total[:, COLS:] + second[...].astype(jnp.float32)).astype(jnp.bfloat16)

    pl.when(place_ref[0] == 0)(lambda: put(*residual))
    pl.when(place_ref[0] == 1)(lambda: put(*residual[::-1]))
    again_ref[...] = out_ref[...]


def terms(offsets, core, kept, received, weights):
    count = len(offsets)
    shapes = [(CHUNK, PAIR_COLS)] * count if offsets != (4,) else [(CHUNK // 2, PAIR_COLS)] * 2
    return pl.pallas_call(
        functools.partial(terms_kernel, offsets),
        out_shape=[jax.ShapeDtypeStruct(shape, jnp.bfloat16) for shape in shapes],
        in_specs=[SMEM, VMEM, VMEM] + [HBM] * 5,
        out_specs=[VMEM] * len(shapes),
        scratch_shapes=[
            pltpu.VMEM((count, 2 * CHUNK, PAIR_COLS), jnp.bfloat16),
            pltpu.VMEM((1, 16, 128), jnp.bfloat16),
            pltpu.SemaphoreType.DMA((3 * count,)),
        ],
        compiler_params=pltpu.CompilerParams(vmem_limit_bytes=24 * MIB),
        name="terms",
    )(core.reshape(1), kept, received, *weights)


def ring_step(kernel, name, *operands):
    specs = [SMEM if operand.ndim == 1 else VMEM for operand in operands]
    return pl.pallas_call(
        kernel,
        out_shape=[jax.ShapeDtypeStruct((CHUNK, PAIR_COLS), jnp.bfloat16)] * 2,
        in_specs=specs,
        out_specs=[VMEM] * 2,
        compiler_params=pltpu.CompilerParams(vmem_limit_bytes=8 * MIB),
        name=name,
    )(*operands)


def ring_reduce(operands, place, residual):
    up, down = terms((4,), *operands)
    up, down = along_z(up, 1), along_z(down, -1)
    offsets = (3, 5, 2, 6, 1, 7, 0)
    term = dict(zip(offsets, terms(offsets, *operands)))
    for hop in (3, 2, 1):
        up, down = ring_step(hop_kernel, "hop", up, down, term[hop], term[N_Z - hop])
        up, down = along_z(up, 1), along_z(down, -1)
    return ring_step(mix_kernel, "mix", up, down, term[0], place, *residual)


GATHER_OFFSETS = [
    (dy, dx, core)
    for core in (0, 1)
    for dy, dx in ((0, 0), (1, 0), (0, 3), (0, 1), (0, 2), (1, 3), (1, 1), (1, 2))
]


def gather_ctx(block):
    other = to_other_y_hi(block)
    left, right = along_x(block, 1), along_x(block, -1)
    far = along_x(left, 1)
    left_other, right_other = to_other_y_hi(left), along_x(other, -1)
    far_other = along_x(right_other, -1)
    mine = [block, other, left, right, far, left_other, right_other, far_other]
    return mine + [
        to_other_core(jnp.stack(mine[:4])),
        to_other_core(jnp.stack(mine[4:7])),
        to_other_core(far_other),
    ]


CLASSES = [list(range(0, N_CTX, 2)), list(range(1, N_CTX, 2))]


def gather_class(block):
    return lax.all_gather(block, "ctx", axis=0, tiled=False, axis_index_groups=CLASSES)


def owners():
    me = lax.axis_index("ctx")
    return [
        ((me & 8) ^ (8 * dy)) | ((me + 2 * dx) & 6) | ((me & 1) ^ dc)
        for dy, dx, dc in GATHER_OFFSETS
    ]


def take_kernel(place_ref, k_ref, v_ref, out_ref, sems):
    columns = pl.ds(pl.multiple_of(place_ref[0] * HEAD_DIM, HEAD_DIM), HEAD_DIM)
    copies = [
        pltpu.make_async_copy(src.at[:, columns], out_ref.at[:, pl.ds(i * HEAD_DIM, HEAD_DIM)], sems.at[i])
        for i, src in enumerate((k_ref, v_ref))
    ]
    for copy in copies:
        copy.start()
    for copy in copies:
        copy.wait()


def take_kv(place, keys, values):
    rows = keys.shape[0]
    return pl.pallas_call(
        take_kernel,
        out_shape=jax.ShapeDtypeStruct((rows, 2 * HEAD_DIM), jnp.bfloat16),
        in_specs=[SMEM, HBM, HBM],
        out_specs=VMEM,
        scratch_shapes=[pltpu.SemaphoreType.DMA((2,))],
        compiler_params=pltpu.CompilerParams(vmem_limit_bytes=60 * MIB),
        name="take_kv",
    )(place.reshape(1), keys, values)


def attend_kernel(tiles, tile_chunks, chains, earlier, meta_ref, q_ref, *rest):
    pieces, outs, (kv, sems) = rest[: -2 - len(tiles) - earlier], rest[-2 - len(tiles) : -2], rest[-2:]
    blocks = []
    for piece in pieces:
        blocks += [piece] if len(piece.shape) == 2 else [piece.at[b] for b in range(piece.shape[0])]
    copies = []
    for block in blocks:
        for part in range(block.shape[0] // CHUNK):
            source = block.at[pl.ds(part * CHUNK, CHUNK)]
            copies.append(
                pltpu.make_async_copy(source, kv.at[meta_ref[len(copies)]], sems.at[len(copies)])
            )
            copies[-1].start()
    for copy in copies:
        copy.wait()
    span = tile_chunks * CHUNK
    for tile, (heads, out_ref) in enumerate(zip(tiles, outs)):
        limit = meta_ref[len(copies) + 2 * tile]
        first = pl.multiple_of(meta_ref[len(copies) + 2 * tile + 1], CHUNK)
        rows = q_ref.at[pl.ds(first, CHUNK)]
        each = len(heads) // chains
        queries = [
            jnp.concatenate(
                [rows[:, h * HEAD_DIM : (h + 1) * HEAD_DIM] for h in heads[g * each : (g + 1) * each]],
                axis=0,
            )
            for g in range(chains)
        ]
        height = each * CHUNK

        def step(i, state, masked):
            here = pl.ds(i * tile_chunks, tile_chunks)
            keys = kv[here, :, :HEAD_DIM].reshape(span, HEAD_DIM)
            values = kv[here, :, HEAD_DIM:].reshape(span, HEAD_DIM)
            values = jnp.concatenate([values, jnp.ones(values.shape, values.dtype)], axis=1)
            if masked:
                column = lax.broadcasted_iota(jnp.int32, (height, span), 1) + i * span
                row = lax.broadcasted_iota(jnp.int32, (height, span), 0) % CHUNK
                visible = column <= row + (limit - 1) * CHUNK
            scores = [
                lax.dot_general(
                    query, keys, (((1,), (1,)), ((), ())), preferred_element_type=jnp.float32
                )
                for query in queries
            ]
            after = []
            for score, (highest, weighted) in zip(scores, state):
                if masked:
                    score = jnp.where(visible, score, masked_score)
                new_high = jnp.maximum(highest, jnp.max(score, axis=1, keepdims=True))
                fade = jnp.exp2((highest - new_high) * scale_log2)
                scores_here = score * scale_log2 - new_high * scale_log2
                weights = jnp.exp2(scores_here).astype(jnp.bfloat16)
                weighted = weighted * fade + jnp.dot(
                    weights, values, preferred_element_type=jnp.float32
                )
                after.append((new_high, weighted))
            return tuple(after)

        state = tuple(
            (
                jnp.full((height, 1), masked_score, jnp.float32),
                jnp.zeros((height, 2 * HEAD_DIM), jnp.float32),
            )
            for _ in range(chains)
        )
        whole = lax.div(limit - 1, jnp.int32(tile_chunks))
        state = lax.fori_loop(0, whole, functools.partial(step, masked=False), state)
        state = step(whole, state, True)
        for g, (_, weighted) in enumerate(state):
            result = (weighted[:, :HEAD_DIM] / weighted[:, HEAD_DIM:]).astype(jnp.bfloat16)
            for j in range(each):
                h = heads[g * each + j]
                out_ref[:, h * HEAD_DIM : (h + 1) * HEAD_DIM] = result[
                    j * CHUNK : (j + 1) * CHUNK
                ]


def attend(meta, queries, pieces, chunks, tiles, tile_chunks, chains, name, *earlier):
    return pl.pallas_call(
        functools.partial(attend_kernel, tiles, tile_chunks, chains, len(earlier)),
        out_shape=[jax.ShapeDtypeStruct((CHUNK, queries.shape[1]), jnp.bfloat16)] * len(tiles),
        in_specs=[SMEM, VMEM] + [HBM] * (len(pieces) + len(earlier)),
        out_specs=[VMEM] * len(tiles),
        scratch_shapes=[
            pltpu.VMEM((chunks, CHUNK, 2 * HEAD_DIM), jnp.bfloat16),
            pltpu.SemaphoreType.DMA((chunks,)),
        ],
        compiler_params=pltpu.CompilerParams(vmem_limit_bytes=32 * MIB),
        cost_estimate=pl.CostEstimate(
            flops=2_200_000_000, bytes_accessed=5_000_000, transcendentals=10_000_000
        ),
        name=name,
    )(meta, queries, *pieces, *earlier)


def ring_gather(block, again, work, first_hop):
    half = block.shape[0] // 2
    below, above = block, again
    offsets, blocks, state = (0,), (block,), ()
    if first_hop == 2:
        below, above = along_z(block, 1), along_z(again, -1)
        offsets, blocks = (0, 1, 7), (block, above, below)
    for hop in range(first_hop, 5):
        if hop == 4:
            below, above = below[:half], above[half:]
        below, above = along_z(below, 1), along_z(above, -1)
        below, above, *state = together(below, above, *work(offsets, blocks, state))
        offsets, blocks = (hop, 8 - hop), (above, below)
    return (4,), (below, above), state


def rope(value, cosine, sine):
    return value * cosine + pltpu.roll(value, HEAD_DIM // 2, axis=1) * sine


def take_blocks(offsets, refs):
    if offsets == (4,):
        return [jnp.concatenate([refs[0][...], refs[1][...]], axis=0)], refs[2:]
    return [ref[...] for ref in refs[: len(offsets)]], refs[len(offsets) :]


def project_kernel(offsets, first, z_ref, *refs):
    last = offsets == (4,)
    blocks, (gain_ref, w_ref, *refs) = take_blocks(offsets, refs)
    w_vmem, sems = refs[-2:]
    copies = []
    for i, offset in enumerate(offsets):
        source = (z_ref[0] + offset) & 7
        for y_lo in (0, 1):
            rows = pl.ds(y_lo * COLS, COLS)
            copies.append(
                pltpu.make_async_copy(
                    w_ref.at[y_lo * N_Z + source], w_vmem.at[i, rows], sems.at[len(copies)]
                )
            )
            copies[-1].start()
    if first:
        squares, total = jnp.zeros((CHUNK, 128), jnp.float32), None
    else:
        squares, total = refs[0][...], refs[1][...]
    for i, (offset, block) in enumerate(zip(offsets, blocks)):
        wide = block.astype(jnp.float32)
        for at in range(0, PAIR_COLS, 128):
            squares = squares + wide[:, at : at + 128] * wide[:, at : at + 128]
        scaled = (wide * gain_ref[offset : offset + 1]).astype(jnp.bfloat16)
        copies[2 * i].wait()
        copies[2 * i + 1].wait()
        part = jnp.dot(scaled, w_vmem[i], preferred_element_type=jnp.float32)
        total = part if total is None else total + part
    if not last:
        squares_ref, total_ref = refs[-4:-2]
        squares_ref[...], total_ref[...] = squares, total
        return
    cos_ref, sin_ref, q_ref, kv_ref = refs[2:6]
    mean = jnp.sum(squares, axis=1, keepdims=True) / (16 * COLS)
    total = total * lax.rsqrt(mean + norm_eps)
    cosine, sine = cos_ref[...], sin_ref[...]
    for h in range(GROUP):
        at = slice(h * HEAD_DIM, (h + 1) * HEAD_DIM)
        q_ref[:, at] = rope(total[:, at], cosine, sine).astype(jnp.bfloat16)
    at = GROUP * HEAD_DIM
    kv_ref[:, :HEAD_DIM] = rope(total[:, at : at + HEAD_DIM], cosine, sine).astype(jnp.bfloat16)
    kv_ref[:, HEAD_DIM:] = total[:, at + HEAD_DIM :].astype(jnp.bfloat16)


def project(z, gain, weights, rotation, offsets, blocks, state):
    width = weights.shape[2]
    shapes = ((CHUNK, 128), jnp.float32), ((CHUNK, width), jnp.float32)
    extra = ()
    if offsets == (4,):
        shapes = ((CHUNK, GROUP * HEAD_DIM), jnp.bfloat16), ((CHUNK, 2 * HEAD_DIM), jnp.bfloat16)
        extra = rotation
    return pl.pallas_call(
        functools.partial(project_kernel, offsets, not state),
        out_shape=[jax.ShapeDtypeStruct(*shape) for shape in shapes],
        in_specs=[SMEM] + [VMEM] * (len(blocks) + 1) + [HBM] + [VMEM] * (len(state) + len(extra)),
        out_specs=[VMEM] * 2,
        scratch_shapes=[
            pltpu.VMEM((len(offsets), PAIR_COLS, width), jnp.bfloat16),
            pltpu.SemaphoreType.DMA((2 * len(offsets),)),
        ],
        compiler_params=pltpu.CompilerParams(vmem_limit_bytes=16 * MIB),
        cost_estimate=pl.CostEstimate(
            flops=2 * CHUNK * PAIR_COLS * width * len(offsets),
            bytes_accessed=2 * PAIR_COLS * width * len(offsets),
            transcendentals=0,
        ),
        name="norm_project",
    )(z.reshape(1), *blocks, gain, weights, *state, *extra)


def finish_kernel(offsets, place_ref, *refs):
    last = offsets == (4,)
    blocks, (total_ref, w_ref, *outs, w_vmem, sems) = take_blocks(offsets, refs)
    copies = []
    for i, offset in enumerate(offsets):
        source = (place_ref[1] + offset) & 7
        for j in (0, 1):
            at = (place_ref[1] - 2 * source - j) & 7
            at = at + N_Z * ((source >> 2) ^ place_ref[0])
            copies.append(
                pltpu.make_async_copy(w_ref.at[:, at], w_vmem.at[i, j], sems.at[len(copies)])
            )
            copies[-1].start()
    total = total_ref[...].astype(jnp.float32)
    for i, block in enumerate(blocks):
        for j in (0, 1):
            copies[2 * i + j].wait()
            total = total + jnp.dot(
                block[:, j * 2 * HEAD_DIM : (j + 1) * 2 * HEAD_DIM],
                w_vmem[i, j].reshape(2 * HEAD_DIM, PAIR_COLS),
                preferred_element_type=jnp.float32,
            )
    if not last:
        outs[0][...] = total
        return
    own_ref, other_ref = outs
    first, second = total[:, :COLS].astype(jnp.bfloat16), total[:, COLS:].astype(jnp.bfloat16)

    @pl.when(place_ref[0] == 0)
    def _():
        own_ref[...] = first
        other_ref[...] = second

    @pl.when(place_ref[0] == 1)
    def _():
        own_ref[...] = second
        other_ref[...] = first


def finish(place, mixed, weights, offsets, blocks, state):
    shapes = [jax.ShapeDtypeStruct((CHUNK, PAIR_COLS), jnp.float32)]
    if offsets == (4,):
        shapes = [jax.ShapeDtypeStruct((CHUNK, COLS), jnp.bfloat16)] * 2
    return pl.pallas_call(
        functools.partial(finish_kernel, offsets),
        out_shape=shapes,
        in_specs=[SMEM] + [VMEM] * (len(blocks) + 1) + [HBM],
        out_specs=[VMEM] * len(shapes),
        scratch_shapes=[
            pltpu.VMEM((len(offsets), 2, N_CTX, weights.shape[2], PAIR_COLS), jnp.bfloat16),
            pltpu.SemaphoreType.DMA((2 * len(offsets),)),
        ],
        compiler_params=pltpu.CompilerParams(vmem_limit_bytes=16 * MIB),
        cost_estimate=pl.CostEstimate(
            flops=2 * CHUNK * PAIR_COLS * 4 * HEAD_DIM * len(offsets),
            bytes_accessed=8 * PAIR_COLS * HEAD_DIM * len(offsets),
            transcendentals=0,
        ),
        name="project_out",
    )(place, *blocks, *(state or (mixed,)), weights)


def in_order(first, own, other, axis):
    return jnp.where(
        first, jnp.concatenate([own, other], axis=axis), jnp.concatenate([other, own], axis=axis)
    )


def per_device(
    residual,
    global_q,
    global_k,
    global_v,
    global_wo,
    norm_gain,
    stretch_wq,
    stretch_wk,
    stretch_wv,
    stretch_wo,
):
    me = lax.axis_index("ctx")
    place = lax.axis_index("tp")
    y_lo, z = place // N_Z, place % N_Z
    lower = y_lo == 0
    core = me & 1

    place_pair = jnp.stack([y_lo, z]).astype(jnp.int32)

    class_kv = gather_class(take_kv(place // 2, global_k, global_v))
    ctx_order = [2 * k + side for side in (core, 1 - core) for k in range(N_CTX // 2)]
    slots = [slot for c in ctx_order for slot in (c, 2 * N_CTX - 1 - c)]
    limits = jnp.where(lower, me + 1, 2 * N_CTX - me), jnp.where(lower, 2 * N_CTX - me, me + 1)
    ends = limits[0], y_lo * CHUNK, limits[1], (1 - y_lo) * CHUNK
    meta = jnp.stack([*slots, *ends]).astype(jnp.int32)

    first_weights, mine_a, mine_b = arrange(
        z, jnp.int32(0), core, global_wo, global_wo.shape[0]
    )
    rows = stretch_wo.shape[0] // N_CTX
    (share,) = arrange(z, me * rows, None, stretch_wo, rows)
    share = share.reshape(2, 2, 2, rows, PAIR_COLS)
    residual_kept, residual_given = split(place_pair, residual)
    own_wq, mine_a, came = together(
        permute(stretch_wq, "tp", lambda t: 8 * (t % 2) + t // 2),
        to_other_y_lo(mine_a),
        along_z(share[:, :, 1], 1),
    )
    share = jnp.stack([share[:, :, 0], came], axis=2)
    other_wq, mine_b, came = together(
        to_other_y_lo(own_wq), to_other_y_lo(mine_b), along_z(share[:, 1], 2)
    )
    share = jnp.stack([share[:, 0], came], axis=1)
    weights = pack(place_pair, stretch_wk, stretch_wv, own_wq, other_wq)
    other_a, other_b, residual_came, came, weights = together(
        to_other_core(mine_a),
        to_other_core(mine_b),
        to_other_y_lo(residual_given),
        along_z(share[1], 4),
        weights,
    )
    share = jnp.stack([share[0], came], axis=0).reshape(N_Z, rows, PAIR_COLS)
    share = jnp.concatenate([share, to_other_y_lo(share)], axis=0)

    weights, share, _ = together(weights, share, class_kv[0, :16, :HEAD_DIM])
    gathered_weights = lax.all_gather(weights, "ctx", axis=0, tiled=False)
    last_weights = lax.all_gather(share, "ctx", axis=0, tiled=False)

    kept, given = attend(
        meta,
        global_q,
        [in_vmem(class_kv), to_other_core(class_kv)],
        2 * N_CTX,
        ((0, 1), (0, 1)),
        8,
        2,
        "attend_all",
        other_a,
        residual_came,
    )
    parts = first_weights, mine_a, mine_b, other_a, other_b
    operands = core, kept, to_other_y_lo(given), parts
    mixed, again = ring_reduce(operands, place_pair, (residual_kept, residual_came))

    gain = norm_gain.reshape(2, N_Z, COLS).transpose(1, 0, 2).reshape(N_Z, PAIR_COLS)
    gain = lax.dynamic_slice_in_dim(jnp.concatenate([gain, gain], axis=0), z, N_Z, 0)
    chunk = jnp.where(lower, me, 2 * N_CTX - 1 - me)
    positions = (chunk * CHUNK + jnp.arange(CHUNK, dtype=jnp.int32)).astype(jnp.float32)
    half_dim = HEAD_DIM // 2
    inv_freq = rope_base ** (-(jnp.arange(half_dim).astype(jnp.float32) * 2.0 / HEAD_DIM))
    angles = positions[:, None] * inv_freq[None, :]
    cosine, sine = jnp.cos(angles), jnp.sin(angles)
    rotation = (
        jnp.concatenate([cosine, cosine], axis=1),
        jnp.concatenate([-sine, sine], axis=1),
    )
    work = functools.partial(project, z, gain, gathered_weights, rotation)
    stretch_q, stretch_kv = work(*ring_gather(mixed, again, work, 2))
    pieces = gather_ctx(stretch_kv)
    slots = [jnp.where(lower, c, N_CTX - 1 - c) for c in owners()]
    limit = jnp.where(lower, me + 1, N_CTX - me)
    meta = jnp.stack(slots + [limit, 0]).astype(jnp.int32)
    (attended,) = attend(
        meta, stretch_q, pieces, N_CTX, ((0, 1, 2, 3),), 8, 4, "attend_window"
    )
    work = functools.partial(finish, place_pair, mixed, last_weights)
    own, other = work(*ring_gather(attended, attended, work, 2))
    return in_order(lower, own, to_other_y_lo(other), 0)


def solution(mesh):
    in_specs = (
        P("ctx", "tp"),
        P("ctx", "tp"),
        P("ctx", None),
        P("ctx", None),
        P("tp", None),
        P(),
        P("ctx", "tp"),
        P("ctx", None),
        P("ctx", None),
        P("tp", None),
    )
    return jax.shard_map(
        per_device, mesh=mesh, in_specs=in_specs, out_specs=P("ctx", "tp"), check_vma=False
    )
```
